256 devices in a mesh: gx: 4 (over x), gy: 8 (over y, core), gz: 8 (over z).
Axes of the slice: x: 4, y: 4, z: 8, core: 2. Of those that a mesh axis runs over, the one named last changes fastest.
Arguments:
- volume: bfloat16 [32, 128, 8192], P('gx', 'gy', 'gz'), may hold values from -6 to 6
- weight_top: bfloat16 [3, 3, 3, 64, 64], replicated, may hold values from -0.21875 to 0.21875
- weight_down_a: bfloat16 [3, 3, 3, 64, 128], replicated, may hold values from -0.21875 to 0.21875
- weight_down_b: bfloat16 [3, 3, 3, 128, 128], replicated, may hold values from -0.15625 to 0.15625
- weight_low_a: bfloat16 [3, 3, 3, 128, 256], replicated, may hold values from -0.15625 to 0.15625
- weight_low_b: bfloat16 [3, 3, 3, 256, 256], replicated, may hold values from -0.109375 to 0.109375
- weight_lift_low: bfloat16 [256, 2, 2, 2, 128], replicated, may hold values from -0.5 to 0.5
- weight_up_mid: bfloat16 [3, 3, 3, 256, 128], replicated, may hold values from -0.109375 to 0.109375
- weight_lift_top: bfloat16 [128, 2, 2, 2, 64], replicated, may hold values from -0.75 to 0.75
- weight_out: bfloat16 [3, 3, 3, 128, 64], replicated, may hold values from -0.15625 to 0.15625
Outputs:
- decoded: bfloat16 [32, 128, 8192], P('gx', 'gy', 'gz')
The draws below stay inside these ranges and needn't reach their ends.
All inputs are finite; a program needn't handle non-finite values.
Results may differ from the reference program's by a relative error of at most 0.02.
Values may be sent and summed in bfloat16 or wider, within the bound.
A program may use at most 64 MiB of HBM per device.

```python
import jax
import jax.numpy as jnp
from jax import lax

C3 = 64
C4 = 128
C5 = 256
NX = 32
NY = 128
NZ = 128


def steps_of(rng, dims, cuts, smallest, largest):
    loudness, own = 1.0, jax.random.fold_in(rng, 6)
    for axis_at, blocks in cuts:
        draws = jnp.exp(jax.random.uniform(jax.random.fold_in(own, axis_at), (blocks,), jnp.float32, smallest / len(cuts), largest / len(cuts)))
        loudness = loudness * jnp.repeat(draws, dims[axis_at] // blocks).reshape([-1 if axis == axis_at else 1 for axis in range(len(dims))])
    return loudness


def centred(own_key, dims, deviation, bound, split=(), held_as=jnp.bfloat16):
    factor_of = steps_of(own_key, dims, split, -0.22, 0.18) if split else 1.0
    array = jax.random.normal(own_key, dims, jnp.float32) * deviation * factor_of
    return jnp.minimum(jnp.maximum(array, -bound), bound).astype(held_as)


def setup_inputs(seed: int = 0) -> dict:
    key_of = jax.random.split(jax.random.key(seed), 11)
    volume = centred(key_of[0], (NX, NY, NZ * C3), 1.0, 6.0, ((0, 4), (1, 8), (2, 8)))
    weight_top = centred(key_of[1], (3, 3, 3, C3, C3), (27 * C3 // 2) ** -0.5, 0.21875)
    weight_down_a = centred(key_of[2], (3, 3, 3, C3, C4), (27 * C3 // 2) ** -0.5, 0.21875)
    weight_down_b = centred(key_of[3], (3, 3, 3, C4, C4), (27 * C4 // 2) ** -0.5, 0.15625)
    weight_low_a = centred(key_of[4], (3, 3, 3, C4, C5), (27 * C4 // 2) ** -0.5, 0.15625)
    weight_low_b = centred(key_of[5], (3, 3, 3, C5, C5), (27 * C5 // 2) ** -0.5, 0.109375)
    weight_lift_low = centred(key_of[6], (C5, 2, 2, 2, C4), (C5 // 2) ** -0.5, 0.5)
    weight_up_mid = centred(key_of[7], (3, 3, 3, 2 * C4, C4), (27 * C4) ** -0.5, 0.109375)
    weight_lift_top = centred(key_of[8], (C4, 2, 2, 2, C3), (C4 // 2) ** -0.5, 0.75)
    weight_out = centred(key_of[9], (3, 3, 3, 2 * C3, C3), (27 * C3) ** -0.5, 0.15625)
    return {"volume": volume, "weight_top": weight_top, "weight_down_a": weight_down_a, "weight_down_b": weight_down_b, "weight_low_a": weight_low_a, "weight_low_b": weight_low_b, "weight_lift_low": weight_lift_low, "weight_up_mid": weight_up_mid, "weight_lift_top": weight_lift_top, "weight_out": weight_out}


def conv(field, weight):
    out = lax.conv_general_dilated(field[None].astype(jnp.float32), weight.astype(jnp.float32), (1, 1, 1), "SAME", dimension_numbers=("NDHWC", "DHWIO", "NDHWC"), precision=lax.Precision.HIGHEST)
    return out[0]


def activate(total):
    return jnp.maximum(total, 0.0).astype(jnp.bfloat16)


def pool(field):
    size_x, size_y, size_z, channels = field.shape
    blocks = field.reshape(size_x // 2, 2, size_y // 2, 2, size_z // 2, 2, channels)
    return jnp.max(blocks, axis=(1, 3, 5))


def lift(field, weight):
    size_x, size_y, size_z, channels = field.shape
    out = jnp.einsum("ijkc,cabdo->iajbkdo", field.astype(jnp.float32), weight.astype(jnp.float32), precision=lax.Precision.HIGHEST)
    return out.reshape(2 * size_x, 2 * size_y, 2 * size_z, out.shape[-1]).astype(jnp.bfloat16)


def reference(volume, weight_top, weight_down_a, weight_down_b, weight_low_a, weight_low_b, weight_lift_low, weight_up_mid, weight_lift_top, weight_out):
    field = volume.reshape(NX, NY, NZ, C3)
    skip_top = activate(conv(field, weight_top))
    first_mid = activate(conv(pool(skip_top), weight_down_a))
    skip_mid = activate(conv(first_mid, weight_down_b))
    first_low = activate(conv(pool(skip_mid), weight_low_a))
    coarse_out = activate(conv(first_low, weight_low_b))
    lifted_mid = lift(coarse_out, weight_lift_low)
    merged_mid = activate(conv(jnp.concatenate([lifted_mid, skip_mid], axis=-1), weight_up_mid))
    lifted_top = lift(merged_mid, weight_lift_top)
    decoded = conv(jnp.concatenate([lifted_top, skip_top], axis=-1), weight_out).astype(jnp.bfloat16)
    return decoded.reshape(NX, NY, NZ * C3)
```

```python
import functools

import jax
import jax.numpy as jnp
from jax import lax
from jax.experimental import pallas as pl
from jax.experimental.pallas import tpu as pltpu
from jax.sharding import PartitionSpec as P

F32 = jnp.float32
BF16 = jnp.bfloat16
MESH = pl.DeviceIdType.MESH

DIRS = [
    (dx, dy, dz)
    for dx in (0, -1, 1)
    for dz in (0, -1, 1)
    for dy in (0, -1, 1)
    if (dx, dy, dz) != (0, 0, 0)
]
LOW_DIRS = [
    (dx, dy, dz)
    for dx in (0, -1, 1, -2, 2)
    for dz in (0, -1, 1)
    for dy in (0, -1, 1)
    if (dx, dy, dz) != (0, 0, 0)
]


def dot(a, b):
    return jnp.dot(a, b, preferred_element_type=F32)


def side(step):
    return 0 if step == 1 else 1


SCRATCH = dict(
    k_top=((1728, 64), BF16),
    k_da=((1728, 128), BF16),
    k_db=((3456, 128), BF16),
    k_la=((3456, 256), BF16),
    k_lb=((6912, 256), BF16),
    k_ll=((256, 1024), BF16),
    k_um=((6912, 128), BF16),
    k_lt=((128, 512), BF16),
    k_out=((3456, 64), BF16),
    t_top=((9, 512, 256), BF16),
    t_skip=((9, 512, 256), BF16),
    t_lift=((9, 512, 256), BF16),
    t_da=((9, 256, 256), BF16),
    t_lt=((256, 256), BF16),
    wide=((10, 320, 128), F32),
    vol0=((10, 16, 1280), BF16),
    vol1=((10, 16, 1280), BF16),
    vol2=((10, 16, 1280), BF16),
    skip0=((10, 16, 1280), BF16),
    skip1=((10, 16, 1280), BF16),
    skip2=((10, 16, 1280), BF16),
    lift0=((10, 16, 1280), BF16),
    lift1=((10, 16, 1280), BF16),
    lift2=((10, 16, 1280), BF16),
    vol_a=((2, 4, 16, 128), BF16),
    vol_b=((2, 2, 16, 128), BF16),
    vol_r=((2, 12, 16, 128), BF16),
    skip_a=((2, 4, 16, 128), BF16),
    skip_b=((2, 2, 16, 128), BF16),
    skip_r=((2, 12, 16, 128), BF16),
    tmp=((4, 16, 128), F32),
    top_out=((8, 128, 128), F32),
    part=((4, 128, 256), F32),
    pm=((4, 6, 16, 128), BF16),
    pm_y=((2, 2, 16, 128), BF16),
    pm_r=((2, 3, 3, 2, 16, 128), BF16),
    pm_t=((2, 2, 16, 128), F32),
    pm_wide=((8, 24, 768), F32),
    pm_s=((3, 8, 16, 768), BF16),
    fm_wide=((6, 10, 24, 128), F32),
    fm_s=((6, 64, 1152), BF16),
    sm_out=((4, 8, 8, 128), F32),
    sm=((8, 6, 16, 128), BF16),
    sm_y=((2, 4, 16, 128), BF16),
    sm_r=((2, 3, 3, 4, 16, 128), BF16),
    sm_t=((4, 16, 128), F32),
    pl_t=((2, 4, 8, 128), F32),
    pl_f=((2, 16, 128), F32),
    pl_r=((5, 3, 3, 2, 16, 128), BF16),
    pl_g=((3, 16, 128), F32),
    pl_wide=((8, 10, 16, 128), F32),
    pl_s=((8, 64, 1152), BF16),
    fl_wide=((6, 8, 16, 256), F32),
    fl_s=((6, 48, 2304), BF16),
    jm_wide=((2, 8, 12, 24, 128), F32),
    jm_s=((3, 8, 12, 16, 256), BF16),
    mg_wide=((2, 6, 10, 32, 128), F32),
)
NAMES = list(SCRATCH)
WEIGHTS = ("k_top", "k_da", "k_db", "k_la", "k_lb", "k_ll", "k_um", "k_lt", "k_out")


class Exchange:
    def __init__(self, dirs, message, send, recv, here, sizes):
        self.dirs, self.message = dirs, message
        self.send, self.recv = send, recv
        self.here, self.sizes = here, sizes

    def inside(self, step, sign):
        ok = None
        for at, size, s in zip(self.here, self.sizes, step):
            s = s * sign
            if s == 0:
                continue
            this = at + s < size if s > 0 else at + s >= 0
            ok = this if ok is None else jnp.logical_and(ok, this)
        return ok

    def copy(self, i):
        step = self.dirs[i]
        src, dst = self.message(step)
        there = tuple(at + s for at, s in zip(self.here, step))
        return pltpu.make_async_remote_copy(
            src_ref=src,
            dst_ref=dst,
            send_sem=self.send.at[i],
            recv_sem=self.recv.at[i],
            device_id=there,
            device_id_type=MESH,
        )

    def start(self):
        for i, step in enumerate(self.dirs):
            pl.when(self.inside(step, 1))(lambda i=i: self.copy(i).start())

    def wait_recv(self):
        for i, step in enumerate(self.dirs):
            pl.when(self.inside(step, -1))(lambda i=i: self.copy(i).wait_recv())

    def wait_send(self):
        for i, step in enumerate(self.dirs):
            pl.when(self.inside(step, 1))(lambda i=i: self.copy(i).wait_send())


def kernel(sizes, *refs):
    vol, weights, out = refs[0], refs[1:10], refs[10]
    n = len(NAMES)
    b = dict(zip(NAMES, refs[11 : 11 + n]))
    (load_sem, vol_ss, vol_rs, skip_ss, skip_rs, pm_ss, pm_rs, sm_ss, sm_rs, pl_ss, pl_rs) = refs[11 + n :]
    here = tuple(lax.axis_index(name) for name in ("gx", "gy", "gz"))
    gx, gy, gz = here
    tile = lambda t: slice(128 * t, 128 * t + 128)

    vol1 = b["vol1"]
    vol_load = pltpu.make_async_copy(vol, vol1.at[1:9, :, 128:1152], load_sem.at[9])
    vol_load.start()
    loads = {}
    for i, name in enumerate(WEIGHTS):
        loads[name] = pltpu.make_async_copy(weights[i], b[name], load_sem.at[i])
        loads[name].start()

    def zero(ref, *at):
        if at:
            ref[at] = jnp.zeros(ref.at[at].shape, ref.dtype)
        else:
            ref[...] = jnp.zeros(ref.shape, ref.dtype)

    everything = slice(None)
    for name in ("vol1", "skip1"):
        zero(b[name], slice(0, 1))
        zero(b[name], slice(9, 10))
        zero(b[name], slice(1, 9), everything, tile(0))
        zero(b[name], slice(1, 9), everything, tile(9))
    for name in ("vol_r", "skip_r", "pm_r", "sm_r", "pl_r"):
        zero(b[name])
    for name, width, lo, hi in (("pm", 4, 1, 3), ("sm", 8, 2, 6)):
        zero(b[name], slice(0, lo))
        zero(b[name], slice(hi, width))
        zero(b[name], slice(lo, hi), slice(0, 1))
        zero(b[name], slice(lo, hi), slice(5, 6))

    barrier = pltpu.get_barrier_semaphore()
    low_x = Exchange(LOW_DIRS, None, None, None, here, sizes)
    for step in LOW_DIRS:

        @pl.when(low_x.inside(step, 1))
        def _(step=step):
            pl.semaphore_signal(
                barrier,
                inc=1,
                device_id=tuple(at + s for at, s in zip(here, step)),
                device_id_type=MESH,
            )

    def reach(at, size, far):
        count = jnp.int32(1)
        for s in range(1, far + 1):
            count = count + jnp.where(at >= s, 1, 0) + jnp.where(at + s < size, 1, 0)
        return count

    greeted = reach(gx, sizes[0], 2) * reach(gy, sizes[1], 1) * reach(gz, sizes[2], 1) - 1

    wide = b["wide"]
    tmp = b["tmp"]

    def stage_top(cells, a, bb):
        for x in range(1, 9):
            for t in range(1, 9):
                wide[t, 32 * x + 8 : 32 * x + 24, :] = cells[x, :, tile(t)].astype(F32)
        for s, y in ((0, 15), (1, 0)):
            for tp in range(4):
                pair = [
                    wide[2 * tp + h + 1, pl.ds(32 + 8 + y, 8, stride=32), :] for h in range(2)
                ]
                a[s, tp] = jnp.concatenate(pair, axis=0).astype(BF16)
            for xs, x in ((0, 8), (1, 1)):
                for t in range(8):
                    tmp[2 * s + xs, t : t + 1, :] = wide[t + 1, 32 * x + 8 + y : 32 * x + 9 + y, :]
                for t in range(8, 16):
                    tmp[2 * s + xs, t : t + 1, :] = jnp.zeros((1, 128), F32)
                bb[s, xs] = tmp[2 * s + xs].astype(BF16)

    def top_message(cells, a, bb, r):
        def message(step):
            dx, dy, dz = step
            if dy == 0:
                sx = {0: slice(1, 9), 1: slice(8, 9), -1: slice(1, 2)}[dx]
                tx = {0: slice(1, 9), 1: slice(0, 1), -1: slice(9, 10)}[dx]
                sz = {0: slice(128, 1152), 1: tile(8), -1: tile(1)}[dz]
                tz = {0: slice(128, 1152), 1: tile(0), -1: tile(9)}[dz]
                return cells.at[sx, :, sz], cells.at[tx, :, tz]
            s = side(dy)
            if dx == 0 and dz == 0:
                return a.at[s], r.at[s, 0:4]
            if dz == 0:
                return bb.at[s, side(dx)], r.at[s, 6 + side(dx)]
            tp = 3 if dz == 1 else 0
            slot = 4 + side(dz) if dx == 0 else 8 + 2 * side(dx) + side(dz)
            return a.at[s, tp], r.at[s, slot]

        return message

    def shift_top(cells, r, below, above):
        for x in range(10):
            for t in range(10) if x in (0, 9) else (0, 9):
                wide[t, 32 * x + 8 : 32 * x + 24, :] = cells[x, :, tile(t)].astype(F32)
        for s, row in ((0, 7), (1, 24)):
            rows = pl.ds(32 + row, 8, stride=32)
            for tp in range(4):
                both = r[s, tp].astype(F32)
                wide[2 * tp + 1, rows, :] = both[0:8]
                wide[2 * tp + 2, rows, :] = both[8:16]
            for zs, t, half in ((0, 0, 8), (1, 9, 0)):
                wide[t, rows, :] = r[s, 4 + zs].astype(F32)[half : half + 8]
            for xs, x, keep in ((0, 0, 7), (1, 9, 0)):
                at = slice(32 * x + row, 32 * x + row + 1)
                tmp[xs] = r[s, 6 + xs].astype(F32)
                for t in range(8):
                    wide[t + 1, at, :] = tmp[xs, t : t + 1, :]
                for zs, t, half in ((0, 0, 8), (1, 9, 0)):
                    tmp[2 + zs] = r[s, 8 + 2 * xs + zs].astype(F32)
                    wide[t, at, :] = tmp[2 + zs, half + keep : half + keep + 1, :]
        for x in range(10):
            for t in range(10):
                below[x, :, tile(t)] = wide[t, 32 * x + 7 : 32 * x + 23, :].astype(BF16)
                above[x, :, tile(t)] = wide[t, 32 * x + 9 : 32 * x + 25, :].astype(BF16)

    def conv_top(shifted, kernels, emit):
        @pl.loop(0, 4)
        def _(g):
            lanes = pl.ds(pl.multiple_of(256 * g, 256), 512)
            total = None
            for dx in range(3):
                for dy in range(3):
                    piece = shifted[dy][dx : dx + 8, :, lanes].reshape(128, 512)
                    term = dot(piece, kernels[3 * dx + dy])
                    total = term if total is None else total + term
            emit(g, total)

    low_half = lax.broadcasted_iota(jnp.int32, (64, 128), 1) < 64

    def band(raw, stride, first, target):
        for k in range(9):
            doubled = []
            for dz in range(3):
                at = (3 * k + dz) * stride + first
                half = raw[at : at + 64, :].astype(F32)
                doubled.append(jnp.concatenate([half, half], axis=1))
            nothing = jnp.zeros((64, 128), F32)
            pick = lambda dz: doubled[dz] if 0 <= dz < 3 else nothing
            for zi in range(8):
                for h in range(2):
                    block = jnp.where(low_half, pick(zi - 1 - 2 * h), pick(zi - 2 - 2 * h))
                    target[k, 64 * zi : 64 * zi + 64, tile(h)] = block.astype(BF16)

    vol_load.wait()
    stage_top(vol1, b["vol_a"], b["vol_b"])
    vol_x = Exchange(
        DIRS, top_message(vol1, b["vol_a"], b["vol_b"], b["vol_r"]), vol_ss, vol_rs, here, sizes
    )
    pl.semaphore_wait(barrier, greeted)
    vol_x.start()
    loads["k_top"].wait()
    band(b["k_top"], 64, 0, b["t_top"])
    loads["k_da"].wait()
    for k in range(9):
        for zi in range(4):
            for zo in range(2):
                dz = zi - zo
                if 0 <= dz < 3:
                    block = b["k_da"][64 * (3 * k + dz) : 64 * (3 * k + dz) + 64, :]
                else:
                    block = jnp.zeros((64, 128), BF16)
                b["t_da"][k, 64 * zi : 64 * zi + 64, tile(zo)] = block
    vol_x.wait_recv()
    shift_top(vol1, b["vol_r"], b["vol0"], b["vol2"])
    top_out = b["top_out"]
    skip1 = b["skip1"]

    def emit_top(g, total):
        kept = jnp.maximum(total, 0.0)
        for h in range(2):
            top_out[2 * g + h] = kept[:, tile(h)]
        skip1[1:9, :, pl.ds(pl.multiple_of(256 * g + 128, 128), 256)] = kept.astype(BF16).reshape(8, 16, 256)

    conv_top((b["vol0"], vol1, b["vol2"]), b["t_top"], emit_top)

    pm, pm_wide = b["pm"], b["pm_wide"]
    first_lanes = lax.broadcasted_iota(jnp.int32, (8, 128), 1) < 64
    for xp in range(2):
        for q in range(4):
            held = []
            for xm in (2 * xp, 2 * xp + 1):
                found = []
                for j in (2 * q, 2 * q + 1):
                    parts = [
                        top_out[j, pl.ds(16 * x + p, 8, stride=2), :]
                        for x in (2 * xm, 2 * xm + 1)
                        for p in range(2)
                    ]
                    most = jnp.maximum(jnp.maximum(parts[0], parts[1]), jnp.maximum(parts[2], parts[3]))
                    found.append(jnp.maximum(most, pltpu.roll(most, 64, 1)))
                cell = jnp.where(first_lanes, found[0], found[1])
                pm_wide[xm + 2, 2:10, tile(q + 1)] = cell
                held.append(cell)
            pm[xp + 1, q + 1] = jnp.concatenate(held, axis=0).astype(BF16)
    for s, y in ((0, 6), (1, 0)):
        for xm in range(4):
            for q in range(4):
                row = 4 * q + 2 * (xm % 2)
                b["pm_t"][s, xm // 2, row : row + 2, :] = pm_wide[xm + 2, y + 2 : y + 4, tile(q + 1)]
        for xp in range(2):
            b["pm_y"][s, xp] = b["pm_t"][s, xp].astype(BF16)

    def pm_message(step):
        dx, dy, dz = step
        if dy == 0:
            sx = {0: slice(1, 3), 1: slice(2, 3), -1: slice(1, 2)}[dx]
            tx = {0: slice(1, 3), 1: slice(0, 1), -1: slice(3, 4)}[dx]
            sz = {0: slice(1, 5), 1: slice(4, 5), -1: slice(1, 2)}[dz]
            tz = {0: slice(1, 5), 1: slice(0, 1), -1: slice(5, 6)}[dz]
            return pm.at[sx, sz], pm.at[tx, tz]
        s = side(dy)
        xs = {0: slice(0, 2), 1: slice(1, 2), -1: slice(0, 1)}[dx]
        return b["pm_y"].at[s, xs], b["pm_r"].at[s, dx + 1, dz + 1, xs]

    pm_x = Exchange(DIRS, pm_message, pm_ss, pm_rs, here, sizes)
    pm_x.start()

    stage_top(skip1, b["skip_a"], b["skip_b"])
    skip_x = Exchange(
        DIRS, top_message(skip1, b["skip_a"], b["skip_b"], b["skip_r"]), skip_ss, skip_rs, here, sizes
    )
    skip_x.start()
    loads["k_out"].wait()
    band(b["k_out"], 128, 64, b["t_skip"])

    pm_x.wait_recv()
    for xp in range(4):
        for zp in range(6):
            if 1 <= xp < 3 and 1 <= zp < 5:
                continue
            both = pm[xp, zp].astype(F32)
            pm_wide[2 * xp, 2:10, tile(zp)] = both[0:8]
            pm_wide[2 * xp + 1, 2:10, tile(zp)] = both[8:16]
    for s, y in ((0, 0), (1, 10)):
        for dx in (-1, 0, 1):
            for xp in {0: (0, 1), 1: (1,), -1: (0,)}[dx]:
                base = {0: 2 + 2 * xp, 1: 0, -1: 6}[dx]
                for dz in (-1, 0, 1):
                    slot = b["pm_t"].at[0, (dz + 1) % 2]
                    slot[...] = b["pm_r"][s, dx + 1, dz + 1, xp].astype(F32)
                    for q in {0: (0, 1, 2, 3), 1: (3,), -1: (0,)}[dz]:
                        to = {0: q + 1, 1: 0, -1: 5}[dz]
                        for xi in range(2):
                            row = 4 * q + 2 * xi
                            pm_wide[base + xi, y : y + 2, tile(to)] = slot[row : row + 2, :]
    pm_s = b["pm_s"]
    for x in range(8):
        for dy in range(3):
            pm_s[dy, x] = pm_wide[x, dy : dy + 16, :].astype(BF16)

    def flag(ok):
        return jnp.where(ok, 1.0, 0.0).astype(F32)

    def valid(at, local, size, first, index):
        place = at * local + first + index
        return flag(jnp.logical_and(place >= 0, place < local * size))

    def row_mask(rows, lanes, used, at, local, size, first):
        place = lax.broadcasted_iota(jnp.int32, (rows, lanes), 0)
        whole = place + (at * local + first)
        ok = jnp.logical_and(whole >= 0, whole < local * size)
        return jnp.logical_and(ok, place < used)

    fm_wide = b["fm_wide"]
    mid_rows = row_mask(16, 128, 10, gy, 8, sizes[1], -1)
    for j in range(5):
        total = None
        for dx in range(3):
            for dy in range(3):
                piece = pm_s[dy, dx : dx + 6, :, 128 * j : 128 * j + 256].reshape(96, 256)
                term = dot(piece, b["t_da"][3 * dx + dy])
                total = term if total is None else total + term
        total = jnp.maximum(total, 0.0)
        for x in range(6):
            for h in range(2):
                z = 2 * j + h
                keep = valid(gx, 4, sizes[0], -1, x) * valid(gz, 8, sizes[2], -1, z)
                cell = total[16 * x : 16 * x + 16, tile(h)]
                fm_wide[x, z, 0:16, :] = jnp.where(mid_rows, cell, 0.0) * keep

    def gather(wide_ref, target, xs, pairs, lanes):
        for x in range(xs):
            for zp in range(pairs):
                for dy in range(3):
                    for dz in range(3):
                        both = jnp.concatenate(
                            [wide_ref[x, 2 * zp + h + dz, dy : dy + 8, :] for h in range(2)], axis=0
                        )
                        at = (3 * dy + dz) * lanes
                        target[x, 16 * zp : 16 * zp + 16, at : at + lanes] = both.astype(BF16)

    def conv_rows(source, xs, kernels):
        rows, depth = source.shape[1], source.shape[2]
        total = None
        for dx in range(3):
            piece = source[dx : dx + xs].reshape(xs * rows, depth)
            term = dot(piece, kernels[dx * depth : (dx + 1) * depth, :])
            total = term if total is None else total + term
        return jnp.maximum(total, 0.0)

    gather(fm_wide, b["fm_s"], 6, 4, 128)
    loads["k_db"].wait()
    sm_out, sm = b["sm_out"], b["sm"]
    skip_mid = conv_rows(b["fm_s"], 4, b["k_db"])
    sm_out[...] = skip_mid.reshape(4, 8, 8, 128)
    sm[2:6, 1:5] = skip_mid.astype(BF16).reshape(4, 4, 16, 128)

    pl_t, pl_f, pl_r = b["pl_t"], b["pl_f"], b["pl_r"]
    for x in range(2):
        for z in range(4):
            parts = [sm_out[2 * x + i, 2 * z + k] for i in range(2) for k in range(2)]
            pl_t[x, z] = jnp.maximum(jnp.maximum(parts[0], parts[1]), jnp.maximum(parts[2], parts[3]))
            pl_f[x, 4 * z : 4 * z + 4, :] = jnp.maximum(
                pl_t[x, z, pl.ds(0, 4, stride=2), :], pl_t[x, z, pl.ds(1, 4, stride=2), :]
            )
        pl_r[2, 1, 1, x] = pl_f[x].astype(BF16)

    def pl_message(step):
        dx, dy, dz = step
        planes = {2: slice(1, 2), -2: slice(0, 1)}.get(dx, slice(0, 2))
        return pl_r.at[2, 1, 1, planes], pl_r.at[2 - dx, 1 - dz, 1 - dy, planes]

    pl_x = Exchange(LOW_DIRS, pl_message, pl_ss, pl_rs, here, sizes)
    pl_x.start()

    sm_t = b["sm_t"]
    for s, y in ((0, 6), (1, 0)):
        for x in range(4):
            for z in range(8):
                sm_t[x, 2 * z : 2 * z + 2, :] = sm_out[x, z, y : y + 2, :]
            b["sm_y"][s, x] = sm_t[x].astype(BF16)

    def sm_message(step):
        dx, dy, dz = step
        if dy == 0:
            sx = {0: slice(2, 6), 1: slice(4, 6), -1: slice(2, 4)}[dx]
            tx = {0: slice(2, 6), 1: slice(0, 2), -1: slice(6, 8)}[dx]
            sz = {0: slice(1, 5), 1: slice(4, 5), -1: slice(1, 2)}[dz]
            tz = {0: slice(1, 5), 1: slice(0, 1), -1: slice(5, 6)}[dz]
            return sm.at[sx, sz], sm.at[tx, tz]
        s = side(dy)
        xs = {0: slice(0, 4), 1: slice(2, 4), -1: slice(0, 2)}[dx]
        return b["sm_y"].at[s, xs], b["sm_r"].at[s, dx + 1, dz + 1, xs]

    sm_x = Exchange(DIRS, sm_message, sm_ss, sm_rs, here, sizes)
    sm_x.start()

    skip_x.wait_recv()
    shift_top(skip1, b["skip_r"], b["skip0"], b["skip2"])

    def emit_part(g, total):
        b["part"][g] = total

    conv_top((b["skip0"], skip1, b["skip2"]), b["t_skip"], emit_part)
    band(b["k_out"], 128, 0, b["t_lift"])

    pl_x.wait_recv()
    pl_wide, pl_g = b["pl_wide"], b["pl_g"]
    planes = [(0, 1), (1, 0), (1, 1), (2, 0), (2, 1), (3, 0), (3, 1), (4, 0)]
    for x, (d, p) in enumerate(planes):
        for zs in range(3):
            for ys in range(3):
                pl_g[ys] = pl_r[d, zs, ys, p].astype(F32)
            for z, to in {0: ((1, 0), (2, 1), (3, 2)), 1: ((0, 3), (1, 4), (2, 5), (3, 6)), 2: ((0, 7), (1, 8), (2, 9))}[zs]:
                pl_wide[x, to, 0:3, :] = pl_g[0, 4 * z + 1 : 4 * z + 4, :]
                pl_wide[x, to, 3:7, :] = pl_g[1, 4 * z : 4 * z + 4, :]
                pl_wide[x, to, 7:10, :] = pl_g[2, 4 * z : 4 * z + 3, :]
    gather(pl_wide, b["pl_s"], 8, 4, 128)
    loads["k_la"].wait()
    first_low = conv_rows(b["pl_s"], 6, b["k_la"])
    fl_wide = b["fl_wide"]
    low_rows = row_mask(8, 256, 8, gy, 4, sizes[1], -2)
    for x in range(6):
        for z in range(8):
            keep = valid(gx, 2, sizes[0], -2, x) * valid(gz, 4, sizes[2], -2, z)
            at = 64 * x + 8 * z
            fl_wide[x, z, 0:8, :] = jnp.where(low_rows, first_low[at : at + 8, :], 0.0) * keep
            fl_wide[x, z, 8:16, :] = jnp.zeros((8, 256), F32)
    gather(fl_wide, b["fl_s"], 6, 3, 256)
    loads["k_lb"].wait()
    coarse = conv_rows(b["fl_s"], 4, b["k_lb"])
    coarse_rows = row_mask(8, 256, 6, gy, 4, sizes[1], -1)
    cells = []
    for x in range(4):
        for z in range(6):
            keep = valid(gx, 2, sizes[0], -1, x) * valid(gz, 4, sizes[2], -1, z)
            at = 48 * x + 8 * z
            cells.append(jnp.where(coarse_rows, coarse[at : at + 8, :], 0.0) * keep)
    coarse = jnp.concatenate(cells, axis=0).astype(BF16)

    jm_wide, jm_s = b["jm_wide"], b["jm_s"]
    loads["k_ll"].wait()
    lifted = dot(coarse, b["k_ll"][...])
    for x in range(4):
        for z in range(6):
            for i in range(2):
                for h in range(2):
                    for k in range(2):
                        at = 48 * x + 8 * z
                        jm_wide[0, 2 * x + i, 2 * z + k, pl.ds(h, 8, stride=2), :] = lifted[
                            at : at + 8, tile(4 * i + 2 * h + k)
                        ]

    sm_x.wait_recv()
    for x in range(8):
        for zp in range(6):
            both = sm[x, zp].astype(F32)
            for h in range(2):
                jm_wide[1, x, 2 * zp + h, 2:10, :] = both[8 * h : 8 * h + 8]
    for s, y in ((0, 0), (1, 10)):
        for dx in (-1, 0, 1):
            for xi in {0: (0, 1, 2, 3), 1: (2, 3), -1: (0, 1)}[dx]:
                x = {0: 2 + xi, 1: xi - 2, -1: 6 + xi}[dx]
                for dz in (-1, 0, 1):
                    slot = sm_t.at[dz + 1]
                    slot[...] = b["sm_r"][s, dx + 1, dz + 1, xi].astype(F32)
                    for z in {0: range(8), 1: (6, 7), -1: (0, 1)}[dz]:
                        to = {0: z + 2, 1: z - 6, -1: 10 + z}[dz]
                        jm_wide[1, x, to, y : y + 2, :] = slot[2 * z : 2 * z + 2, :]
    for x in range(8):
        for z in range(12):
            for dy in range(3):
                for h in range(2):
                    jm_s[dy, x, z, :, tile(h)] = jm_wide[h, x, z, dy : dy + 16, :].astype(BF16)

    mg_wide = b["mg_wide"]
    mg_wide[...] = jnp.zeros(mg_wide.shape, F32)
    loads["k_um"].wait()

    @pl.loop(0, 6)
    def _(x):
        total = None
        for dx in range(3):
            for dy in range(3):
                for dz in range(3):
                    piece = jm_s[dy, x + dx, dz : dz + 10].reshape(160, 256)
                    at = 256 * (9 * dx + 3 * dy + dz)
                    term = dot(piece, b["k_um"][at : at + 256, :])
                    total = term if total is None else total + term
        total = jnp.maximum(total, 0.0)
        inside = valid(gx, 4, sizes[0], -1, x)
        for z in range(10):
            keep = inside * valid(gz, 8, sizes[2], -1, z)
            cell = jnp.where(mid_rows, total[16 * z : 16 * z + 16, :], 0.0) * keep
            for h in range(2):
                mg_wide[h, x, z, pl.ds(h, 16, stride=2), :] = cell

    t_lt = b["t_lt"]
    loads["k_lt"].wait()
    for i in range(2):
        for h in range(2):
            t_lt[128 * h : 128 * h + 128, tile(i)] = b["k_lt"][:, tile(2 * i + h)]
    lift = (b["lift0"], b["lift1"], b["lift2"])
    for x in range(6):
        for dy in range(3):
            halves = [mg_wide[h, x, :, dy + 1 : dy + 17, :].astype(BF16).reshape(160, 128) for h in range(2)]
            piece = jnp.concatenate(halves, axis=1)
            value = dot(piece, t_lt[...]).astype(BF16)
            for i in range(2):
                to = 2 * x + i - 1
                if 0 <= to < 10:
                    for z in range(10):
                        lift[dy][to, :, tile(z)] = value[16 * z : 16 * z + 16, tile(i)]

    def emit_out(g, total):
        total = total + b["part"][g]
        out[:, :, pl.ds(pl.multiple_of(256 * g, 256), 256)] = total.astype(BF16).reshape(8, 16, 256)

    conv_top(lift, b["t_lift"], emit_out)
    for exchange in (vol_x, pm_x, skip_x, pl_x, sm_x):
        exchange.wait_send()


def body(sizes, volume, *weights):
    shapes = ((1728, 64), (1728, 128), (3456, 128), (3456, 256), (6912, 256), (256, 1024), (6912, 128), (128, 512), (3456, 64))
    flat = [w.reshape(s) for w, s in zip(weights, shapes)]
    any_space = pl.BlockSpec(memory_space=pl.ANY)
    few, many = len(DIRS), len(LOW_DIRS)
    counts = (10, few, few, few, few, few, few, few, few, many, many)
    return pl.pallas_call(
        functools.partial(kernel, sizes),
        out_shape=jax.ShapeDtypeStruct(volume.shape, BF16),
        in_specs=[any_space] * 10,
        out_specs=pl.BlockSpec(memory_space=pltpu.VMEM),
        scratch_shapes=[pltpu.VMEM(s, d) for s, d in SCRATCH.values()]
        + [pltpu.SemaphoreType.DMA((c,)) for c in counts],
        compiler_params=pltpu.CompilerParams(
            collective_id=0, has_side_effects=True, vmem_limit_bytes=56 * 1024 * 1024
        ),
    )(volume, *flat)


def solution(mesh):
    placed = (P("gx", "gy", "gz"),) + (P(),) * 9
    sizes = tuple(mesh.shape[name] for name in ("gx", "gy", "gz"))
    return jax.shard_map(
        functools.partial(body, sizes),
        mesh=mesh,
        in_specs=placed,
        out_specs=P("gx", "gy", "gz"),
        check_vma=False,
    )
```

```python
import functools

import jax
import jax.numpy as jnp
from jax import lax
from jax.experimental import pallas as pl
from jax.experimental.pallas import tpu as pltpu
from jax.sharding import PartitionSpec as P

F32 = jnp.float32
BF16 = jnp.bfloat16
MESH = pl.DeviceIdType.MESH


def directions(far):
    steps = [
        (dx, dy, dz)
        for dx in range(-far, far + 1)
        for dy in (-1, 0, 1)
        for dz in (-1, 0, 1)
        if (dx, dy, dz) != (0, 0, 0)
    ]
    return sorted(steps, key=lambda step: -sum(abs(s) for s in step))


DIRS = directions(1)
LOW_DIRS = directions(2)


def dot(a, b):
    return jnp.dot(a, b, preferred_element_type=F32)


def side(step):
    return 0 if step == 1 else 1


SCRATCH = dict(
    k_top=((1728, 64), BF16),
    k_da=((1728, 128), BF16),
    k_db=((3456, 128), BF16),
    k_la=((3456, 256), BF16),
    k_lb=((6912, 256), BF16),
    k_ll=((256, 1024), BF16),
    k_um=((6912, 128), BF16),
    k_lt=((512, 128), BF16),
    k_out=((1728, 128), BF16),
    raw_ll=((256, 4, 2, 128), BF16),
    t_top=((9, 512, 256), BF16),
    t_skip=((9, 512, 256), BF16),
    t_lift=((9, 512, 256), BF16),
    t_da=((9, 256, 256), BF16),
    t_lt=((256, 256), BF16),
    t_um=((2, 9, 512, 256), BF16),
    wide=((10, 320, 128), F32),
    vol0=((10, 16, 1280), BF16),
    vol1=((10, 16, 1280), BF16),
    vol2=((10, 16, 1280), BF16),
    skip0=((10, 16, 1280), BF16),
    skip1=((10, 16, 1280), BF16),
    skip2=((10, 16, 1280), BF16),
    lift0=((10, 16, 1280), BF16),
    lift1=((10, 16, 1280), BF16),
    lift2=((10, 16, 1280), BF16),
    vol_a=((2, 4, 16, 128), BF16),
    vol_b=((2, 2, 16, 128), BF16),
    vol_r=((2, 12, 16, 128), BF16),
    skip_a=((2, 4, 16, 128), BF16),
    skip_b=((2, 2, 16, 128), BF16),
    skip_r=((2, 12, 16, 128), BF16),
    tmp=((4, 16, 128), F32),
    top_out=((8, 128, 128), F32),
    part=((512, 256), F32),
    pm=((4, 6, 16, 128), BF16),
    pm_y=((2, 2, 16, 128), BF16),
    pm_r=((2, 3, 3, 2, 16, 128), BF16),
    pm_t=((2, 2, 16, 128), F32),
    pm_wide=((8, 24, 768), F32),
    pm_s=((3, 8, 16, 768), BF16),
    fm_wide=((6, 10, 24, 128), F32),
    fm_s=((6, 64, 1152), BF16),
    sm_out=((4, 8, 8, 128), F32),
    sm=((8, 6, 16, 128), BF16),
    sm_y=((2, 4, 16, 128), BF16),
    sm_r=((2, 3, 3, 4, 16, 128), BF16),
    sm_t=((4, 16, 128), F32),
    pl_t=((2, 4, 8, 128), F32),
    pl_f=((2, 16, 128), F32),
    pl_r=((5, 3, 3, 2, 16, 128), BF16),
    pl_g=((3, 16, 128), F32),
    pl_wide=((8, 10, 16, 128), F32),
    pl_s=((8, 64, 1152), BF16),
    fl_wide=((6, 8, 16, 256), F32),
    fl_s=((6, 48, 2304), BF16),
    jm_wide=((2, 8, 12, 24, 128), F32),
    jm_s=((2, 3, 8, 16, 1536), BF16),
    jm_part=((480, 256), F32),
    mg_wide=((2, 6, 10, 32, 128), F32),
)
NAMES = list(SCRATCH)
WEIGHTS = ("k_top", "k_da", "k_db", "k_la", "k_lb", "raw_ll", "k_um", "k_lt", "k_out")
ORDER = ("k_top", "k_da", "k_out", "k_um", "raw_ll", "k_lt", "k_db", "k_la", "k_lb")


class Exchange:
    def __init__(self, dirs, message, send, recv, here, sizes):
        self.dirs, self.message = dirs, message
        self.send, self.recv = send, recv
        self.here, self.sizes = here, sizes

    def inside(self, step, sign):
        ok = None
        for at, size, s in zip(self.here, self.sizes, step):
            s = s * sign
            if s == 0:
                continue
            this = at + s < size if s > 0 else at + s >= 0
            ok = this if ok is None else jnp.logical_and(ok, this)
        return ok

    def copy(self, i):
        step = self.dirs[i]
        src, dst = self.message(step)
        there = tuple(at + s for at, s in zip(self.here, step))
        return pltpu.make_async_remote_copy(
            src_ref=src,
            dst_ref=dst,
            send_sem=self.send.at[i],
            recv_sem=self.recv.at[i],
            device_id=there,
            device_id_type=MESH,
        )

    def start(self):
        for i, step in enumerate(self.dirs):
            pl.when(self.inside(step, 1))(lambda i=i: self.copy(i).start())

    def wait_recv(self):
        for i, step in enumerate(self.dirs):
            pl.when(self.inside(step, -1))(lambda i=i: self.copy(i).wait_recv())

    def wait_send(self):
        for i, step in enumerate(self.dirs):
            pl.when(self.inside(step, 1))(lambda i=i: self.copy(i).wait_send())


def kernel(sizes, *refs):
    vol, weights, out = refs[0], refs[1:10], refs[10]
    n = len(NAMES)
    b = dict(zip(NAMES, refs[11 : 11 + n]))
    (load_sem, vol_ss, vol_rs, skip_ss, skip_rs, pm_ss, pm_rs, sm_ss, sm_rs, pl_ss, pl_rs) = refs[11 + n :]
    here = tuple(lax.axis_index(name) for name in ("gx", "gy", "gz"))
    gx, gy, gz = here
    tile = lambda t: slice(128 * t, 128 * t + 128)

    vol1 = b["vol1"]
    vol_load = pltpu.make_async_copy(vol, vol1.at[1:9, :, 128:1152], load_sem.at[9])
    vol_load.start()
    loads = {}
    for name in ORDER:
        i = WEIGHTS.index(name)
        loads[name] = pltpu.make_async_copy(weights[i], b[name], load_sem.at[i])
        loads[name].start()

    def zero(ref, *at):
        if at:
            ref[at] = jnp.zeros(ref.at[at].shape, ref.dtype)
        else:
            ref[...] = jnp.zeros(ref.shape, ref.dtype)

    everything = slice(None)
    for name in ("vol1", "skip1"):
        zero(b[name], slice(0, 1))
        zero(b[name], slice(9, 10))
        zero(b[name], slice(1, 9), everything, tile(0))
        zero(b[name], slice(1, 9), everything, tile(9))
    for name in ("vol_r", "skip_r", "pm_r", "sm_r", "pl_r"):
        zero(b[name])
    mg_wide = b["mg_wide"]
    zero(mg_wide)
    for name, width, lo, hi in (("pm", 4, 1, 3), ("sm", 8, 2, 6)):
        zero(b[name], slice(0, lo))
        zero(b[name], slice(hi, width))
        zero(b[name], slice(lo, hi), slice(0, 1))
        zero(b[name], slice(lo, hi), slice(5, 6))

    barrier = pltpu.get_barrier_semaphore()
    low_x = Exchange(LOW_DIRS, None, None, None, here, sizes)
    for step in LOW_DIRS:

        @pl.when(low_x.inside(step, 1))
        def _(step=step):
            pl.semaphore_signal(
                barrier,
                inc=1,
                device_id=tuple(at + s for at, s in zip(here, step)),
                device_id_type=MESH,
            )

    def reach(at, size, far):
        count = jnp.int32(1)
        for s in range(1, far + 1):
            count = count + jnp.where(at >= s, 1, 0) + jnp.where(at + s < size, 1, 0)
        return count

    greeted = reach(gx, sizes[0], 2) * reach(gy, sizes[1], 1) * reach(gz, sizes[2], 1) - 1

    wide = b["wide"]
    tmp = b["tmp"]

    def stage_top(cells, a, bb):
        for x in range(1, 9):
            for t in range(1, 9):
                wide[t, 32 * x + 8 : 32 * x + 24, :] = cells[x, :, tile(t)].astype(F32)
        for s, y in ((0, 15), (1, 0)):
            for tp in range(4):
                pair = [
                    wide[2 * tp + h + 1, pl.ds(32 + 8 + y, 8, stride=32), :] for h in range(2)
                ]
                a[s, tp] = jnp.concatenate(pair, axis=0).astype(BF16)
            for xs, x in ((0, 8), (1, 1)):
                for t in range(8):
                    tmp[2 * s + xs, t : t + 1, :] = wide[t + 1, 32 * x + 8 + y : 32 * x + 9 + y, :]
                for t in range(8, 16):
                    tmp[2 * s + xs, t : t + 1, :] = jnp.zeros((1, 128), F32)
                bb[s, xs] = tmp[2 * s + xs].astype(BF16)

    def top_message(cells, a, bb, r):
        def message(step):
            dx, dy, dz = step
            if dy == 0:
                sx = {0: slice(1, 9), 1: slice(8, 9), -1: slice(1, 2)}[dx]
                tx = {0: slice(1, 9), 1: slice(0, 1), -1: slice(9, 10)}[dx]
                sz = {0: slice(128, 1152), 1: tile(8), -1: tile(1)}[dz]
                tz = {0: slice(128, 1152), 1: tile(0), -1: tile(9)}[dz]
                return cells.at[sx, :, sz], cells.at[tx, :, tz]
            s = side(dy)
            if dx == 0 and dz == 0:
                return a.at[s], r.at[s, 0:4]
            if dz == 0:
                return bb.at[s, side(dx)], r.at[s, 6 + side(dx)]
            tp = 3 if dz == 1 else 0
            slot = 4 + side(dz) if dx == 0 else 8 + 2 * side(dx) + side(dz)
            return a.at[s, tp], r.at[s, slot]

        return message

    def shift_top(cells, r, below, above):
        for x in range(10):
            for t in range(10) if x in (0, 9) else (0, 9):
                wide[t, 32 * x + 8 : 32 * x + 24, :] = cells[x, :, tile(t)].astype(F32)
        for s, row in ((0, 7), (1, 24)):
            rows = pl.ds(32 + row, 8, stride=32)
            for tp in range(4):
                both = r[s, tp].astype(F32)
                wide[2 * tp + 1, rows, :] = both[0:8]
                wide[2 * tp + 2, rows, :] = both[8:16]
            for zs, t, half in ((0, 0, 8), (1, 9, 0)):
                wide[t, rows, :] = r[s, 4 + zs].astype(F32)[half : half + 8]
            for xs, x, keep in ((0, 0, 7), (1, 9, 0)):
                at = slice(32 * x + row, 32 * x + row + 1)
                tmp[xs] = r[s, 6 + xs].astype(F32)
                for t in range(8):
                    wide[t + 1, at, :] = tmp[xs, t : t + 1, :]
                for zs, t, half in ((0, 0, 8), (1, 9, 0)):
                    tmp[2 + zs] = r[s, 8 + 2 * xs + zs].astype(F32)
                    wide[t, at, :] = tmp[2 + zs, half + keep : half + keep + 1, :]
        for x in range(10):
            for t in range(10):
                below[x, :, tile(t)] = wide[t, 32 * x + 7 : 32 * x + 23, :].astype(BF16)
                above[x, :, tile(t)] = wide[t, 32 * x + 9 : 32 * x + 25, :].astype(BF16)

    def conv_top(shifted, kernels):
        total = None
        for dx in range(3):
            for dy in range(3):
                piece = jnp.concatenate(
                    [
                        shifted[dy][dx : dx + 8, :, 256 * g : 256 * g + 512].reshape(128, 512)
                        for g in range(4)
                    ],
                    axis=0,
                )
                term = dot(piece, kernels[3 * dx + dy])
                total = term if total is None else total + term
        return total

    low_half = lax.broadcasted_iota(jnp.int32, (64, 128), 1) < 64

    def band(block, target, k):
        nothing = jnp.zeros((64, 128), F32)
        blocks = [block(dz) for dz in range(3)]
        pick = lambda dz: blocks[dz] if 0 <= dz < 3 else nothing
        for zi in range(8):
            for h in range(2):
                both = jnp.where(low_half, pick(zi - 1 - 2 * h), pick(zi - 2 - 2 * h))
                target[k, 64 * zi : 64 * zi + 64, tile(h)] = both.astype(BF16)

    def pairs(block, count, depth, target):
        for zi in range(count):
            for zo in range(count - 2):
                value = block(zi - zo) if 0 <= zi - zo < 3 else jnp.zeros((depth, 128), BF16)
                target[depth * zi : depth * zi + depth, tile(zo)] = value

    eye = jnp.where(
        lax.broadcasted_iota(jnp.int32, (128, 128), 0) == lax.broadcasted_iota(jnp.int32, (128, 128), 1),
        1.0,
        0.0,
    ).astype(BF16)

    def turned(block):
        return lax.dot_general(eye, block, (((1,), (1,)), ((), ())), preferred_element_type=F32)

    vol_load.wait()
    stage_top(vol1, b["vol_a"], b["vol_b"])
    vol_x = Exchange(
        DIRS, top_message(vol1, b["vol_a"], b["vol_b"], b["vol_r"]), vol_ss, vol_rs, here, sizes
    )
    pl.semaphore_wait(barrier, greeted)
    vol_x.start()
    loads["k_top"].wait()
    for k in range(9):

        def top_block(dz, k=k):
            half = b["k_top"][64 * (3 * k + dz) : 64 * (3 * k + dz) + 64, :].astype(F32)
            return jnp.concatenate([half, half], axis=1)

        band(top_block, b["t_top"], k)
    loads["k_da"].wait()
    for k in range(9):
        pairs(
            lambda dz, k=k: b["k_da"][64 * (3 * k + dz) : 64 * (3 * k + dz) + 64, :],
            4,
            64,
            b["t_da"].at[k],
        )
    vol_x.wait_recv()
    shift_top(vol1, b["vol_r"], b["vol0"], b["vol2"])
    top_out = b["top_out"]
    skip1 = b["skip1"]

    kept = jnp.maximum(conv_top((b["vol0"], vol1, b["vol2"]), b["t_top"]), 0.0)
    for g in range(4):
        block = kept[128 * g : 128 * g + 128]
        for h in range(2):
            top_out[2 * g + h] = block[:, tile(h)]
        skip1[1:9, :, 256 * g + 128 : 256 * g + 384] = block.astype(BF16).reshape(8, 16, 256)

    pm, pm_wide = b["pm"], b["pm_wide"]
    first_lanes = lax.broadcasted_iota(jnp.int32, (8, 128), 1) < 64
    for xp in range(2):
        for q in range(4):
            held = []
            for xm in (2 * xp, 2 * xp + 1):
                found = []
                for j in (2 * q, 2 * q + 1):
                    parts = [
                        top_out[j, pl.ds(16 * x + p, 8, stride=2), :]
                        for x in (2 * xm, 2 * xm + 1)
                        for p in range(2)
                    ]
                    most = jnp.maximum(jnp.maximum(parts[0], parts[1]), jnp.maximum(parts[2], parts[3]))
                    found.append(jnp.maximum(most, pltpu.roll(most, 64, 1)))
                cell = jnp.where(first_lanes, found[0], found[1])
                pm_wide[xm + 2, 2:10, tile(q + 1)] = cell
                held.append(cell)
            pm[xp + 1, q + 1] = jnp.concatenate(held, axis=0).astype(BF16)
    for s, y in ((0, 6), (1, 0)):
        for xm in range(4):
            for q in range(4):
                row = 4 * q + 2 * (xm % 2)
                b["pm_t"][s, xm // 2, row : row + 2, :] = pm_wide[xm + 2, y + 2 : y + 4, tile(q + 1)]
        for xp in range(2):
            b["pm_y"][s, xp] = b["pm_t"][s, xp].astype(BF16)

    def pm_message(step):
        dx, dy, dz = step
        if dy == 0:
            sx = {0: slice(1, 3), 1: slice(2, 3), -1: slice(1, 2)}[dx]
            tx = {0: slice(1, 3), 1: slice(0, 1), -1: slice(3, 4)}[dx]
            sz = {0: slice(1, 5), 1: slice(4, 5), -1: slice(1, 2)}[dz]
            tz = {0: slice(1, 5), 1: slice(0, 1), -1: slice(5, 6)}[dz]
            return pm.at[sx, sz], pm.at[tx, tz]
        s = side(dy)
        xs = {0: slice(0, 2), 1: slice(1, 2), -1: slice(0, 1)}[dx]
        return b["pm_y"].at[s, xs], b["pm_r"].at[s, dx + 1, dz + 1, xs]

    pm_x = Exchange(DIRS, pm_message, pm_ss, pm_rs, here, sizes)
    pm_x.start()

    stage_top(skip1, b["skip_a"], b["skip_b"])
    skip_x = Exchange(
        DIRS, top_message(skip1, b["skip_a"], b["skip_b"], b["skip_r"]), skip_ss, skip_rs, here, sizes
    )
    skip_x.start()
    loads["k_out"].wait()
    for k in range(9):
        turns = []
        for dz in range(3):
            block = b["k_out"][64 * (3 * k + dz) : 64 * (3 * k + dz) + 64, :]
            turns.append(turned(jnp.concatenate([block, block], axis=0)))
        band(lambda dz: turns[dz][0:64], b["t_lift"], k)
        band(lambda dz: turns[dz][64:128], b["t_skip"], k)
    loads["k_um"].wait()
    for half in range(2):
        for k in range(9):

            def up_block(dz, half=half, k=k):
                at = 256 * (3 * k + dz) + 128 * half
                return b["k_um"][at : at + 128, :]

            pairs(up_block, 4, 128, b["t_um"].at[half, k])
    loads["raw_ll"].wait()
    for q in range(0, 256, 64):
        raw = b["raw_ll"][q : q + 64].astype(F32)
        for i in range(4):
            for k in range(2):
                b["k_ll"][q : q + 64, tile(2 * i + k)] = raw[:, i, k, :].astype(BF16)
    t_lt = b["t_lt"]
    loads["k_lt"].wait()
    for i in range(2):
        for h in range(2):
            at = 128 * (2 * i + h)
            t_lt[128 * h : 128 * h + 128, tile(i)] = turned(b["k_lt"][at : at + 128, :]).astype(BF16)

    pm_x.wait_recv()
    for xp in range(4):
        for zp in range(6):
            if 1 <= xp < 3 and 1 <= zp < 5:
                continue
            both = pm[xp, zp].astype(F32)
            pm_wide[2 * xp, 2:10, tile(zp)] = both[0:8]
            pm_wide[2 * xp + 1, 2:10, tile(zp)] = both[8:16]
    for s, y in ((0, 0), (1, 10)):
        for dx in (-1, 0, 1):
            for xp in {0: (0, 1), 1: (1,), -1: (0,)}[dx]:
                base = {0: 2 + 2 * xp, 1: 0, -1: 6}[dx]
                for dz in (-1, 0, 1):
                    slot = b["pm_t"].at[0, (dz + 1) % 2]
                    slot[...] = b["pm_r"][s, dx + 1, dz + 1, xp].astype(F32)
                    for q in {0: (0, 1, 2, 3), 1: (3,), -1: (0,)}[dz]:
                        to = {0: q + 1, 1: 0, -1: 5}[dz]
                        for xi in range(2):
                            row = 4 * q + 2 * xi
                            pm_wide[base + xi, y : y + 2, tile(to)] = slot[row : row + 2, :]
    pm_s = b["pm_s"]
    for x in range(8):
        for dy in range(3):
            pm_s[dy, x] = pm_wide[x, dy : dy + 16, :].astype(BF16)

    def flag(ok):
        return jnp.where(ok, 1.0, 0.0).astype(F32)

    def valid(at, local, size, first, index):
        place = at * local + first + index
        return flag(jnp.logical_and(place >= 0, place < local * size))

    def row_mask(rows, lanes, used, at, local, size, first):
        place = lax.broadcasted_iota(jnp.int32, (rows, lanes), 0)
        whole = place + (at * local + first)
        ok = jnp.logical_and(whole >= 0, whole < local * size)
        return jnp.logical_and(ok, place < used)

    fm_wide = b["fm_wide"]
    mid_rows = row_mask(16, 128, 10, gy, 8, sizes[1], -1)
    first_mid = None
    for dx in range(3):
        for dy in range(3):
            piece = jnp.concatenate(
                [pm_s[dy, dx : dx + 6, :, 128 * j : 128 * j + 256].reshape(96, 256) for j in range(5)],
                axis=0,
            )
            term = dot(piece, b["t_da"][3 * dx + dy])
            first_mid = term if first_mid is None else first_mid + term
    first_mid = jnp.maximum(first_mid, 0.0)
    for x in range(6):
        for z in range(10):
            keep = valid(gx, 4, sizes[0], -1, x) * valid(gz, 8, sizes[2], -1, z)
            at = 96 * (z // 2) + 16 * x
            cell = first_mid[at : at + 16, tile(z % 2)]
            fm_wide[x, z, 0:16, :] = jnp.where(mid_rows, cell, 0.0) * keep

    def gather(wide_ref, target, xs, pairs, lanes):
        for x in range(xs):
            for zp in range(pairs):
                for dy in range(3):
                    for dz in range(3):
                        both = jnp.concatenate(
                            [wide_ref[x, 2 * zp + h + dz, dy : dy + 8, :] for h in range(2)], axis=0
                        )
                        at = (3 * dy + dz) * lanes
                        target[x, 16 * zp : 16 * zp + 16, at : at + lanes] = both.astype(BF16)

    def conv_rows(source, xs, kernels):
        rows, depth = source.shape[1], source.shape[2]
        total = None
        for dx in range(3):
            piece = source[dx : dx + xs].reshape(xs * rows, depth)
            term = dot(piece, kernels[dx * depth : (dx + 1) * depth, :])
            total = term if total is None else total + term
        return jnp.maximum(total, 0.0)

    gather(fm_wide, b["fm_s"], 6, 4, 128)
    loads["k_db"].wait()
    sm_out, sm = b["sm_out"], b["sm"]
    skip_mid = conv_rows(b["fm_s"], 4, b["k_db"])
    sm_out[...] = skip_mid.reshape(4, 8, 8, 128)
    sm[2:6, 1:5] = skip_mid.astype(BF16).reshape(4, 4, 16, 128)

    sm_t = b["sm_t"]
    for s, y in ((0, 6), (1, 0)):
        for x in range(4):
            for z in range(8):
                sm_t[x, 2 * z : 2 * z + 2, :] = sm_out[x, z, y : y + 2, :]
            b["sm_y"][s, x] = sm_t[x].astype(BF16)

    def sm_message(step):
        dx, dy, dz = step
        if dy == 0:
            sx = {0: slice(2, 6), 1: slice(4, 6), -1: slice(2, 4)}[dx]
            tx = {0: slice(2, 6), 1: slice(0, 2), -1: slice(6, 8)}[dx]
            sz = {0: slice(1, 5), 1: slice(4, 5), -1: slice(1, 2)}[dz]
            tz = {0: slice(1, 5), 1: slice(0, 1), -1: slice(5, 6)}[dz]
            return sm.at[sx, sz], sm.at[tx, tz]
        s = side(dy)
        xs = {0: slice(0, 4), 1: slice(2, 4), -1: slice(0, 2)}[dx]
        return b["sm_y"].at[s, xs], b["sm_r"].at[s, dx + 1, dz + 1, xs]

    sm_x = Exchange(DIRS, sm_message, sm_ss, sm_rs, here, sizes)
    sm_x.start()

    pl_t, pl_f, pl_r = b["pl_t"], b["pl_f"], b["pl_r"]
    for x in range(2):
        for z in range(4):
            parts = [sm_out[2 * x + i, 2 * z + k] for i in range(2) for k in range(2)]
            pl_t[x, z] = jnp.maximum(jnp.maximum(parts[0], parts[1]), jnp.maximum(parts[2], parts[3]))
            pl_f[x, 4 * z : 4 * z + 4, :] = jnp.maximum(
                pl_t[x, z, pl.ds(0, 4, stride=2), :], pl_t[x, z, pl.ds(1, 4, stride=2), :]
            )
        pl_r[2, 1, 1, x] = pl_f[x].astype(BF16)

    def pl_message(step):
        dx, dy, dz = step
        planes = {2: slice(1, 2), -2: slice(0, 1)}.get(dx, slice(0, 2))
        return pl_r.at[2, 1, 1, planes], pl_r.at[2 - dx, 1 - dz, 1 - dy, planes]

    pl_x = Exchange(LOW_DIRS, pl_message, pl_ss, pl_rs, here, sizes)
    pl_x.start()

    skip_x.wait_recv()
    shift_top(skip1, b["skip_r"], b["skip0"], b["skip2"])

    b["part"][...] = conv_top((b["skip0"], skip1, b["skip2"]), b["t_skip"])

    jm_wide, jm_s = b["jm_wide"], b["jm_s"]
    sm_x.wait_recv()
    for x in range(8):
        for zp in range(6):
            both = sm[x, zp].astype(F32)
            for h in range(2):
                jm_wide[1, x, 2 * zp + h, 2:10, :] = both[8 * h : 8 * h + 8]
    for s, y in ((0, 0), (1, 10)):
        for dx in (-1, 0, 1):
            for xi in {0: (0, 1, 2, 3), 1: (2, 3), -1: (0, 1)}[dx]:
                x = {0: 2 + xi, 1: xi - 2, -1: 6 + xi}[dx]
                for dz in (-1, 0, 1):
                    slot = sm_t.at[dz + 1]
                    slot[...] = b["sm_r"][s, dx + 1, dz + 1, xi].astype(F32)
                    for z in {0: range(8), 1: (6, 7), -1: (0, 1)}[dz]:
                        to = {0: z + 2, 1: z - 6, -1: 10 + z}[dz]
                        jm_wide[1, x, to, y : y + 2, :] = slot[2 * z : 2 * z + 2, :]

    def shift_mid(half):
        for x in range(8):
            for z in range(12):
                for dy in range(3):
                    jm_s[half, dy, x, :, tile(z)] = jm_wide[half, x, z, dy : dy + 16, :].astype(BF16)

    def conv_mid(half):
        total = None
        for dx in range(3):
            for dy in range(3):
                piece = jnp.concatenate(
                    [
                        jm_s[half, dy, dx : dx + 6, :, 256 * j : 256 * j + 512].reshape(96, 512)
                        for j in range(5)
                    ],
                    axis=0,
                )
                term = dot(piece, b["t_um"][half, 3 * dx + dy])
                total = term if total is None else total + term
        return total

    shift_mid(1)
    b["jm_part"][...] = conv_mid(1)

    pl_x.wait_recv()
    pl_wide, pl_g = b["pl_wide"], b["pl_g"]
    planes = [(0, 1), (1, 0), (1, 1), (2, 0), (2, 1), (3, 0), (3, 1), (4, 0)]
    for x, (d, p) in enumerate(planes):
        for zs in range(3):
            for ys in range(3):
                pl_g[ys] = pl_r[d, zs, ys, p].astype(F32)
            for z, to in {0: ((1, 0), (2, 1), (3, 2)), 1: ((0, 3), (1, 4), (2, 5), (3, 6)), 2: ((0, 7), (1, 8), (2, 9))}[zs]:
                pl_wide[x, to, 0:3, :] = pl_g[0, 4 * z + 1 : 4 * z + 4, :]
                pl_wide[x, to, 3:7, :] = pl_g[1, 4 * z : 4 * z + 4, :]
                pl_wide[x, to, 7:10, :] = pl_g[2, 4 * z : 4 * z + 3, :]
    gather(pl_wide, b["pl_s"], 8, 4, 128)
    loads["k_la"].wait()
    first_low = conv_rows(b["pl_s"], 6, b["k_la"])
    fl_wide = b["fl_wide"]
    low_rows = row_mask(8, 256, 8, gy, 4, sizes[1], -2)
    for x in range(6):
        for z in range(8):
            keep = valid(gx, 2, sizes[0], -2, x) * valid(gz, 4, sizes[2], -2, z)
            at = 64 * x + 8 * z
            fl_wide[x, z, 0:8, :] = jnp.where(low_rows, first_low[at : at + 8, :], 0.0) * keep
            fl_wide[x, z, 8:16, :] = jnp.zeros((8, 256), F32)
    gather(fl_wide, b["fl_s"], 6, 3, 256)
    loads["k_lb"].wait()
    coarse = conv_rows(b["fl_s"], 4, b["k_lb"])
    coarse_rows = row_mask(8, 256, 6, gy, 4, sizes[1], -1)
    cells = []
    for x in range(4):
        for z in range(6):
            keep = valid(gx, 2, sizes[0], -1, x) * valid(gz, 4, sizes[2], -1, z)
            at = 48 * x + 8 * z
            cells.append(jnp.where(coarse_rows, coarse[at : at + 8, :], 0.0) * keep)
    coarse = jnp.concatenate(cells, axis=0).astype(BF16)

    lifted = dot(coarse, b["k_ll"][...])
    for x in range(4):
        for z in range(6):
            for i in range(2):
                for h in range(2):
                    for k in range(2):
                        at = 48 * x + 8 * z
                        jm_wide[0, 2 * x + i, 2 * z + k, pl.ds(h, 8, stride=2), :] = lifted[
                            at : at + 8, tile(4 * i + 2 * h + k)
                        ]

    mg_wide = b["mg_wide"]
    shift_mid(0)
    merged = jnp.maximum(conv_mid(0) + b["jm_part"][...], 0.0)
    for x in range(6):
        for z in range(10):
            keep = valid(gx, 4, sizes[0], -1, x) * valid(gz, 8, sizes[2], -1, z)
            at = 96 * (z // 2) + 16 * x
            cell = jnp.where(mid_rows, merged[at : at + 16, tile(z % 2)], 0.0) * keep
            for h in range(2):
                mg_wide[h, x, z, pl.ds(h, 16, stride=2), :] = cell

    lift = (b["lift0"], b["lift1"], b["lift2"])
    for x in range(6):
        for dy in range(3):
            halves = [mg_wide[h, x, :, dy + 1 : dy + 17, :].astype(BF16).reshape(160, 128) for h in range(2)]
            piece = jnp.concatenate(halves, axis=1)
            value = dot(piece, t_lt[...]).astype(BF16)
            for i in range(2):
                to = 2 * x + i - 1
                if 0 <= to < 10:
                    for z in range(10):
                        lift[dy][to, :, tile(z)] = value[16 * z : 16 * z + 16, tile(i)]

    total = conv_top(lift, b["t_lift"]) + b["part"][...]
    for g in range(4):
        out[:, :, 256 * g : 256 * g + 256] = total[128 * g : 128 * g + 128].astype(BF16).reshape(8, 16, 256)
    for exchange in (vol_x, pm_x, skip_x, pl_x, sm_x):
        exchange.wait_send()


def body(sizes, volume, *weights):
    w_top, w_da, w_db, w_la, w_lb, w_ll, w_um, w_lt, w_out = weights
    flat = [
        w_top.reshape(1728, 64),
        w_da.reshape(1728, 128),
        w_db.reshape(3456, 128),
        w_la.reshape(3456, 256),
        w_lb.reshape(6912, 256),
        w_ll.reshape(256, 4, 2, 128),
        w_um.reshape(6912, 128),
        w_lt.transpose(1, 2, 3, 4, 0).reshape(512, 128),
        w_out.swapaxes(3, 4).reshape(1728, 128),
    ]
    any_space = pl.BlockSpec(memory_space=pl.ANY)
    few, many = len(DIRS), len(LOW_DIRS)
    counts = (10, few, few, few, few, few, few, few, few, many, many)
    return pl.pallas_call(
        functools.partial(kernel, sizes),
        out_shape=jax.ShapeDtypeStruct(volume.shape, BF16),
        in_specs=[any_space] * 10,
        out_specs=pl.BlockSpec(memory_space=pltpu.VMEM),
        scratch_shapes=[pltpu.VMEM(s, d) for s, d in SCRATCH.values()]
        + [pltpu.SemaphoreType.DMA((c,)) for c in counts],
        compiler_params=pltpu.CompilerParams(
            collective_id=0, has_side_effects=True, vmem_limit_bytes=56 * 1024 * 1024
        ),
    )(volume, *flat)


def solution(mesh):
    placed = (P("gx", "gy", "gz"),) + (P(),) * 9
    sizes = tuple(mesh.shape[name] for name in ("gx", "gy", "gz"))
    return jax.shard_map(
        functools.partial(body, sizes),
        mesh=mesh,
        in_specs=placed,
        out_specs=P("gx", "gy", "gz"),
        check_vma=False,
    )
```

```python
import functools

import jax
import jax.numpy as jnp
from jax import lax
from jax.experimental import pallas as pl
from jax.experimental.pallas import tpu as pltpu
from jax.sharding import PartitionSpec as P

F32 = jnp.float32
BF16 = jnp.bfloat16
MESH = pl.DeviceIdType.MESH


def directions(far):
    steps = [
        (dx, dy, dz)
        for dx in range(-far, far + 1)
        for dy in (-1, 0, 1)
        for dz in (-1, 0, 1)
        if (dx, dy, dz) != (0, 0, 0)
    ]
    return sorted(steps, key=lambda step: -sum(abs(s) for s in step))


DIRS = directions(1)
LOW_DIRS = directions(2)


def dot(a, b):
    return jnp.dot(a, b, preferred_element_type=F32)


def side(step):
    return 0 if step == 1 else 1


SCRATCH = dict(
    k_top=((1728, 64), BF16),
    k_da=((1728, 128), BF16),
    k_db=((3456, 128), BF16),
    k_la=((3456, 256), BF16),
    k_lb=((6912, 256), BF16),
    k_ll=((256, 1024), BF16),
    k_um=((6912, 128), BF16),
    k_lt=((512, 128), BF16),
    k_out=((1728, 128), BF16),
    raw_ll=((256, 4, 2, 128), BF16),
    t_top=((9, 512, 256), BF16),
    t_skip=((9, 512, 256), BF16),
    t_lift=((9, 512, 256), BF16),
    t_da=((9, 256, 256), BF16),
    t_lt=((256, 256), BF16),
    t_um=((2, 9, 512, 256), BF16),
    wide=((10, 320, 128), F32),
    vol0=((10, 16, 1280), BF16),
    vol1=((10, 16, 1280), BF16),
    vol2=((10, 16, 1280), BF16),
    skip0=((10, 16, 1280), BF16),
    skip1=((10, 16, 1280), BF16),
    skip2=((10, 16, 1280), BF16),
    lift0=((10, 16, 1280), BF16),
    lift1=((10, 16, 1280), BF16),
    lift2=((10, 16, 1280), BF16),
    vol_a=((2, 4, 16, 128), BF16),
    vol_b=((2, 2, 16, 128), BF16),
    vol_r=((2, 12, 16, 128), BF16),
    skip_a=((2, 4, 16, 128), BF16),
    skip_b=((2, 2, 16, 128), BF16),
    skip_r=((2, 12, 16, 128), BF16),
    tmp=((4, 16, 128), F32),
    top_out=((8, 128, 128), F32),
    part=((512, 256), F32),
    pm=((4, 6, 16, 128), BF16),
    pm_y=((2, 2, 16, 128), BF16),
    pm_r=((2, 3, 3, 2, 16, 128), BF16),
    pm_t=((2, 2, 16, 128), F32),
    pm_wide=((8, 24, 768), F32),
    pm_s=((3, 8, 16, 768), BF16),
    fm_wide=((6, 10, 24, 128), F32),
    fm_s=((6, 64, 1152), BF16),
    sm_out=((4, 8, 8, 128), F32),
    sm=((8, 6, 16, 128), BF16),
    sm_y=((2, 4, 16, 128), BF16),
    sm_r=((2, 3, 3, 4, 16, 128), BF16),
    sm_t=((4, 16, 128), F32),
    pl_t=((2, 4, 8, 128), F32),
    pl_f=((2, 16, 128), F32),
    pl_r=((5, 3, 3, 2, 16, 128), BF16),
    pl_g=((3, 16, 128), F32),
    pl_wide=((8, 10, 16, 128), F32),
    pl_s=((8, 64, 1152), BF16),
    fl_wide=((6, 8, 16, 256), F32),
    fl_s=((6, 48, 2304), BF16),
    jm_wide=((2, 8, 12, 24, 128), F32),
    jm_s=((2, 3, 8, 16, 1536), BF16),
    jm_part=((480, 256), F32),
    mg_wide=((2, 6, 10, 32, 128), F32),
)
NAMES = list(SCRATCH)
WEIGHTS = ("k_top", "k_da", "k_db", "k_la", "k_lb", "raw_ll", "k_um", "k_lt", "k_out")
ORDER = ("k_top", "k_da", "raw_ll", "k_out", "k_um", "k_db", "k_lt", "k_la", "k_lb")


class Exchange:
    def __init__(self, dirs, message, send, recv, here, sizes):
        self.dirs, self.message = dirs, message
        self.send, self.recv = send, recv
        self.here, self.sizes = here, sizes

    def inside(self, step, sign):
        ok = None
        for at, size, s in zip(self.here, self.sizes, step):
            s = s * sign
            if s == 0:
                continue
            this = at + s < size if s > 0 else at + s >= 0
            ok = this if ok is None else jnp.logical_and(ok, this)
        return ok

    def copy(self, i):
        step = self.dirs[i]
        src, dst = self.message(step)
        there = tuple(at + s for at, s in zip(self.here, step))
        return pltpu.make_async_remote_copy(
            src_ref=src,
            dst_ref=dst,
            send_sem=self.send.at[i],
            recv_sem=self.recv.at[i],
            device_id=there,
            device_id_type=MESH,
        )

    def start(self):
        for i, step in enumerate(self.dirs):
            pl.when(self.inside(step, 1))(lambda i=i: self.copy(i).start())

    def wait_recv(self):
        for i, step in enumerate(self.dirs):
            pl.when(self.inside(step, -1))(lambda i=i: self.copy(i).wait_recv())

    def wait_send(self):
        for i, step in enumerate(self.dirs):
            pl.when(self.inside(step, 1))(lambda i=i: self.copy(i).wait_send())


def kernel(sizes, *refs):
    vol, weights, out = refs[0], refs[1:10], refs[10]
    n = len(NAMES)
    b = dict(zip(NAMES, refs[11 : 11 + n]))
    (load_sem, vol_ss, vol_rs, skip_ss, skip_rs, pm_ss, pm_rs, sm_ss, sm_rs, pl_ss, pl_rs) = refs[11 + n :]
    here = tuple(lax.axis_index(name) for name in ("gx", "gy", "gz"))
    gx, gy, gz = here
    tile = lambda t: slice(128 * t, 128 * t + 128)

    vol1 = b["vol1"]
    vol_load = pltpu.make_async_copy(vol, vol1.at[1:9, :, 128:1152], load_sem.at[9])
    vol_load.start()

    def zero(ref, *at):
        if at:
            ref[at] = jnp.zeros(ref.at[at].shape, ref.dtype)
        else:
            ref[...] = jnp.zeros(ref.shape, ref.dtype)

    everything = slice(None)
    for name in ("vol1", "skip1"):
        zero(b[name], slice(0, 1))
        zero(b[name], slice(9, 10))
        zero(b[name], slice(1, 9), everything, tile(0))
        zero(b[name], slice(1, 9), everything, tile(9))
    for name in ("vol_r", "skip_r", "pm_r", "sm_r", "pl_r"):
        zero(b[name])
    mg_wide = b["mg_wide"]
    zero(mg_wide)
    for name, width, lo, hi in (("pm", 4, 1, 3), ("sm", 8, 2, 6)):
        zero(b[name], slice(0, lo))
        zero(b[name], slice(hi, width))
        zero(b[name], slice(lo, hi), slice(0, 1))
        zero(b[name], slice(lo, hi), slice(5, 6))

    barrier = pltpu.get_barrier_semaphore()
    low_x = Exchange(LOW_DIRS, None, None, None, here, sizes)
    for step in LOW_DIRS:

        @pl.when(low_x.inside(step, 1))
        def _(step=step):
            pl.semaphore_signal(
                barrier,
                inc=1,
                device_id=tuple(at + s for at, s in zip(here, step)),
                device_id_type=MESH,
            )

    loads = {}
    for name in ORDER:
        i = WEIGHTS.index(name)
        loads[name] = pltpu.make_async_copy(weights[i], b[name], load_sem.at[i])
        loads[name].start()

    def reach(at, size, far):
        count = jnp.int32(1)
        for s in range(1, far + 1):
            count = count + jnp.where(at >= s, 1, 0) + jnp.where(at + s < size, 1, 0)
        return count

    greeted = reach(gx, sizes[0], 2) * reach(gy, sizes[1], 1) * reach(gz, sizes[2], 1) - 1

    wide = b["wide"]
    tmp = b["tmp"]

    def stage_top(cells, a, bb):
        for x in range(1, 9):
            for t in range(1, 9):
                wide[t, 32 * x + 8 : 32 * x + 24, :] = cells[x, :, tile(t)].astype(F32)
        for s, y in ((0, 15), (1, 0)):
            for tp in range(4):
                pair = [
                    wide[2 * tp + h + 1, pl.ds(32 + 8 + y, 8, stride=32), :] for h in range(2)
                ]
                a[s, tp] = jnp.concatenate(pair, axis=0).astype(BF16)
            for xs, x in ((0, 8), (1, 1)):
                for t in range(8):
                    tmp[2 * s + xs, t : t + 1, :] = wide[t + 1, 32 * x + 8 + y : 32 * x + 9 + y, :]
                for t in range(8, 16):
                    tmp[2 * s + xs, t : t + 1, :] = jnp.zeros((1, 128), F32)
                bb[s, xs] = tmp[2 * s + xs].astype(BF16)

    def top_message(cells, a, bb, r):
        def message(step):
            dx, dy, dz = step
            if dy == 0:
                sx = {0: slice(1, 9), 1: slice(8, 9), -1: slice(1, 2)}[dx]
                tx = {0: slice(1, 9), 1: slice(0, 1), -1: slice(9, 10)}[dx]
                sz = {0: slice(128, 1152), 1: tile(8), -1: tile(1)}[dz]
                tz = {0: slice(128, 1152), 1: tile(0), -1: tile(9)}[dz]
                return cells.at[sx, :, sz], cells.at[tx, :, tz]
            s = side(dy)
            if dx == 0 and dz == 0:
                return a.at[s], r.at[s, 0:4]
            if dz == 0:
                return bb.at[s, side(dx)], r.at[s, 6 + side(dx)]
            tp = 3 if dz == 1 else 0
            slot = 4 + side(dz) if dx == 0 else 8 + 2 * side(dx) + side(dz)
            return a.at[s, tp], r.at[s, slot]

        return message

    def shift_top(cells, r, below, above):
        for x in range(10):
            for t in range(10) if x in (0, 9) else (0, 9):
                wide[t, 32 * x + 8 : 32 * x + 24, :] = cells[x, :, tile(t)].astype(F32)
        for s, row in ((0, 7), (1, 24)):
            rows = pl.ds(32 + row, 8, stride=32)
            for tp in range(4):
                both = r[s, tp].astype(F32)
                wide[2 * tp + 1, rows, :] = both[0:8]
                wide[2 * tp + 2, rows, :] = both[8:16]
            for zs, t, half in ((0, 0, 8), (1, 9, 0)):
                wide[t, rows, :] = r[s, 4 + zs].astype(F32)[half : half + 8]
            for xs, x, keep in ((0, 0, 7), (1, 9, 0)):
                at = slice(32 * x + row, 32 * x + row + 1)
                tmp[xs] = r[s, 6 + xs].astype(F32)
                for t in range(8):
                    wide[t + 1, at, :] = tmp[xs, t : t + 1, :]
                for zs, t, half in ((0, 0, 8), (1, 9, 0)):
                    tmp[2 + zs] = r[s, 8 + 2 * xs + zs].astype(F32)
                    wide[t, at, :] = tmp[2 + zs, half + keep : half + keep + 1, :]
        for x in range(10):
            for t in range(10):
                below[x, :, tile(t)] = wide[t, 32 * x + 7 : 32 * x + 23, :].astype(BF16)
                above[x, :, tile(t)] = wide[t, 32 * x + 9 : 32 * x + 25, :].astype(BF16)

    def conv_top(shifted, kernels):
        total = None
        for dx in range(3):
            for dy in range(3):
                piece = jnp.concatenate(
                    [
                        shifted[dy][dx : dx + 8, :, 256 * g : 256 * g + 512].reshape(128, 512)
                        for g in range(4)
                    ],
                    axis=0,
                )
                term = dot(piece, kernels[3 * dx + dy])
                total = term if total is None else total + term
        return total

    low_half = lax.broadcasted_iota(jnp.int32, (64, 128), 1) < 64

    def band(block, target, k):
        nothing = jnp.zeros((64, 128), F32)
        blocks = [block(dz) for dz in range(3)]
        pick = lambda dz: blocks[dz] if 0 <= dz < 3 else nothing
        for zi in range(8):
            for h in range(2):
                both = jnp.where(low_half, pick(zi - 1 - 2 * h), pick(zi - 2 - 2 * h))
                target[k, 64 * zi : 64 * zi + 64, tile(h)] = both.astype(BF16)

    def pairs(block, count, depth, target):
        for zi in range(count):
            for zo in range(count - 2):
                value = block(zi - zo) if 0 <= zi - zo < 3 else jnp.zeros((depth, 128), BF16)
                target[depth * zi : depth * zi + depth, tile(zo)] = value

    eye = jnp.where(
        lax.broadcasted_iota(jnp.int32, (128, 128), 0) == lax.broadcasted_iota(jnp.int32, (128, 128), 1),
        1.0,
        0.0,
    ).astype(BF16)

    def turned(block):
        return lax.dot_general(eye, block, (((1,), (1,)), ((), ())), preferred_element_type=F32)

    vol_load.wait()
    stage_top(vol1, b["vol_a"], b["vol_b"])
    vol_x = Exchange(
        DIRS, top_message(vol1, b["vol_a"], b["vol_b"], b["vol_r"]), vol_ss, vol_rs, here, sizes
    )
    pl.semaphore_wait(barrier, greeted)
    vol_x.start()
    loads["k_top"].wait()
    for k in range(9):

        def top_block(dz, k=k):
            half = b["k_top"][64 * (3 * k + dz) : 64 * (3 * k + dz) + 64, :].astype(F32)
            return jnp.concatenate([half, half], axis=1)

        band(top_block, b["t_top"], k)
    loads["k_da"].wait()
    for k in range(9):
        pairs(
            lambda dz, k=k: b["k_da"][64 * (3 * k + dz) : 64 * (3 * k + dz) + 64, :],
            4,
            64,
            b["t_da"].at[k],
        )
    loads["raw_ll"].wait()
    for q in range(0, 256, 64):
        raw = b["raw_ll"][q : q + 64].astype(F32)
        for i in range(4):
            for k in range(2):
                b["k_ll"][q : q + 64, tile(2 * i + k)] = raw[:, i, k, :].astype(BF16)
    loads["k_out"].wait()
    for k in range(9):
        turns = []
        for dz in range(3):
            block = b["k_out"][64 * (3 * k + dz) : 64 * (3 * k + dz) + 64, :]
            turns.append(turned(jnp.concatenate([block, block], axis=0)))
        band(lambda dz: turns[dz][0:64], b["t_lift"], k)
        band(lambda dz: turns[dz][64:128], b["t_skip"], k)
    vol_x.wait_recv()
    shift_top(vol1, b["vol_r"], b["vol0"], b["vol2"])
    top_out = b["top_out"]
    skip1 = b["skip1"]

    kept = jnp.maximum(conv_top((b["vol0"], vol1, b["vol2"]), b["t_top"]), 0.0)
    for g in range(4):
        block = kept[128 * g : 128 * g + 128]
        for h in range(2):
            top_out[2 * g + h] = block[:, tile(h)]
        skip1[1:9, :, 256 * g + 128 : 256 * g + 384] = block.astype(BF16).reshape(8, 16, 256)

    pm, pm_wide = b["pm"], b["pm_wide"]
    first_lanes = lax.broadcasted_iota(jnp.int32, (8, 128), 1) < 64
    for xp in range(2):
        for q in range(4):
            held = []
            for xm in (2 * xp, 2 * xp + 1):
                found = []
                for j in (2 * q, 2 * q + 1):
                    parts = [
                        top_out[j, pl.ds(16 * x + p, 8, stride=2), :]
                        for x in (2 * xm, 2 * xm + 1)
                        for p in range(2)
                    ]
                    most = jnp.maximum(jnp.maximum(parts[0], parts[1]), jnp.maximum(parts[2], parts[3]))
                    found.append(jnp.maximum(most, pltpu.roll(most, 64, 1)))
                cell = jnp.where(first_lanes, found[0], found[1])
                pm_wide[xm + 2, 2:10, tile(q + 1)] = cell
                held.append(cell)
            pm[xp + 1, q + 1] = jnp.concatenate(held, axis=0).astype(BF16)
    for s, y in ((0, 6), (1, 0)):
        for xm in range(4):
            for q in range(4):
                row = 4 * q + 2 * (xm % 2)
                b["pm_t"][s, xm // 2, row : row + 2, :] = pm_wide[xm + 2, y + 2 : y + 4, tile(q + 1)]
        for xp in range(2):
            b["pm_y"][s, xp] = b["pm_t"][s, xp].astype(BF16)

    def pm_message(step):
        dx, dy, dz = step
        if dy == 0:
            sx = {0: slice(1, 3), 1: slice(2, 3), -1: slice(1, 2)}[dx]
            tx = {0: slice(1, 3), 1: slice(0, 1), -1: slice(3, 4)}[dx]
            sz = {0: slice(1, 5), 1: slice(4, 5), -1: slice(1, 2)}[dz]
            tz = {0: slice(1, 5), 1: slice(0, 1), -1: slice(5, 6)}[dz]
            return pm.at[sx, sz], pm.at[tx, tz]
        s = side(dy)
        xs = {0: slice(0, 2), 1: slice(1, 2), -1: slice(0, 1)}[dx]
        return b["pm_y"].at[s, xs], b["pm_r"].at[s, dx + 1, dz + 1, xs]

    pm_x = Exchange(DIRS, pm_message, pm_ss, pm_rs, here, sizes)
    pm_x.start()

    stage_top(skip1, b["skip_a"], b["skip_b"])
    skip_x = Exchange(
        DIRS, top_message(skip1, b["skip_a"], b["skip_b"], b["skip_r"]), skip_ss, skip_rs, here, sizes
    )
    skip_x.start()
    loads["k_um"].wait()
    for half in range(2):
        for k in range(9):

            def up_block(dz, half=half, k=k):
                at = 256 * (3 * k + dz) + 128 * half
                return b["k_um"][at : at + 128, :]

            pairs(up_block, 4, 128, b["t_um"].at[half, k])
    pm_x.wait_recv()
    for xp in range(4):
        for zp in range(6):
            if 1 <= xp < 3 and 1 <= zp < 5:
                continue
            both = pm[xp, zp].astype(F32)
            pm_wide[2 * xp, 2:10, tile(zp)] = both[0:8]
            pm_wide[2 * xp + 1, 2:10, tile(zp)] = both[8:16]
    for s, y in ((0, 0), (1, 10)):
        for dx in (-1, 0, 1):
            for xp in {0: (0, 1), 1: (1,), -1: (0,)}[dx]:
                base = {0: 2 + 2 * xp, 1: 0, -1: 6}[dx]
                for dz in (-1, 0, 1):
                    slot = b["pm_t"].at[0, (dz + 1) % 2]
                    slot[...] = b["pm_r"][s, dx + 1, dz + 1, xp].astype(F32)
                    for q in {0: (0, 1, 2, 3), 1: (3,), -1: (0,)}[dz]:
                        to = {0: q + 1, 1: 0, -1: 5}[dz]
                        for xi in range(2):
                            row = 4 * q + 2 * xi
                            pm_wide[base + xi, y : y + 2, tile(to)] = slot[row : row + 2, :]
    pm_s = b["pm_s"]
    for x in range(8):
        for dy in range(3):
            pm_s[dy, x] = pm_wide[x, dy : dy + 16, :].astype(BF16)

    def flag(ok):
        return jnp.where(ok, 1.0, 0.0).astype(F32)

    def valid(at, local, size, first, index):
        place = at * local + first + index
        return flag(jnp.logical_and(place >= 0, place < local * size))

    def row_mask(rows, lanes, used, at, local, size, first):
        place = lax.broadcasted_iota(jnp.int32, (rows, lanes), 0)
        whole = place + (at * local + first)
        ok = jnp.logical_and(whole >= 0, whole < local * size)
        return jnp.logical_and(ok, place < used)

    fm_wide = b["fm_wide"]
    mid_rows = row_mask(16, 128, 10, gy, 8, sizes[1], -1)
    first_mid = None
    for dx in range(3):
        for dy in range(3):
            piece = jnp.concatenate(
                [pm_s[dy, dx : dx + 6, :, 128 * j : 128 * j + 256].reshape(96, 256) for j in range(5)],
                axis=0,
            )
            term = dot(piece, b["t_da"][3 * dx + dy])
            first_mid = term if first_mid is None else first_mid + term
    first_mid = jnp.maximum(first_mid, 0.0)
    for x in range(6):
        for z in range(10):
            keep = valid(gx, 4, sizes[0], -1, x) * valid(gz, 8, sizes[2], -1, z)
            at = 96 * (z // 2) + 16 * x
            cell = first_mid[at : at + 16, tile(z % 2)]
            fm_wide[x, z, 0:16, :] = jnp.where(mid_rows, cell, 0.0) * keep

    def gather(wide_ref, target, xs, pairs, lanes):
        for x in range(xs):
            for zp in range(pairs):
                for dy in range(3):
                    for dz in range(3):
                        both = jnp.concatenate(
                            [wide_ref[x, 2 * zp + h + dz, dy : dy + 8, :] for h in range(2)], axis=0
                        )
                        at = (3 * dy + dz) * lanes
                        target[x, 16 * zp : 16 * zp + 16, at : at + lanes] = both.astype(BF16)

    def conv_rows(source, xs, kernels):
        rows, depth = source.shape[1], source.shape[2]
        total = None
        for dx in range(3):
            piece = source[dx : dx + xs].reshape(xs * rows, depth)
            term = dot(piece, kernels[dx * depth : (dx + 1) * depth, :])
            total = term if total is None else total + term
        return jnp.maximum(total, 0.0)

    gather(fm_wide, b["fm_s"], 6, 4, 128)
    loads["k_db"].wait()
    sm_out, sm = b["sm_out"], b["sm"]
    skip_mid = conv_rows(b["fm_s"], 4, b["k_db"])
    sm_out[...] = skip_mid.reshape(4, 8, 8, 128)
    sm[2:6, 1:5] = skip_mid.astype(BF16).reshape(4, 4, 16, 128)

    sm_t = b["sm_t"]
    for s, y in ((0, 6), (1, 0)):
        for x in range(4):
            for z in range(8):
                sm_t[x, 2 * z : 2 * z + 2, :] = sm_out[x, z, y : y + 2, :]
            b["sm_y"][s, x] = sm_t[x].astype(BF16)

    def sm_message(step):
        dx, dy, dz = step
        if dy == 0:
            sx = {0: slice(2, 6), 1: slice(4, 6), -1: slice(2, 4)}[dx]
            tx = {0: slice(2, 6), 1: slice(0, 2), -1: slice(6, 8)}[dx]
            sz = {0: slice(1, 5), 1: slice(4, 5), -1: slice(1, 2)}[dz]
            tz = {0: slice(1, 5), 1: slice(0, 1), -1: slice(5, 6)}[dz]
            return sm.at[sx, sz], sm.at[tx, tz]
        s = side(dy)
        xs = {0: slice(0, 4), 1: slice(2, 4), -1: slice(0, 2)}[dx]
        return b["sm_y"].at[s, xs], b["sm_r"].at[s, dx + 1, dz + 1, xs]

    sm_x = Exchange(DIRS, sm_message, sm_ss, sm_rs, here, sizes)
    sm_x.start()

    pl_t, pl_f, pl_r = b["pl_t"], b["pl_f"], b["pl_r"]
    for x in range(2):
        for z in range(4):
            parts = [sm_out[2 * x + i, 2 * z + k] for i in range(2) for k in range(2)]
            pl_t[x, z] = jnp.maximum(jnp.maximum(parts[0], parts[1]), jnp.maximum(parts[2], parts[3]))
            pl_f[x, 4 * z : 4 * z + 4, :] = jnp.maximum(
                pl_t[x, z, pl.ds(0, 4, stride=2), :], pl_t[x, z, pl.ds(1, 4, stride=2), :]
            )
        pl_r[2, 1, 1, x] = pl_f[x].astype(BF16)

    def pl_message(step):
        dx, dy, dz = step
        planes = {2: slice(1, 2), -2: slice(0, 1)}.get(dx, slice(0, 2))
        return pl_r.at[2, 1, 1, planes], pl_r.at[2 - dx, 1 - dz, 1 - dy, planes]

    pl_x = Exchange(LOW_DIRS, pl_message, pl_ss, pl_rs, here, sizes)
    pl_x.start()

    skip_x.wait_recv()
    shift_top(skip1, b["skip_r"], b["skip0"], b["skip2"])

    b["part"][...] = conv_top((b["skip0"], skip1, b["skip2"]), b["t_skip"])

    t_lt = b["t_lt"]
    loads["k_lt"].wait()
    for i in range(2):
        for h in range(2):
            at = 128 * (2 * i + h)
            t_lt[128 * h : 128 * h + 128, tile(i)] = turned(b["k_lt"][at : at + 128, :]).astype(BF16)

    jm_wide, jm_s = b["jm_wide"], b["jm_s"]
    sm_x.wait_recv()
    for x in range(8):
        for zp in range(6):
            both = sm[x, zp].astype(F32)
            for h in range(2):
                jm_wide[1, x, 2 * zp + h, 2:10, :] = both[8 * h : 8 * h + 8]
    for s, y in ((0, 0), (1, 10)):
        for dx in (-1, 0, 1):
            for xi in {0: (0, 1, 2, 3), 1: (2, 3), -1: (0, 1)}[dx]:
                x = {0: 2 + xi, 1: xi - 2, -1: 6 + xi}[dx]
                for dz in (-1, 0, 1):
                    slot = sm_t.at[dz + 1]
                    slot[...] = b["sm_r"][s, dx + 1, dz + 1, xi].astype(F32)
                    for z in {0: range(8), 1: (6, 7), -1: (0, 1)}[dz]:
                        to = {0: z + 2, 1: z - 6, -1: 10 + z}[dz]
                        jm_wide[1, x, to, y : y + 2, :] = slot[2 * z : 2 * z + 2, :]

    def shift_mid(half):
        for x in range(8):
            for z in range(12):
                for dy in range(3):
                    jm_s[half, dy, x, :, tile(z)] = jm_wide[half, x, z, dy : dy + 16, :].astype(BF16)

    def conv_mid(half):
        total = None
        for dx in range(3):
            for dy in range(3):
                piece = jnp.concatenate(
                    [
                        jm_s[half, dy, dx : dx + 6, :, 256 * j : 256 * j + 512].reshape(96, 512)
                        for j in range(5)
                    ],
                    axis=0,
                )
                term = dot(piece, b["t_um"][half, 3 * dx + dy])
                total = term if total is None else total + term
        return total

    shift_mid(1)
    b["jm_part"][...] = conv_mid(1)

    pl_x.wait_recv()
    pl_wide, pl_g = b["pl_wide"], b["pl_g"]
    planes = [(0, 1), (1, 0), (1, 1), (2, 0), (2, 1), (3, 0), (3, 1), (4, 0)]
    for x, (d, p) in enumerate(planes):
        for zs in range(3):
            for ys in range(3):
                pl_g[ys] = pl_r[d, zs, ys, p].astype(F32)
            for z, to in {0: ((1, 0), (2, 1), (3, 2)), 1: ((0, 3), (1, 4), (2, 5), (3, 6)), 2: ((0, 7), (1, 8), (2, 9))}[zs]:
                pl_wide[x, to, 0:3, :] = pl_g[0, 4 * z + 1 : 4 * z + 4, :]
                pl_wide[x, to, 3:7, :] = pl_g[1, 4 * z : 4 * z + 4, :]
                pl_wide[x, to, 7:10, :] = pl_g[2, 4 * z : 4 * z + 3, :]
    gather(pl_wide, b["pl_s"], 8, 4, 128)
    loads["k_la"].wait()
    first_low = conv_rows(b["pl_s"], 6, b["k_la"])
    fl_wide = b["fl_wide"]
    low_rows = row_mask(8, 256, 8, gy, 4, sizes[1], -2)
    for x in range(6):
        for z in range(8):
            keep = valid(gx, 2, sizes[0], -2, x) * valid(gz, 4, sizes[2], -2, z)
            at = 64 * x + 8 * z
            fl_wide[x, z, 0:8, :] = jnp.where(low_rows, first_low[at : at + 8, :], 0.0) * keep
            fl_wide[x, z, 8:16, :] = jnp.zeros((8, 256), F32)
    gather(fl_wide, b["fl_s"], 6, 3, 256)
    loads["k_lb"].wait()
    coarse = conv_rows(b["fl_s"], 4, b["k_lb"])
    coarse_rows = row_mask(8, 256, 6, gy, 4, sizes[1], -1)
    cells = []
    for x in range(4):
        for z in range(6):
            keep = valid(gx, 2, sizes[0], -1, x) * valid(gz, 4, sizes[2], -1, z)
            at = 48 * x + 8 * z
            cells.append(jnp.where(coarse_rows, coarse[at : at + 8, :], 0.0) * keep)
    coarse = jnp.concatenate(cells, axis=0).astype(BF16)

    lifted = dot(coarse, b["k_ll"][...])
    for x in range(4):
        for z in range(6):
            for i in range(2):
                for h in range(2):
                    for k in range(2):
                        at = 48 * x + 8 * z
                        jm_wide[0, 2 * x + i, 2 * z + k, pl.ds(h, 8, stride=2), :] = lifted[
                            at : at + 8, tile(4 * i + 2 * h + k)
                        ]

    mg_wide = b["mg_wide"]
    shift_mid(0)
    merged = jnp.maximum(conv_mid(0) + b["jm_part"][...], 0.0)
    for x in range(6):
        for z in range(10):
            keep = valid(gx, 4, sizes[0], -1, x) * valid(gz, 8, sizes[2], -1, z)
            at = 96 * (z // 2) + 16 * x
            cell = jnp.where(mid_rows, merged[at : at + 16, tile(z % 2)], 0.0) * keep
            for h in range(2):
                mg_wide[h, x, z, pl.ds(h, 16, stride=2), :] = cell

    lift = (b["lift0"], b["lift1"], b["lift2"])
    for x in range(6):
        for dy in range(3):
            halves = [mg_wide[h, x, :, dy + 1 : dy + 17, :].astype(BF16).reshape(160, 128) for h in range(2)]
            piece = jnp.concatenate(halves, axis=1)
            value = dot(piece, t_lt[...]).astype(BF16)
            for i in range(2):
                to = 2 * x + i - 1
                if 0 <= to < 10:
                    for z in range(10):
                        lift[dy][to, :, tile(z)] = value[16 * z : 16 * z + 16, tile(i)]

    total = conv_top(lift, b["t_lift"]) + b["part"][...]
    for g in range(4):
        out[:, :, 256 * g : 256 * g + 256] = total[128 * g : 128 * g + 128].astype(BF16).reshape(8, 16, 256)
    for exchange in (vol_x, pm_x, skip_x, pl_x, sm_x):
        exchange.wait_send()


def body(sizes, volume, *weights):
    w_top, w_da, w_db, w_la, w_lb, w_ll, w_um, w_lt, w_out = weights
    flat = [
        w_top.reshape(1728, 64),
        w_da.reshape(1728, 128),
        w_db.reshape(3456, 128),
        w_la.reshape(3456, 256),
        w_lb.reshape(6912, 256),
        w_ll.reshape(256, 4, 2, 128),
        w_um.reshape(6912, 128),
        w_lt.transpose(1, 2, 3, 4, 0).reshape(512, 128),
        w_out.swapaxes(3, 4).reshape(1728, 128),
    ]
    any_space = pl.BlockSpec(memory_space=pl.ANY)
    few, many = len(DIRS), len(LOW_DIRS)
    counts = (10, few, few, few, few, few, few, few, few, many, many)
    return pl.pallas_call(
        functools.partial(kernel, sizes),
        out_shape=pltpu.VMEM(volume.shape, BF16),
        in_specs=[any_space] * 10,
        out_specs=pl.BlockSpec(memory_space=pltpu.VMEM),
        scratch_shapes=[pltpu.VMEM(s, d) for s, d in SCRATCH.values()]
        + [pltpu.SemaphoreType.DMA((c,)) for c in counts],
        compiler_params=pltpu.CompilerParams(
            collective_id=0, has_side_effects=True, vmem_limit_bytes=56 * 1024 * 1024
        ),
    )(volume, *flat)


def solution(mesh):
    placed = (P("gx", "gy", "gz"),) + (P(),) * 9
    sizes = tuple(mesh.shape[name] for name in ("gx", "gy", "gz"))
    return jax.shard_map(
        functools.partial(body, sizes),
        mesh=mesh,
        in_specs=placed,
        out_specs=P("gx", "gy", "gz"),
        check_vma=False,
    )
```

```python
import functools

import jax
import jax.numpy as jnp
from jax import lax
from jax.experimental import pallas as pl
from jax.experimental.pallas import tpu as pltpu
from jax.sharding import PartitionSpec as P

F32 = jnp.float32
BF16 = jnp.bfloat16
MESH = pl.DeviceIdType.MESH


def farthest_first(steps):
    return sorted(steps, key=lambda step: -sum(abs(s) for s in step))


DIRS = farthest_first(
    [
        (dx, dy, dz)
        for dx in (-1, 0, 1)
        for dy in (-1, 0, 1)
        for dz in (-1, 0, 1)
        if (dx, dy, dz) != (0, 0, 0)
    ]
)
LINE_DIRS = farthest_first([(dx, 0, 0) for dx in (-2, -1, 1, 2)])
PLANE_DIRS = [step for step in DIRS if step[0] == 0]
GREETED = DIRS + LINE_DIRS[:2]


def dot(a, b):
    return jnp.dot(a, b, preferred_element_type=F32)


def side(step):
    return 0 if step == 1 else 1


SCRATCH = dict(
    k_top=((1728, 64), BF16),
    k_da=((1728, 128), BF16),
    k_db=((3456, 128), BF16),
    k_la=((3456, 256), BF16),
    k_lb=((6912, 256), BF16),
    k_ll=((256, 1024), BF16),
    k_um=((6912, 128), BF16),
    k_lt=((512, 128), BF16),
    k_out=((1728, 128), BF16),
    raw_ll=((256, 4, 2, 128), BF16),
    t_top=((9, 512, 256), BF16),
    t_skip=((9, 512, 256), BF16),
    t_lift=((9, 384, 256), BF16),
    t_da=((9, 256, 256), BF16),
    t_lt=((256, 256), BF16),
    t_um=((2, 9, 512, 256), BF16),
    wide=((10, 320, 128), F32),
    vol0=((10, 16, 1280), BF16),
    vol1=((10, 16, 1280), BF16),
    vol2=((10, 16, 1280), BF16),
    skip0=((10, 16, 1280), BF16),
    skip1=((10, 16, 1280), BF16),
    skip2=((10, 16, 1280), BF16),
    lift0=((10, 16, 1152), BF16),
    lift1=((10, 16, 1152), BF16),
    lift2=((10, 16, 1152), BF16),
    vol_a=((2, 4, 16, 128), BF16),
    vol_b=((2, 2, 16, 128), BF16),
    vol_r=((2, 12, 16, 128), BF16),
    skip_a=((2, 4, 16, 128), BF16),
    skip_b=((2, 2, 16, 128), BF16),
    skip_r=((2, 12, 16, 128), BF16),
    tmp=((4, 16, 128), F32),
    top_out=((8, 128, 128), F32),
    part=((512, 256), F32),
    pm=((4, 6, 16, 128), BF16),
    pm_y=((2, 2, 16, 128), BF16),
    pm_r=((2, 3, 3, 2, 16, 128), BF16),
    pm_t=((2, 2, 16, 128), F32),
    pm_wide=((8, 24, 768), F32),
    pm_s=((3, 8, 16, 768), BF16),
    fm_wide=((6, 10, 24, 128), F32),
    fm_s=((6, 64, 1152), BF16),
    sm_out=((4, 8, 8, 128), F32),
    sm=((8, 6, 16, 128), BF16),
    sm_y=((2, 4, 16, 128), BF16),
    sm_e=((2, 2, 16, 128), BF16),
    sm_r=((2, 3, 4, 16, 128), BF16),
    sm_c=((2, 3, 2, 16, 128), BF16),
    sm_u=((2, 16, 128), F32),
    sm_t=((4, 16, 128), F32),
    pl_t=((2, 4, 8, 128), F32),
    pl_f=((2, 16, 128), F32),
    pl_r=((3, 3, 8, 16, 128), BF16),
    pl_g=((3, 16, 128), F32),
    pl_wide=((8, 10, 16, 128), F32),
    pl_s=((8, 64, 1152), BF16),
    fl_wide=((6, 8, 16, 256), F32),
    fl_s=((6, 48, 2304), BF16),
    jm_wide=((2, 8, 12, 24, 128), F32),
    jm_s=((2, 3, 8, 16, 1536), BF16),
    jm_part=((480, 256), F32),
    mg_wide=((2, 6, 10, 32, 128), F32),
)
NAMES = list(SCRATCH)
WEIGHTS = ("k_top", "k_da", "k_db", "k_la", "k_lb", "raw_ll", "k_um", "k_lt", "k_out")
ORDER = ("k_top", "k_da", "raw_ll", "k_out", "k_um", "k_db", "k_lt", "k_la", "k_lb")


class Exchange:
    def __init__(self, dirs, message, send, recv, here, sizes):
        self.dirs, self.message = dirs, message
        self.send, self.recv = send, recv
        self.here, self.sizes = here, sizes

    def inside(self, step, sign):
        ok = None
        for at, size, s in zip(self.here, self.sizes, step):
            s = s * sign
            if s == 0:
                continue
            this = at + s < size if s > 0 else at + s >= 0
            ok = this if ok is None else jnp.logical_and(ok, this)
        return ok

    def copy(self, i):
        step = self.dirs[i]
        src, dst = self.message(step)
        there = tuple(at + s for at, s in zip(self.here, step))
        return pltpu.make_async_remote_copy(
            src_ref=src,
            dst_ref=dst,
            send_sem=self.send.at[i],
            recv_sem=self.recv.at[i],
            device_id=there,
            device_id_type=MESH,
        )

    def start(self):
        for i, step in enumerate(self.dirs):
            pl.when(self.inside(step, 1))(lambda i=i: self.copy(i).start())

    def wait_recv(self):
        for i, step in enumerate(self.dirs):
            pl.when(self.inside(step, -1))(lambda i=i: self.copy(i).wait_recv())

    def wait_send(self):
        for i, step in enumerate(self.dirs):
            pl.when(self.inside(step, 1))(lambda i=i: self.copy(i).wait_send())


def kernel(sizes, *refs):
    vol, weights, out = refs[0], refs[1:10], refs[10]
    n = len(NAMES)
    b = dict(zip(NAMES, refs[11 : 11 + n]))
    (load_sem, vol_ss, vol_rs, skip_ss, skip_rs, pm_ss, pm_rs, sm_ss, sm_rs, line_ss, line_rs, pl_ss, pl_rs) = refs[11 + n :]
    here = tuple(lax.axis_index(name) for name in ("gx", "gy", "gz"))
    gx, gy, gz = here
    tile = lambda t: slice(128 * t, 128 * t + 128)

    vol1 = b["vol1"]
    vol_loads = [
        pltpu.make_async_copy(vol.at[x], vol1.at[x + 1, :, 128:1152], load_sem.at[9 + x]) for x in range(8)
    ]
    for load in vol_loads:
        load.start()

    def zero(ref, *at):
        if at:
            ref[at] = jnp.zeros(ref.at[at].shape, ref.dtype)
        else:
            ref[...] = jnp.zeros(ref.shape, ref.dtype)

    everything = slice(None)
    for name in ("vol1", "skip1"):
        zero(b[name], slice(0, 1))
        zero(b[name], slice(9, 10))
        zero(b[name], slice(1, 9), everything, tile(0))
        zero(b[name], slice(1, 9), everything, tile(9))
    for name in ("vol_r", "skip_r", "pm_r", "sm_r", "sm_c", "pl_r"):
        zero(b[name])
    for name, width, lo, hi in (("pm", 4, 1, 3), ("sm", 8, 2, 6)):
        zero(b[name], slice(0, lo))
        zero(b[name], slice(hi, width))
        zero(b[name], slice(lo, hi), slice(0, 1))
        zero(b[name], slice(lo, hi), slice(5, 6))

    barrier = pltpu.get_barrier_semaphore()
    greeting = Exchange(GREETED, None, None, None, here, sizes)
    for step in GREETED:

        @pl.when(greeting.inside(step, 1))
        def _(step=step):
            pl.semaphore_signal(
                barrier,
                inc=1,
                device_id=tuple(at + s for at, s in zip(here, step)),
                device_id_type=MESH,
            )

    loads = {}
    for name in ORDER:
        i = WEIGHTS.index(name)
        loads[name] = pltpu.make_async_copy(weights[i], b[name], load_sem.at[i])
        loads[name].start()

    def reach(at, size, far):
        return jnp.where(at >= far, 1, 0) + jnp.where(at + far < size, 1, 0)

    greeted = reach(gx, sizes[0], 2) - 1
    around = 1
    for at, size in zip(here, sizes):
        around = around * (1 + reach(at, size, 1))
    greeted = greeted + around

    wide = b["wide"]
    tmp = b["tmp"]

    def stage_top(cells, a, bb):
        for x in range(1, 9):
            for t in range(1, 9):
                wide[t, 32 * x + 8 : 32 * x + 24, :] = cells[x, :, tile(t)].astype(F32)
        for s, y in ((0, 15), (1, 0)):
            for tp in range(4):
                pair = [
                    wide[2 * tp + h + 1, pl.ds(32 + 8 + y, 8, stride=32), :] for h in range(2)
                ]
                a[s, tp] = jnp.concatenate(pair, axis=0).astype(BF16)
            for xs, x in ((0, 8), (1, 1)):
                for t in range(8):
                    tmp[2 * s + xs, t : t + 1, :] = wide[t + 1, 32 * x + 8 + y : 32 * x + 9 + y, :]
                for t in range(8, 16):
                    tmp[2 * s + xs, t : t + 1, :] = jnp.zeros((1, 128), F32)
                bb[s, xs] = tmp[2 * s + xs].astype(BF16)

    def top_message(cells, a, bb, r):
        def message(step):
            dx, dy, dz = step
            if dy == 0:
                sx = {0: slice(1, 9), 1: slice(8, 9), -1: slice(1, 2)}[dx]
                tx = {0: slice(1, 9), 1: slice(0, 1), -1: slice(9, 10)}[dx]
                sz = {0: slice(128, 1152), 1: tile(8), -1: tile(1)}[dz]
                tz = {0: slice(128, 1152), 1: tile(0), -1: tile(9)}[dz]
                return cells.at[sx, :, sz], cells.at[tx, :, tz]
            s = side(dy)
            if dx == 0 and dz == 0:
                return a.at[s], r.at[s, 0:4]
            if dz == 0:
                return bb.at[s, side(dx)], r.at[s, 6 + side(dx)]
            tp = 3 if dz == 1 else 0
            slot = 4 + side(dz) if dx == 0 else 8 + 2 * side(dx) + side(dz)
            return a.at[s, tp], r.at[s, slot]

        return message

    def shift_top(cells, r, below, above):
        for x in range(10):
            for t in range(10) if x in (0, 9) else (0, 9):
                wide[t, 32 * x + 8 : 32 * x + 24, :] = cells[x, :, tile(t)].astype(F32)
        for s, row in ((0, 7), (1, 24)):
            rows = pl.ds(32 + row, 8, stride=32)
            for tp in range(4):
                both = r[s, tp].astype(F32)
                wide[2 * tp + 1, rows, :] = both[0:8]
                wide[2 * tp + 2, rows, :] = both[8:16]
            for zs, t, half in ((0, 0, 8), (1, 9, 0)):
                wide[t, rows, :] = r[s, 4 + zs].astype(F32)[half : half + 8]
            for xs, x, keep in ((0, 0, 7), (1, 9, 0)):
                at = slice(32 * x + row, 32 * x + row + 1)
                tmp[xs] = r[s, 6 + xs].astype(F32)
                for t in range(8):
                    wide[t + 1, at, :] = tmp[xs, t : t + 1, :]
                for zs, t, half in ((0, 0, 8), (1, 9, 0)):
                    tmp[2 + zs] = r[s, 8 + 2 * xs + zs].astype(F32)
                    wide[t, at, :] = tmp[2 + zs, half + keep : half + keep + 1, :]
        for x in range(10):
            for t in range(10):
                below[x, :, tile(t)] = wide[t, 32 * x + 7 : 32 * x + 23, :].astype(BF16)
                above[x, :, tile(t)] = wide[t, 32 * x + 9 : 32 * x + 25, :].astype(BF16)

    def conv_top(shifted, kernels, depth=512):
        total = None
        for dx in range(3):
            for dy in range(3):
                piece = jnp.concatenate(
                    [
                        shifted[dy][dx : dx + 8, :, 256 * g : 256 * g + depth].reshape(128, depth)
                        for g in range(4)
                    ],
                    axis=0,
                )
                term = dot(piece, kernels[3 * dx + dy])
                total = term if total is None else total + term
        return total

    low_half = lax.broadcasted_iota(jnp.int32, (64, 128), 1) < 64

    def band(block, target, k, lead=1):
        nothing = jnp.zeros((64, 128), F32)
        blocks = [block(dz) for dz in range(3)]
        pick = lambda dz: blocks[dz] if 0 <= dz < 3 else nothing
        for zi in range(6 + 2 * lead):
            for h in range(2):
                both = jnp.where(low_half, pick(zi - lead - 2 * h), pick(zi - lead - 1 - 2 * h))
                target[k, 64 * zi : 64 * zi + 64, tile(h)] = both.astype(BF16)

    def pairs(block, count, depth, target):
        for zi in range(count):
            for zo in range(count - 2):
                value = block(zi - zo) if 0 <= zi - zo < 3 else jnp.zeros((depth, 128), BF16)
                target[depth * zi : depth * zi + depth, tile(zo)] = value

    eye = jnp.where(
        lax.broadcasted_iota(jnp.int32, (128, 128), 0) == lax.broadcasted_iota(jnp.int32, (128, 128), 1),
        1.0,
        0.0,
    ).astype(BF16)

    def turned(block):
        return lax.dot_general(eye, block, (((1,), (1,)), ((), ())), preferred_element_type=F32)

    for load in vol_loads:
        load.wait()
    stage_top(vol1, b["vol_a"], b["vol_b"])
    vol_x = Exchange(
        DIRS, top_message(vol1, b["vol_a"], b["vol_b"], b["vol_r"]), vol_ss, vol_rs, here, sizes
    )
    pl.semaphore_wait(barrier, greeted)
    vol_x.start()
    mg_wide = b["mg_wide"]
    zero(mg_wide)
    loads["k_top"].wait()
    for k in range(9):

        def top_block(dz, k=k):
            half = b["k_top"][64 * (3 * k + dz) : 64 * (3 * k + dz) + 64, :].astype(F32)
            return jnp.concatenate([half, half], axis=1)

        band(top_block, b["t_top"], k)
    loads["k_da"].wait()
    for k in range(9):
        pairs(
            lambda dz, k=k: b["k_da"][64 * (3 * k + dz) : 64 * (3 * k + dz) + 64, :],
            4,
            64,
            b["t_da"].at[k],
        )
    loads["raw_ll"].wait()
    for q in range(0, 256, 64):
        raw = b["raw_ll"][q : q + 64].astype(F32)
        for i in range(4):
            for k in range(2):
                b["k_ll"][q : q + 64, tile(2 * i + k)] = raw[:, i, k, :].astype(BF16)
    loads["k_out"].wait()
    for k in range(9):
        turns = []
        for dz in range(3):
            block = b["k_out"][64 * (3 * k + dz) : 64 * (3 * k + dz) + 64, :]
            turns.append(turned(jnp.concatenate([block, block], axis=0)))
        band(lambda dz: turns[dz][0:64], b["t_lift"], k, 0)
        band(lambda dz: turns[dz][64:128], b["t_skip"], k)
    vol_x.wait_recv()
    shift_top(vol1, b["vol_r"], b["vol0"], b["vol2"])
    top_out = b["top_out"]
    skip1 = b["skip1"]

    kept = jnp.maximum(conv_top((b["vol0"], vol1, b["vol2"]), b["t_top"]), 0.0)
    for g in range(4):
        block = kept[128 * g : 128 * g + 128]
        for h in range(2):
            top_out[2 * g + h] = block[:, tile(h)]
        skip1[1:9, :, 256 * g + 128 : 256 * g + 384] = block.astype(BF16).reshape(8, 16, 256)

    pm, pm_wide = b["pm"], b["pm_wide"]
    first_lanes = lax.broadcasted_iota(jnp.int32, (8, 128), 1) < 64
    for xp in range(2):
        for q in range(4):
            held = []
            for xm in (2 * xp, 2 * xp + 1):
                found = []
                for j in (2 * q, 2 * q + 1):
                    parts = [
                        top_out[j, pl.ds(16 * x + p, 8, stride=2), :]
                        for x in (2 * xm, 2 * xm + 1)
                        for p in range(2)
                    ]
                    most = jnp.maximum(jnp.maximum(parts[0], parts[1]), jnp.maximum(parts[2], parts[3]))
                    found.append(jnp.maximum(most, pltpu.roll(most, 64, 1)))
                cell = jnp.where(first_lanes, found[0], found[1])
                pm_wide[xm + 2, 2:10, tile(q + 1)] = cell
                held.append(cell)
            pm[xp + 1, q + 1] = jnp.concatenate(held, axis=0).astype(BF16)
    for s, y in ((0, 6), (1, 0)):
        for xm in range(4):
            for q in range(4):
                row = 4 * q + 2 * (xm % 2)
                b["pm_t"][s, xm // 2, row : row + 2, :] = pm_wide[xm + 2, y + 2 : y + 4, tile(q + 1)]
        for xp in range(2):
            b["pm_y"][s, xp] = b["pm_t"][s, xp].astype(BF16)

    def pm_message(step):
        dx, dy, dz = step
        if dy == 0:
            sx = {0: slice(1, 3), 1: slice(2, 3), -1: slice(1, 2)}[dx]
            tx = {0: slice(1, 3), 1: slice(0, 1), -1: slice(3, 4)}[dx]
            sz = {0: slice(1, 5), 1: slice(4, 5), -1: slice(1, 2)}[dz]
            tz = {0: slice(1, 5), 1: slice(0, 1), -1: slice(5, 6)}[dz]
            return pm.at[sx, sz], pm.at[tx, tz]
        s = side(dy)
        xs = {0: slice(0, 2), 1: slice(1, 2), -1: slice(0, 1)}[dx]
        return b["pm_y"].at[s, xs], b["pm_r"].at[s, dx + 1, dz + 1, xs]

    pm_x = Exchange(DIRS, pm_message, pm_ss, pm_rs, here, sizes)
    pm_x.start()

    stage_top(skip1, b["skip_a"], b["skip_b"])
    skip_x = Exchange(
        DIRS, top_message(skip1, b["skip_a"], b["skip_b"], b["skip_r"]), skip_ss, skip_rs, here, sizes
    )
    skip_x.start()
    loads["k_um"].wait()
    for half in range(2):
        for k in range(9):

            def up_block(dz, half=half, k=k):
                at = 256 * (3 * k + dz) + 128 * half
                return b["k_um"][at : at + 128, :]

            pairs(up_block, 4, 128, b["t_um"].at[half, k])
    pm_x.wait_recv()
    for xp in range(4):
        for zp in range(6):
            if 1 <= xp < 3 and 1 <= zp < 5:
                continue
            both = pm[xp, zp].astype(F32)
            pm_wide[2 * xp, 2:10, tile(zp)] = both[0:8]
            pm_wide[2 * xp + 1, 2:10, tile(zp)] = both[8:16]
    for s, y in ((0, 0), (1, 10)):
        for dx in (-1, 0, 1):
            for xp in {0: (0, 1), 1: (1,), -1: (0,)}[dx]:
                base = {0: 2 + 2 * xp, 1: 0, -1: 6}[dx]
                for dz in (-1, 0, 1):
                    slot = b["pm_t"].at[0, (dz + 1) % 2]
                    slot[...] = b["pm_r"][s, dx + 1, dz + 1, xp].astype(F32)
                    for q in {0: (0, 1, 2, 3), 1: (3,), -1: (0,)}[dz]:
                        to = {0: q + 1, 1: 0, -1: 5}[dz]
                        for xi in range(2):
                            row = 4 * q + 2 * xi
                            pm_wide[base + xi, y : y + 2, tile(to)] = slot[row : row + 2, :]
    pm_s = b["pm_s"]
    for x in range(8):
        for dy in range(3):
            pm_s[dy, x] = pm_wide[x, dy : dy + 16, :].astype(BF16)

    def flag(ok):
        return jnp.where(ok, 1.0, 0.0).astype(F32)

    def valid(at, local, size, first, index):
        place = at * local + first + index
        return flag(jnp.logical_and(place >= 0, place < local * size))

    def row_mask(rows, lanes, used, at, local, size, first):
        place = lax.broadcasted_iota(jnp.int32, (rows, lanes), 0)
        whole = place + (at * local + first)
        ok = jnp.logical_and(whole >= 0, whole < local * size)
        return jnp.logical_and(ok, place < used)

    fm_wide = b["fm_wide"]
    mid_rows = row_mask(16, 128, 10, gy, 8, sizes[1], -1)
    first_mid = None
    for dx in range(3):
        for dy in range(3):
            piece = jnp.concatenate(
                [pm_s[dy, dx : dx + 6, :, 128 * j : 128 * j + 256].reshape(96, 256) for j in range(5)],
                axis=0,
            )
            term = dot(piece, b["t_da"][3 * dx + dy])
            first_mid = term if first_mid is None else first_mid + term
    first_mid = jnp.maximum(first_mid, 0.0)
    for x in range(6):
        for z in range(10):
            keep = valid(gx, 4, sizes[0], -1, x) * valid(gz, 8, sizes[2], -1, z)
            at = 96 * (z // 2) + 16 * x
            cell = first_mid[at : at + 16, tile(z % 2)]
            fm_wide[x, z, 0:16, :] = jnp.where(mid_rows, cell, 0.0) * keep

    def gather(wide_ref, target, xs, pairs, lanes):
        for x in range(xs):
            for zp in range(pairs):
                for dy in range(3):
                    for dz in range(3):
                        both = jnp.concatenate(
                            [wide_ref[x, 2 * zp + h + dz, dy : dy + 8, :] for h in range(2)], axis=0
                        )
                        at = (3 * dy + dz) * lanes
                        target[x, 16 * zp : 16 * zp + 16, at : at + lanes] = both.astype(BF16)

    def conv_rows(source, xs, kernels):
        rows, depth = source.shape[1], source.shape[2]
        total = None
        for dx in range(3):
            piece = source[dx : dx + xs].reshape(xs * rows, depth)
            term = dot(piece, kernels[dx * depth : (dx + 1) * depth, :])
            total = term if total is None else total + term
        return jnp.maximum(total, 0.0)

    gather(fm_wide, b["fm_s"], 6, 4, 128)
    loads["k_db"].wait()
    sm_out, sm = b["sm_out"], b["sm"]
    skip_mid = conv_rows(b["fm_s"], 4, b["k_db"])
    sm_out[...] = skip_mid.reshape(4, 8, 8, 128)
    sm[2:6, 1:5] = skip_mid.astype(BF16).reshape(4, 4, 16, 128)

    pl_t, pl_f, pl_r = b["pl_t"], b["pl_f"], b["pl_r"]
    for x in range(2):
        for z in range(4):
            parts = [sm_out[2 * x + i, 2 * z + k] for i in range(2) for k in range(2)]
            pl_t[x, z] = jnp.maximum(jnp.maximum(parts[0], parts[1]), jnp.maximum(parts[2], parts[3]))
            pl_f[x, 4 * z : 4 * z + 4, :] = jnp.maximum(
                pl_t[x, z, pl.ds(0, 4, stride=2), :], pl_t[x, z, pl.ds(1, 4, stride=2), :]
            )
        pl_r[1, 1, 3 + x] = pl_f[x].astype(BF16)

    def line_message(step):
        sx, tx = {
            1: (slice(3, 5), slice(1, 3)),
            -1: (slice(3, 5), slice(5, 7)),
            2: (slice(4, 5), slice(0, 1)),
            -2: (slice(3, 4), slice(7, 8)),
        }[step[0]]
        return pl_r.at[1, 1, sx], pl_r.at[1, 1, tx]

    def pl_message(step):
        return pl_r.at[1, 1], pl_r.at[1 - step[2], 1 - step[1]]

    line_x = Exchange(LINE_DIRS, line_message, line_ss, line_rs, here, sizes)
    pl_x = Exchange(PLANE_DIRS, pl_message, pl_ss, pl_rs, here, sizes)
    line_x.start()

    sm_t = b["sm_t"]
    for s, y in ((0, 6), (1, 0)):
        for x in range(4):
            for z in range(8):
                sm_t[x, 2 * z : 2 * z + 2, :] = sm_out[x, z, y : y + 2, :]
            b["sm_y"][s, x] = sm_t[x].astype(BF16)
        for zs, z in ((0, 6), (1, 0)):
            for x in range(4):
                b["sm_u"][zs, 4 * x : 4 * x + 4, :] = sm_t[x, 2 * z : 2 * z + 4, :]
            b["sm_e"][s, zs] = b["sm_u"][zs].astype(BF16)

    def sm_message(step):
        dx, dy, dz = step
        if dy == 0:
            sx = {0: slice(2, 6), 1: slice(4, 6), -1: slice(2, 4)}[dx]
            tx = {0: slice(2, 6), 1: slice(0, 2), -1: slice(6, 8)}[dx]
            sz = {0: slice(1, 5), 1: slice(4, 5), -1: slice(1, 2)}[dz]
            tz = {0: slice(1, 5), 1: slice(0, 1), -1: slice(5, 6)}[dz]
            return sm.at[sx, sz], sm.at[tx, tz]
        s = side(dy)
        if dz != 0:
            return b["sm_e"].at[s, side(dz)], b["sm_c"].at[s, dx + 1, side(dz)]
        xs = {0: slice(0, 4), 1: slice(2, 4), -1: slice(0, 2)}[dx]
        return b["sm_y"].at[s, xs], b["sm_r"].at[s, dx + 1, xs]

    sm_x = Exchange(DIRS, sm_message, sm_ss, sm_rs, here, sizes)
    sm_x.start()

    skip_x.wait_recv()
    shift_top(skip1, b["skip_r"], b["skip0"], b["skip2"])

    b["part"][...] = conv_top((b["skip0"], skip1, b["skip2"]), b["t_skip"])
    line_x.wait_recv()
    pl_x.start()

    t_lt = b["t_lt"]
    loads["k_lt"].wait()
    for i in range(2):
        for h in range(2):
            at = 128 * (2 * i + h)
            swapped = [b["k_lt"][at + 64 : at + 128, :], b["k_lt"][at : at + 64, :]]
            t_lt[128 * h : 128 * h + 128, tile(i)] = turned(jnp.concatenate(swapped, axis=0)).astype(BF16)

    jm_wide, jm_s = b["jm_wide"], b["jm_s"]
    sm_x.wait_recv()
    for x in range(8):
        for zp in range(6):
            both = sm[x, zp].astype(F32)
            for h in range(2):
                jm_wide[1, x, 2 * zp + h, 2:10, :] = both[8 * h : 8 * h + 8]
    for s, y in ((0, 0), (1, 10)):
        for dx in (-1, 0, 1):
            for xi in {0: (0, 1, 2, 3), 1: (2, 3), -1: (0, 1)}[dx]:
                x = {0: 2 + xi, 1: xi - 2, -1: 6 + xi}[dx]
                slot = sm_t.at[xi % 2]
                slot[...] = b["sm_r"][s, dx + 1, xi].astype(F32)
                for z in range(8):
                    jm_wide[1, x, z + 2, y : y + 2, :] = slot[2 * z : 2 * z + 2, :]
            for zs, to in ((0, 0), (1, 10)):
                slot = sm_t.at[2 + zs]
                slot[...] = b["sm_c"][s, dx + 1, zs].astype(F32)
                for xi in {0: (0, 1, 2, 3), 1: (2, 3), -1: (0, 1)}[dx]:
                    x = {0: 2 + xi, 1: xi - 2, -1: 6 + xi}[dx]
                    for z in range(2):
                        row = 4 * xi + 2 * z
                        jm_wide[1, x, to + z, y : y + 2, :] = slot[row : row + 2, :]

    def shift_mid(half):
        for x in range(8):
            for z in range(12):
                for dy in range(3):
                    jm_s[half, dy, x, :, tile(z)] = jm_wide[half, x, z, dy : dy + 16, :].astype(BF16)

    def conv_mid(half):
        total = None
        for dx in range(3):
            for dy in range(3):
                piece = jnp.concatenate(
                    [
                        jm_s[half, dy, dx : dx + 6, :, 256 * j : 256 * j + 512].reshape(96, 512)
                        for j in range(5)
                    ],
                    axis=0,
                )
                term = dot(piece, b["t_um"][half, 3 * dx + dy])
                total = term if total is None else total + term
        return total

    shift_mid(1)
    b["jm_part"][...] = conv_mid(1)

    pl_x.wait_recv()
    pl_wide, pl_g = b["pl_wide"], b["pl_g"]
    for x in range(8):
        for zs in range(3):
            for ys in range(3):
                pl_g[ys] = pl_r[zs, ys, x].astype(F32)
            for z, to in {0: ((1, 0), (2, 1), (3, 2)), 1: ((0, 3), (1, 4), (2, 5), (3, 6)), 2: ((0, 7), (1, 8), (2, 9))}[zs]:
                pl_wide[x, to, 0:3, :] = pl_g[0, 4 * z + 1 : 4 * z + 4, :]
                pl_wide[x, to, 3:7, :] = pl_g[1, 4 * z : 4 * z + 4, :]
                pl_wide[x, to, 7:10, :] = pl_g[2, 4 * z : 4 * z + 3, :]
    gather(pl_wide, b["pl_s"], 8, 4, 128)
    loads["k_la"].wait()
    first_low = conv_rows(b["pl_s"], 6, b["k_la"])
    fl_wide = b["fl_wide"]
    low_rows = row_mask(8, 256, 8, gy, 4, sizes[1], -2)
    for x in range(6):
        for z in range(8):
            keep = valid(gx, 2, sizes[0], -2, x) * valid(gz, 4, sizes[2], -2, z)
            at = 64 * x + 8 * z
            fl_wide[x, z, 0:8, :] = jnp.where(low_rows, first_low[at : at + 8, :], 0.0) * keep
            fl_wide[x, z, 8:16, :] = jnp.zeros((8, 256), F32)
    gather(fl_wide, b["fl_s"], 6, 3, 256)
    loads["k_lb"].wait()
    coarse = conv_rows(b["fl_s"], 4, b["k_lb"])
    coarse_rows = row_mask(8, 256, 6, gy, 4, sizes[1], -1)
    cells = []
    for x in range(4):
        for z in range(6):
            keep = valid(gx, 2, sizes[0], -1, x) * valid(gz, 4, sizes[2], -1, z)
            at = 48 * x + 8 * z
            cells.append(jnp.where(coarse_rows, coarse[at : at + 8, :], 0.0) * keep)
    coarse = jnp.concatenate(cells, axis=0).astype(BF16)

    lifted = dot(coarse, b["k_ll"][...])
    for x in range(4):
        for z in range(6):
            for i in range(2):
                for h in range(2):
                    for k in range(2):
                        at = 48 * x + 8 * z
                        jm_wide[0, 2 * x + i, 2 * z + k, pl.ds(h, 8, stride=2), :] = lifted[
                            at : at + 8, tile(4 * i + 2 * h + k)
                        ]

    mg_wide = b["mg_wide"]
    shift_mid(0)
    merged = jnp.maximum(conv_mid(0) + b["jm_part"][...], 0.0)
    for x in range(6):
        for z in range(10):
            keep = valid(gx, 4, sizes[0], -1, x) * valid(gz, 8, sizes[2], -1, z)
            at = 96 * (z // 2) + 16 * x
            cell = jnp.where(mid_rows, merged[at : at + 16, tile(z % 2)], 0.0) * keep
            for h in range(2):
                mg_wide[h, x, z, pl.ds(h, 16, stride=2), :] = cell

    lift_half = lax.broadcasted_iota(jnp.int32, (16, 128), 1) < 64
    lift = (b["lift0"], b["lift1"], b["lift2"])
    for x in range(6):
        for dy in range(3):
            halves = [mg_wide[h, x, :, dy + 1 : dy + 17, :].astype(BF16).reshape(160, 128) for h in range(2)]
            piece = jnp.concatenate(halves, axis=1)
            value = dot(piece, t_lt[...]).astype(BF16)
            for i in range(2):
                to = 2 * x + i - 1
                if 0 <= to < 10:
                    for t in range(9):
                        lift[dy][to, :, tile(t)] = jnp.where(
                            lift_half,
                            value[16 * t : 16 * t + 16, tile(i)],
                            value[16 * t + 16 : 16 * t + 32, tile(i)],
                        )

    total = conv_top(lift, b["t_lift"], 384) + b["part"][...]
    for g in range(4):
        out[:, :, 256 * g : 256 * g + 256] = total[128 * g : 128 * g + 128].astype(BF16).reshape(8, 16, 256)
    for exchange in (vol_x, pm_x, skip_x, line_x, pl_x, sm_x):
        exchange.wait_send()


def body(sizes, volume, *weights):
    w_top, w_da, w_db, w_la, w_lb, w_ll, w_um, w_lt, w_out = weights
    flat = [
        w_top.reshape(1728, 64),
        w_da.reshape(1728, 128),
        w_db.reshape(3456, 128),
        w_la.reshape(3456, 256),
        w_lb.reshape(6912, 256),
        w_ll.reshape(256, 4, 2, 128),
        w_um.reshape(6912, 128),
        w_lt.transpose(1, 2, 3, 4, 0).reshape(512, 128),
        w_out.swapaxes(3, 4).reshape(1728, 128),
    ]
    any_space = pl.BlockSpec(memory_space=pl.ANY)
    few, line, plane = len(DIRS), len(LINE_DIRS), len(PLANE_DIRS)
    counts = (17, few, few, few, few, few, few, few, few, line, line, plane, plane)
    return pl.pallas_call(
        functools.partial(kernel, sizes),
        out_shape=pltpu.VMEM(volume.shape, BF16),
        in_specs=[any_space] * 10,
        out_specs=pl.BlockSpec(memory_space=pltpu.VMEM),
        scratch_shapes=[pltpu.VMEM(s, d) for s, d in SCRATCH.values()]
        + [pltpu.SemaphoreType.DMA((c,)) for c in counts],
        compiler_params=pltpu.CompilerParams(
            collective_id=0, has_side_effects=True, vmem_limit_bytes=56 * 1024 * 1024
        ),
    )(volume, *flat)


def solution(mesh):
    placed = (P("gx", "gy", "gz"),) + (P(),) * 9
    sizes = tuple(mesh.shape[name] for name in ("gx", "gy", "gz"))
    return jax.shard_map(
        functools.partial(body, sizes),
        mesh=mesh,
        in_specs=placed,
        out_specs=P("gx", "gy", "gz"),
        check_vma=False,
    )
```

```python
import functools

import jax
import jax.numpy as jnp
from jax import lax
from jax.experimental import pallas as pl
from jax.experimental.pallas import tpu as pltpu
from jax.sharding import PartitionSpec as P

F32 = jnp.float32
BF16 = jnp.bfloat16
MESH = pl.DeviceIdType.MESH


def farthest_first(steps):
    return sorted(steps, key=lambda step: -(2 * abs(step[0]) + abs(step[1]) + 3 * abs(step[2])))


DIRS = farthest_first(
    [
        (dx, dy, dz)
        for dx in (-1, 0, 1)
        for dy in (-1, 0, 1)
        for dz in (-1, 0, 1)
        if (dx, dy, dz) != (0, 0, 0)
    ]
)
LINE_DIRS = farthest_first([(dx, 0, 0) for dx in (-2, -1, 1, 2)])
PLANE_DIRS = [step for step in DIRS if step[0] == 0]
GREETED = DIRS + LINE_DIRS[:2]


def dot(a, b):
    return jnp.dot(a, b, preferred_element_type=F32)


def in_plane(step):
    return step[1] == 0


def off_plane(step):
    return step[1] != 0


def side(step):
    return 0 if step == 1 else 1


SCRATCH = dict(
    k_top=((1728, 64), BF16),
    k_da=((1728, 128), BF16),
    k_db=((3456, 128), BF16),
    k_la=((3456, 256), BF16),
    k_lb=((6912, 256), BF16),
    k_ll=((256, 1024), BF16),
    k_um=((6912, 128), BF16),
    k_lt=((512, 128), BF16),
    k_out=((1728, 128), BF16),
    raw_ll=((256, 4, 2, 128), BF16),
    t_top=((9, 512, 256), BF16),
    t_skip=((9, 512, 256), BF16),
    t_lift=((9, 384, 256), BF16),
    t_da=((9, 256, 256), BF16),
    t_lt=((256, 256), BF16),
    t_um=((2, 9, 512, 256), BF16),
    wide=((10, 320, 128), F32),
    vol0=((10, 16, 1280), BF16),
    vol1=((10, 16, 1280), BF16),
    vol2=((10, 16, 1280), BF16),
    skip0=((10, 16, 1280), BF16),
    skip1=((10, 16, 1280), BF16),
    skip2=((10, 16, 1280), BF16),
    lift0=((10, 16, 1152), BF16),
    lift1=((10, 16, 1152), BF16),
    lift2=((10, 16, 1152), BF16),
    vol_a=((2, 4, 16, 128), BF16),
    vol_b=((2, 2, 16, 128), BF16),
    vol_r=((2, 12, 16, 128), BF16),
    skip_a=((2, 4, 16, 128), BF16),
    skip_b=((2, 2, 16, 128), BF16),
    skip_r=((2, 12, 16, 128), BF16),
    tmp=((4, 16, 128), F32),
    top_out=((8, 128, 128), F32),
    part=((512, 256), F32),
    pm=((4, 6, 16, 128), BF16),
    pm_y=((2, 2, 16, 128), BF16),
    pm_r=((2, 3, 3, 2, 16, 128), BF16),
    pm_t=((2, 2, 16, 128), F32),
    pm_wide=((8, 24, 768), F32),
    pm_s=((3, 8, 16, 768), BF16),
    fm_wide=((6, 10, 24, 128), F32),
    fm_s=((2, 3, 6, 80, 128), BF16),
    sm_out=((4, 8, 8, 128), F32),
    sm=((8, 6, 16, 128), BF16),
    sm_y=((2, 4, 16, 128), BF16),
    sm_e=((2, 2, 16, 128), BF16),
    sm_r=((2, 3, 4, 16, 128), BF16),
    sm_c=((2, 3, 2, 16, 128), BF16),
    sm_u=((2, 16, 128), F32),
    sm_t=((4, 16, 128), F32),
    pl_t=((2, 4, 8, 128), F32),
    pl_f=((2, 16, 128), F32),
    pl_r=((3, 3, 8, 16, 128), BF16),
    pl_g=((3, 16, 128), F32),
    pl_wide=((8, 10, 16, 128), F32),
    pl_s=((2, 3, 8, 80, 128), BF16),
    fl_wide=((6, 8, 16, 256), F32),
    fl_s=((2, 3, 6, 64, 256), BF16),
    jm_wide=((2, 8, 12, 24, 128), F32),
    jm_s=((2, 3, 8, 16, 1536), BF16),
    jm_part=((480, 256), F32),
    mg_wide=((2, 6, 10, 32, 128), F32),
)
NAMES = list(SCRATCH)
WEIGHTS = ("k_top", "k_da", "k_db", "k_la", "k_lb", "raw_ll", "k_um", "k_lt", "k_out")
ORDER = ("k_top", "k_da", "raw_ll", "k_out", "k_um", "k_db", "k_lt", "k_la", "k_lb")


class Exchange:
    def __init__(self, dirs, message, send, recv, here, sizes):
        self.dirs, self.message = dirs, message
        self.send, self.recv = send, recv
        self.here, self.sizes = here, sizes

    def inside(self, step, sign):
        ok = None
        for at, size, s in zip(self.here, self.sizes, step):
            s = s * sign
            if s == 0:
                continue
            this = at + s < size if s > 0 else at + s >= 0
            ok = this if ok is None else jnp.logical_and(ok, this)
        return ok

    def copy(self, i):
        step = self.dirs[i]
        src, dst = self.message(step)
        there = tuple(at + s for at, s in zip(self.here, step))
        return pltpu.make_async_remote_copy(
            src_ref=src,
            dst_ref=dst,
            send_sem=self.send.at[i],
            recv_sem=self.recv.at[i],
            device_id=there,
            device_id_type=MESH,
        )

    def start(self, chosen=lambda step: True):
        for i, step in enumerate(self.dirs):
            if not chosen(step):
                continue
            pl.when(self.inside(step, 1))(lambda i=i: self.copy(i).start())

    def wait_recv(self):
        for i, step in enumerate(self.dirs):
            pl.when(self.inside(step, -1))(lambda i=i: self.copy(i).wait_recv())

    def wait_send(self):
        for i, step in enumerate(self.dirs):
            pl.when(self.inside(step, 1))(lambda i=i: self.copy(i).wait_send())


def kernel(sizes, *refs):
    vol, weights, out = refs[0], refs[1:10], refs[10]
    n = len(NAMES)
    b = dict(zip(NAMES, refs[11 : 11 + n]))
    (load_sem, vol_ss, vol_rs, skip_ss, skip_rs, pm_ss, pm_rs, sm_ss, sm_rs, line_ss, line_rs, pl_ss, pl_rs) = refs[11 + n :]
    here = tuple(lax.axis_index(name) for name in ("gx", "gy", "gz"))
    gx, gy, gz = here
    tile = lambda t: slice(128 * t, 128 * t + 128)

    vol1 = b["vol1"]
    vol_loads = [
        pltpu.make_async_copy(vol.at[x], vol1.at[x + 1, :, 128:1152], load_sem.at[9 + x]) for x in range(8)
    ]
    for load in vol_loads:
        load.start()

    def zero(ref, *at):
        if at:
            ref[at] = jnp.zeros(ref.at[at].shape, ref.dtype)
        else:
            ref[...] = jnp.zeros(ref.shape, ref.dtype)

    everything = slice(None)
    for name in ("vol1", "skip1"):
        zero(b[name], slice(0, 1))
        zero(b[name], slice(9, 10))
        zero(b[name], slice(1, 9), everything, tile(0))
        zero(b[name], slice(1, 9), everything, tile(9))
    for name in ("vol_r", "skip_r", "pm_r", "sm_r", "sm_c", "pl_r"):
        zero(b[name])
    for name, width, lo, hi in (("pm", 4, 1, 3), ("sm", 8, 2, 6)):
        zero(b[name], slice(0, lo))
        zero(b[name], slice(hi, width))
        zero(b[name], slice(lo, hi), slice(0, 1))
        zero(b[name], slice(lo, hi), slice(5, 6))

    barrier = pltpu.get_barrier_semaphore()
    greeting = Exchange(GREETED, None, None, None, here, sizes)
    for step in GREETED:

        @pl.when(greeting.inside(step, 1))
        def _(step=step):
            pl.semaphore_signal(
                barrier,
                inc=1,
                device_id=tuple(at + s for at, s in zip(here, step)),
                device_id_type=MESH,
            )

    loads = {}
    for name in ORDER:
        i = WEIGHTS.index(name)
        loads[name] = pltpu.make_async_copy(weights[i], b[name], load_sem.at[i])
        loads[name].start()

    def reach(at, size, far):
        return jnp.where(at >= far, 1, 0) + jnp.where(at + far < size, 1, 0)

    greeted = reach(gx, sizes[0], 2) - 1
    around = 1
    for at, size in zip(here, sizes):
        around = around * (1 + reach(at, size, 1))
    greeted = greeted + around

    wide = b["wide"]
    tmp = b["tmp"]

    def stage_top(cells, a, bb):
        for x in range(1, 9):
            for t in range(1, 9):
                wide[t, 32 * x + 8 : 32 * x + 24, :] = cells[x, :, tile(t)].astype(F32)
        for s, y in ((0, 15), (1, 0)):
            for tp in range(4):
                pair = [
                    wide[2 * tp + h + 1, pl.ds(32 + 8 + y, 8, stride=32), :] for h in range(2)
                ]
                a[s, tp] = jnp.concatenate(pair, axis=0).astype(BF16)
            for xs, x in ((0, 8), (1, 1)):
                for t in range(8):
                    tmp[2 * s + xs, t : t + 1, :] = wide[t + 1, 32 * x + 8 + y : 32 * x + 9 + y, :]
                for t in range(8, 16):
                    tmp[2 * s + xs, t : t + 1, :] = jnp.zeros((1, 128), F32)
                bb[s, xs] = tmp[2 * s + xs].astype(BF16)

    def top_message(cells, a, bb, r):
        def message(step):
            dx, dy, dz = step
            if dy == 0:
                sx = {0: slice(1, 9), 1: slice(8, 9), -1: slice(1, 2)}[dx]
                tx = {0: slice(1, 9), 1: slice(0, 1), -1: slice(9, 10)}[dx]
                sz = {0: slice(128, 1152), 1: tile(8), -1: tile(1)}[dz]
                tz = {0: slice(128, 1152), 1: tile(0), -1: tile(9)}[dz]
                return cells.at[sx, :, sz], cells.at[tx, :, tz]
            s = side(dy)
            if dx == 0 and dz == 0:
                return a.at[s], r.at[s, 0:4]
            if dz == 0:
                return bb.at[s, side(dx)], r.at[s, 6 + side(dx)]
            tp = 3 if dz == 1 else 0
            slot = 4 + side(dz) if dx == 0 else 8 + 2 * side(dx) + side(dz)
            return a.at[s, tp], r.at[s, slot]

        return message

    def shift_top(cells, r, below, above):
        for x in range(10):
            for t in range(10) if x in (0, 9) else (0, 9):
                wide[t, 32 * x + 8 : 32 * x + 24, :] = cells[x, :, tile(t)].astype(F32)
        for s, row in ((0, 7), (1, 24)):
            rows = pl.ds(32 + row, 8, stride=32)
            for tp in range(4):
                both = r[s, tp].astype(F32)
                wide[2 * tp + 1, rows, :] = both[0:8]
                wide[2 * tp + 2, rows, :] = both[8:16]
            for zs, t, half in ((0, 0, 8), (1, 9, 0)):
                wide[t, rows, :] = r[s, 4 + zs].astype(F32)[half : half + 8]
            for xs, x, keep in ((0, 0, 7), (1, 9, 0)):
                at = slice(32 * x + row, 32 * x + row + 1)
                tmp[xs] = r[s, 6 + xs].astype(F32)
                for t in range(8):
                    wide[t + 1, at, :] = tmp[xs, t : t + 1, :]
                for zs, t, half in ((0, 0, 8), (1, 9, 0)):
                    tmp[2 + zs] = r[s, 8 + 2 * xs + zs].astype(F32)
                    wide[t, at, :] = tmp[2 + zs, half + keep : half + keep + 1, :]
        for x in range(10):
            for t in range(10):
                below[x, :, tile(t)] = wide[t, 32 * x + 7 : 32 * x + 23, :].astype(BF16)
                above[x, :, tile(t)] = wide[t, 32 * x + 9 : 32 * x + 25, :].astype(BF16)

    def conv_top(shifted, kernels, depth=512):
        total = None
        for dx in range(3):
            for dy in range(3):
                piece = jnp.concatenate(
                    [
                        shifted[dy][dx : dx + 8, :, 256 * g : 256 * g + depth].reshape(128, depth)
                        for g in range(4)
                    ],
                    axis=0,
                )
                term = dot(piece, kernels[3 * dx + dy])
                total = term if total is None else total + term
        return total

    low_half = lax.broadcasted_iota(jnp.int32, (64, 128), 1) < 64

    def band(block, target, k, lead=1):
        nothing = jnp.zeros((64, 128), F32)
        blocks = [block(dz) for dz in range(3)]
        pick = lambda dz: blocks[dz] if 0 <= dz < 3 else nothing
        for zi in range(6 + 2 * lead):
            for h in range(2):
                both = jnp.where(low_half, pick(zi - lead - 2 * h), pick(zi - lead - 1 - 2 * h))
                target[k, 64 * zi : 64 * zi + 64, tile(h)] = both.astype(BF16)

    def pairs(block, count, depth, target):
        for zi in range(count):
            for zo in range(count - 2):
                value = block(zi - zo) if 0 <= zi - zo < 3 else jnp.zeros((depth, 128), BF16)
                target[depth * zi : depth * zi + depth, tile(zo)] = value

    eye = jnp.where(
        lax.broadcasted_iota(jnp.int32, (128, 128), 0) == lax.broadcasted_iota(jnp.int32, (128, 128), 1),
        1.0,
        0.0,
    ).astype(BF16)

    def turned(block):
        return lax.dot_general(eye, block, (((1,), (1,)), ((), ())), preferred_element_type=F32)

    for load in vol_loads:
        load.wait()
    stage_top(vol1, b["vol_a"], b["vol_b"])
    vol_x = Exchange(
        DIRS, top_message(vol1, b["vol_a"], b["vol_b"], b["vol_r"]), vol_ss, vol_rs, here, sizes
    )
    pl.semaphore_wait(barrier, greeted)
    vol_x.start()
    mg_wide = b["mg_wide"]
    zero(mg_wide)
    loads["k_top"].wait()
    for k in range(9):

        def top_block(dz, k=k):
            half = b["k_top"][64 * (3 * k + dz) : 64 * (3 * k + dz) + 64, :].astype(F32)
            return jnp.concatenate([half, half], axis=1)

        band(top_block, b["t_top"], k)
    loads["k_da"].wait()
    for k in range(9):
        pairs(
            lambda dz, k=k: b["k_da"][64 * (3 * k + dz) : 64 * (3 * k + dz) + 64, :],
            4,
            64,
            b["t_da"].at[k],
        )
    vol_x.wait_recv()
    shift_top(vol1, b["vol_r"], b["vol0"], b["vol2"])
    top_out = b["top_out"]
    skip1 = b["skip1"]

    kept = jnp.maximum(conv_top((b["vol0"], vol1, b["vol2"]), b["t_top"]), 0.0)
    for g in range(4):
        block = kept[128 * g : 128 * g + 128]
        for h in range(2):
            top_out[2 * g + h] = block[:, tile(h)]
        skip1[1:9, :, 256 * g + 128 : 256 * g + 384] = block.astype(BF16).reshape(8, 16, 256)

    pm, pm_wide = b["pm"], b["pm_wide"]
    first_lanes = lax.broadcasted_iota(jnp.int32, (8, 128), 1) < 64
    for xp in range(2):
        for q in range(4):
            held = []
            for xm in (2 * xp, 2 * xp + 1):
                found = []
                for j in (2 * q, 2 * q + 1):
                    parts = [
                        top_out[j, pl.ds(16 * x + p, 8, stride=2), :]
                        for x in (2 * xm, 2 * xm + 1)
                        for p in range(2)
                    ]
                    most = jnp.maximum(jnp.maximum(parts[0], parts[1]), jnp.maximum(parts[2], parts[3]))
                    found.append(jnp.maximum(most, pltpu.roll(most, 64, 1)))
                cell = jnp.where(first_lanes, found[0], found[1])
                pm_wide[xm + 2, 2:10, tile(q + 1)] = cell
                held.append(cell)
            pm[xp + 1, q + 1] = jnp.concatenate(held, axis=0).astype(BF16)
    def pm_message(step):
        dx, dy, dz = step
        if dy == 0:
            sx = {0: slice(1, 3), 1: slice(2, 3), -1: slice(1, 2)}[dx]
            tx = {0: slice(1, 3), 1: slice(0, 1), -1: slice(3, 4)}[dx]
            sz = {0: slice(1, 5), 1: slice(4, 5), -1: slice(1, 2)}[dz]
            tz = {0: slice(1, 5), 1: slice(0, 1), -1: slice(5, 6)}[dz]
            return pm.at[sx, sz], pm.at[tx, tz]
        s = side(dy)
        xs = {0: slice(0, 2), 1: slice(1, 2), -1: slice(0, 1)}[dx]
        return b["pm_y"].at[s, xs], b["pm_r"].at[s, dx + 1, dz + 1, xs]

    pm_x = Exchange(DIRS, pm_message, pm_ss, pm_rs, here, sizes)
    pm_x.start(in_plane)
    for s, y in ((0, 6), (1, 0)):
        for xm in range(4):
            for q in range(4):
                row = 4 * q + 2 * (xm % 2)
                b["pm_t"][s, xm // 2, row : row + 2, :] = pm_wide[xm + 2, y + 2 : y + 4, tile(q + 1)]
        for xp in range(2):
            b["pm_y"][s, xp] = b["pm_t"][s, xp].astype(BF16)
    pm_x.start(off_plane)

    skip_x = Exchange(
        DIRS, top_message(skip1, b["skip_a"], b["skip_b"], b["skip_r"]), skip_ss, skip_rs, here, sizes
    )
    skip_x.start(in_plane)
    stage_top(skip1, b["skip_a"], b["skip_b"])
    skip_x.start(off_plane)
    loads["k_out"].wait()
    for k in range(9):
        turns = []
        for dz in range(3):
            block = b["k_out"][64 * (3 * k + dz) : 64 * (3 * k + dz) + 64, :]
            turns.append(turned(jnp.concatenate([block, block], axis=0)))
        band(lambda dz: turns[dz][0:64], b["t_lift"], k, 0)
        band(lambda dz: turns[dz][64:128], b["t_skip"], k)
    loads["raw_ll"].wait()
    for q in range(0, 256, 64):
        raw = b["raw_ll"][q : q + 64].astype(F32)
        for i in range(4):
            for k in range(2):
                b["k_ll"][q : q + 64, tile(2 * i + k)] = raw[:, i, k, :].astype(BF16)
    loads["k_um"].wait()
    for half in range(2):
        for k in range(9):

            def up_block(dz, half=half, k=k):
                at = 256 * (3 * k + dz) + 128 * half
                return b["k_um"][at : at + 128, :]

            pairs(up_block, 4, 128, b["t_um"].at[half, k])
    pm_x.wait_recv()
    for xp in range(4):
        for zp in range(6):
            if 1 <= xp < 3 and 1 <= zp < 5:
                continue
            both = pm[xp, zp].astype(F32)
            pm_wide[2 * xp, 2:10, tile(zp)] = both[0:8]
            pm_wide[2 * xp + 1, 2:10, tile(zp)] = both[8:16]
    for s, y in ((0, 0), (1, 10)):
        for dx in (-1, 0, 1):
            for xp in {0: (0, 1), 1: (1,), -1: (0,)}[dx]:
                base = {0: 2 + 2 * xp, 1: 0, -1: 6}[dx]
                for dz in (-1, 0, 1):
                    slot = b["pm_t"].at[0, (dz + 1) % 2]
                    slot[...] = b["pm_r"][s, dx + 1, dz + 1, xp].astype(F32)
                    for q in {0: (0, 1, 2, 3), 1: (3,), -1: (0,)}[dz]:
                        to = {0: q + 1, 1: 0, -1: 5}[dz]
                        for xi in range(2):
                            row = 4 * q + 2 * xi
                            pm_wide[base + xi, y : y + 2, tile(to)] = slot[row : row + 2, :]
    pm_s = b["pm_s"]
    for x in range(8):
        for dy in range(3):
            pm_s[dy, x] = pm_wide[x, dy : dy + 16, :].astype(BF16)

    def flag(ok):
        return jnp.where(ok, 1.0, 0.0).astype(F32)

    def valid(at, local, size, first, index):
        place = at * local + first + index
        return flag(jnp.logical_and(place >= 0, place < local * size))

    def row_mask(rows, lanes, used, at, local, size, first):
        place = lax.broadcasted_iota(jnp.int32, (rows, lanes), 0)
        whole = place + (at * local + first)
        ok = jnp.logical_and(whole >= 0, whole < local * size)
        return jnp.logical_and(ok, place < used)

    fm_wide = b["fm_wide"]
    mid_rows = row_mask(16, 128, 10, gy, 8, sizes[1], -1)
    first_mid = None
    for dx in range(3):
        for dy in range(3):
            piece = jnp.concatenate(
                [pm_s[dy, dx : dx + 6, :, 128 * j : 128 * j + 256].reshape(96, 256) for j in range(5)],
                axis=0,
            )
            term = dot(piece, b["t_da"][3 * dx + dy])
            first_mid = term if first_mid is None else first_mid + term
    first_mid = jnp.maximum(first_mid, 0.0)
    for x in range(6):
        for z in range(10):
            keep = valid(gx, 4, sizes[0], -1, x) * valid(gz, 8, sizes[2], -1, z)
            at = 96 * (z // 2) + 16 * x
            cell = first_mid[at : at + 16, tile(z % 2)]
            fm_wide[x, z, 0:16, :] = jnp.where(mid_rows, cell, 0.0) * keep

    def gather(wide_ref, target, xs, count):
        for x in range(xs):
            for dy in range(3):
                for odd in range(2):
                    for zp in range(count + 1 - odd):
                        z = 2 * zp + odd
                        both = jnp.concatenate(
                            [wide_ref[x, z + h, dy : dy + 8, :] for h in range(2)], axis=0
                        )
                        target[odd, dy, x, 16 * zp : 16 * zp + 16, :] = both.astype(BF16)

    def conv_rows(source, xs, count, kernels):
        total = None
        for dx in range(3):
            pieces = []
            for dy in range(3):
                for dz in range(3):
                    first = 16 * (dz // 2)
                    piece = source[dz % 2, dy, dx : dx + xs, first : first + 16 * count, :]
                    pieces.append(piece.reshape(xs * 16 * count, source.shape[4]))
            depth = 9 * source.shape[4]
            term = dot(jnp.concatenate(pieces, axis=1), kernels[dx * depth : (dx + 1) * depth, :])
            total = term if total is None else total + term
        return jnp.maximum(total, 0.0)

    gather(fm_wide, b["fm_s"], 6, 4)
    loads["k_db"].wait()
    sm_out, sm = b["sm_out"], b["sm"]
    skip_mid = conv_rows(b["fm_s"], 4, 4, b["k_db"])
    sm_out[...] = skip_mid.reshape(4, 8, 8, 128)
    sm[2:6, 1:5] = skip_mid.astype(BF16).reshape(4, 4, 16, 128)

    pl_t, pl_f, pl_r = b["pl_t"], b["pl_f"], b["pl_r"]
    for x in range(2):
        for z in range(4):
            parts = [sm_out[2 * x + i, 2 * z + k] for i in range(2) for k in range(2)]
            pl_t[x, z] = jnp.maximum(jnp.maximum(parts[0], parts[1]), jnp.maximum(parts[2], parts[3]))
            pl_f[x, 4 * z : 4 * z + 4, :] = jnp.maximum(
                pl_t[x, z, pl.ds(0, 4, stride=2), :], pl_t[x, z, pl.ds(1, 4, stride=2), :]
            )
        pl_r[1, 1, 3 + x] = pl_f[x].astype(BF16)

    def line_message(step):
        sx, tx = {
            1: (slice(3, 5), slice(1, 3)),
            -1: (slice(3, 5), slice(5, 7)),
            2: (slice(4, 5), slice(0, 1)),
            -2: (slice(3, 4), slice(7, 8)),
        }[step[0]]
        return pl_r.at[1, 1, sx], pl_r.at[1, 1, tx]

    def pl_message(step):
        return pl_r.at[1, 1], pl_r.at[1 - step[2], 1 - step[1]]

    line_x = Exchange(LINE_DIRS, line_message, line_ss, line_rs, here, sizes)
    pl_x = Exchange(PLANE_DIRS, pl_message, pl_ss, pl_rs, here, sizes)
    line_x.start()

    sm_t = b["sm_t"]
    for s, y in ((0, 6), (1, 0)):
        for x in range(4):
            for z in range(8):
                sm_t[x, 2 * z : 2 * z + 2, :] = sm_out[x, z, y : y + 2, :]
            b["sm_y"][s, x] = sm_t[x].astype(BF16)
        for zs, z in ((0, 6), (1, 0)):
            for x in range(4):
                b["sm_u"][zs, 4 * x : 4 * x + 4, :] = sm_t[x, 2 * z : 2 * z + 4, :]
            b["sm_e"][s, zs] = b["sm_u"][zs].astype(BF16)

    def sm_message(step):
        dx, dy, dz = step
        if dy == 0:
            sx = {0: slice(2, 6), 1: slice(4, 6), -1: slice(2, 4)}[dx]
            tx = {0: slice(2, 6), 1: slice(0, 2), -1: slice(6, 8)}[dx]
            sz = {0: slice(1, 5), 1: slice(4, 5), -1: slice(1, 2)}[dz]
            tz = {0: slice(1, 5), 1: slice(0, 1), -1: slice(5, 6)}[dz]
            return sm.at[sx, sz], sm.at[tx, tz]
        s = side(dy)
        if dz != 0:
            return b["sm_e"].at[s, side(dz)], b["sm_c"].at[s, dx + 1, side(dz)]
        xs = {0: slice(0, 4), 1: slice(2, 4), -1: slice(0, 2)}[dx]
        return b["sm_y"].at[s, xs], b["sm_r"].at[s, dx + 1, xs]

    sm_x = Exchange(DIRS, sm_message, sm_ss, sm_rs, here, sizes)
    sm_x.start()

    skip_x.wait_recv()
    shift_top(skip1, b["skip_r"], b["skip0"], b["skip2"])

    b["part"][...] = conv_top((b["skip0"], skip1, b["skip2"]), b["t_skip"])
    line_x.wait_recv()
    pl_x.start()

    t_lt = b["t_lt"]
    loads["k_lt"].wait()
    for i in range(2):
        for h in range(2):
            at = 128 * (2 * i + h)
            swapped = [b["k_lt"][at + 64 : at + 128, :], b["k_lt"][at : at + 64, :]]
            t_lt[128 * h : 128 * h + 128, tile(i)] = turned(jnp.concatenate(swapped, axis=0)).astype(BF16)

    jm_wide, jm_s = b["jm_wide"], b["jm_s"]
    sm_x.wait_recv()
    for x in range(8):
        for zp in range(6):
            both = sm[x, zp].astype(F32)
            for h in range(2):
                jm_wide[1, x, 2 * zp + h, 2:10, :] = both[8 * h : 8 * h + 8]
    for s, y in ((0, 0), (1, 10)):
        for dx in (-1, 0, 1):
            for xi in {0: (0, 1, 2, 3), 1: (2, 3), -1: (0, 1)}[dx]:
                x = {0: 2 + xi, 1: xi - 2, -1: 6 + xi}[dx]
                slot = sm_t.at[xi % 2]
                slot[...] = b["sm_r"][s, dx + 1, xi].astype(F32)
                for z in range(8):
                    jm_wide[1, x, z + 2, y : y + 2, :] = slot[2 * z : 2 * z + 2, :]
            for zs, to in ((0, 0), (1, 10)):
                slot = sm_t.at[2 + zs]
                slot[...] = b["sm_c"][s, dx + 1, zs].astype(F32)
                for xi in {0: (0, 1, 2, 3), 1: (2, 3), -1: (0, 1)}[dx]:
                    x = {0: 2 + xi, 1: xi - 2, -1: 6 + xi}[dx]
                    for z in range(2):
                        row = 4 * xi + 2 * z
                        jm_wide[1, x, to + z, y : y + 2, :] = slot[row : row + 2, :]

    def shift_mid(half):
        for x in range(8):
            for z in range(12):
                for dy in range(3):
                    jm_s[half, dy, x, :, tile(z)] = jm_wide[half, x, z, dy : dy + 16, :].astype(BF16)

    def conv_mid(half):
        total = None
        for dx in range(3):
            for dy in range(3):
                piece = jnp.concatenate(
                    [
                        jm_s[half, dy, dx : dx + 6, :, 256 * j : 256 * j + 512].reshape(96, 512)
                        for j in range(5)
                    ],
                    axis=0,
                )
                term = dot(piece, b["t_um"][half, 3 * dx + dy])
                total = term if total is None else total + term
        return total

    shift_mid(1)
    b["jm_part"][...] = conv_mid(1)

    pl_x.wait_recv()
    pl_wide, pl_g = b["pl_wide"], b["pl_g"]
    for x in range(8):
        for zs in range(3):
            for ys in range(3):
                pl_g[ys] = pl_r[zs, ys, x].astype(F32)
            for z, to in {0: ((1, 0), (2, 1), (3, 2)), 1: ((0, 3), (1, 4), (2, 5), (3, 6)), 2: ((0, 7), (1, 8), (2, 9))}[zs]:
                pl_wide[x, to, 0:3, :] = pl_g[0, 4 * z + 1 : 4 * z + 4, :]
                pl_wide[x, to, 3:7, :] = pl_g[1, 4 * z : 4 * z + 4, :]
                pl_wide[x, to, 7:10, :] = pl_g[2, 4 * z : 4 * z + 3, :]
    gather(pl_wide, b["pl_s"], 8, 4)
    loads["k_la"].wait()
    first_low = conv_rows(b["pl_s"], 6, 4, b["k_la"])
    fl_wide = b["fl_wide"]
    low_rows = row_mask(8, 256, 8, gy, 4, sizes[1], -2)
    for x in range(6):
        for z in range(8):
            keep = valid(gx, 2, sizes[0], -2, x) * valid(gz, 4, sizes[2], -2, z)
            at = 64 * x + 8 * z
            fl_wide[x, z, 0:8, :] = jnp.where(low_rows, first_low[at : at + 8, :], 0.0) * keep
            fl_wide[x, z, 8:16, :] = jnp.zeros((8, 256), F32)
    gather(fl_wide, b["fl_s"], 6, 3)
    loads["k_lb"].wait()
    coarse = conv_rows(b["fl_s"], 4, 3, b["k_lb"])
    coarse_rows = row_mask(8, 256, 6, gy, 4, sizes[1], -1)
    cells = []
    for x in range(4):
        for z in range(6):
            keep = valid(gx, 2, sizes[0], -1, x) * valid(gz, 4, sizes[2], -1, z)
            at = 48 * x + 8 * z
            cells.append(jnp.where(coarse_rows, coarse[at : at + 8, :], 0.0) * keep)
    coarse = jnp.concatenate(cells, axis=0).astype(BF16)

    lifted = dot(coarse, b["k_ll"][...])
    for x in range(4):
        for z in range(6):
            for i in range(2):
                for h in range(2):
                    for k in range(2):
                        at = 48 * x + 8 * z
                        jm_wide[0, 2 * x + i, 2 * z + k, pl.ds(h, 8, stride=2), :] = lifted[
                            at : at + 8, tile(4 * i + 2 * h + k)
                        ]

    mg_wide = b["mg_wide"]
    shift_mid(0)
    merged = jnp.maximum(conv_mid(0) + b["jm_part"][...], 0.0)
    for x in range(6):
        for z in range(10):
            keep = valid(gx, 4, sizes[0], -1, x) * valid(gz, 8, sizes[2], -1, z)
            at = 96 * (z // 2) + 16 * x
            cell = jnp.where(mid_rows, merged[at : at + 16, tile(z % 2)], 0.0) * keep
            for h in range(2):
                mg_wide[h, x, z, pl.ds(h, 16, stride=2), :] = cell

    lift_half = lax.broadcasted_iota(jnp.int32, (16, 128), 1) < 64
    lift = (b["lift0"], b["lift1"], b["lift2"])
    for x in range(6):
        for dy in range(3):
            halves = [mg_wide[h, x, :, dy + 1 : dy + 17, :].astype(BF16).reshape(160, 128) for h in range(2)]
            piece = jnp.concatenate(halves, axis=1)
            value = dot(piece, t_lt[...]).astype(BF16)
            for i in range(2):
                to = 2 * x + i - 1
                if 0 <= to < 10:
                    for t in range(9):
                        lift[dy][to, :, tile(t)] = jnp.where(
                            lift_half,
                            value[16 * t : 16 * t + 16, tile(i)],
                            value[16 * t + 16 : 16 * t + 32, tile(i)],
                        )

    total = conv_top(lift, b["t_lift"], 384) + b["part"][...]
    for g in range(4):
        out[:, :, 256 * g : 256 * g + 256] = total[128 * g : 128 * g + 128].astype(BF16).reshape(8, 16, 256)
    for exchange in (vol_x, pm_x, skip_x, line_x, pl_x, sm_x):
        exchange.wait_send()


def body(sizes, volume, *weights):
    w_top, w_da, w_db, w_la, w_lb, w_ll, w_um, w_lt, w_out = weights
    flat = [
        w_top.reshape(1728, 64),
        w_da.reshape(1728, 128),
        w_db.reshape(3456, 128),
        w_la.reshape(3456, 256),
        w_lb.reshape(6912, 256),
        w_ll.reshape(256, 4, 2, 128),
        w_um.reshape(6912, 128),
        w_lt.transpose(1, 2, 3, 4, 0).reshape(512, 128),
        w_out.swapaxes(3, 4).reshape(1728, 128),
    ]
    any_space = pl.BlockSpec(memory_space=pl.ANY)
    few, line, plane = len(DIRS), len(LINE_DIRS), len(PLANE_DIRS)
    counts = (17, few, few, few, few, few, few, few, few, line, line, plane, plane)
    return pl.pallas_call(
        functools.partial(kernel, sizes),
        out_shape=pltpu.VMEM(volume.shape, BF16),
        in_specs=[any_space] * 10,
        out_specs=pl.BlockSpec(memory_space=pltpu.VMEM),
        scratch_shapes=[pltpu.VMEM(s, d) for s, d in SCRATCH.values()]
        + [pltpu.SemaphoreType.DMA((c,)) for c in counts],
        compiler_params=pltpu.CompilerParams(
            collective_id=0, has_side_effects=True, vmem_limit_bytes=56 * 1024 * 1024
        ),
    )(volume, *flat)


def solution(mesh):
    placed = (P("gx", "gy", "gz"),) + (P(),) * 9
    sizes = tuple(mesh.shape[name] for name in ("gx", "gy", "gz"))
    return jax.shard_map(
        functools.partial(body, sizes),
        mesh=mesh,
        in_specs=placed,
        out_specs=P("gx", "gy", "gz"),
        check_vma=False,
    )
```

```python
import functools

import jax
import jax.numpy as jnp
from jax import lax
from jax.experimental import pallas as pl
from jax.experimental.pallas import tpu as pltpu
from jax.sharding import PartitionSpec as P

F32 = jnp.float32
BF16 = jnp.bfloat16
MESH = pl.DeviceIdType.MESH


def farthest_first(steps):
    return sorted(steps, key=lambda step: -(2 * abs(step[0]) + abs(step[1]) + 3 * abs(step[2])))


DIRS = farthest_first(
    [
        (dx, dy, dz)
        for dx in (-1, 0, 1)
        for dy in (-1, 0, 1)
        for dz in (-1, 0, 1)
        if (dx, dy, dz) != (0, 0, 0)
    ]
)
LINE_DIRS = farthest_first([(dx, 0, 0) for dx in (-2, -1, 1, 2)])
PLANE_DIRS = [step for step in DIRS if step[0] == 0]
GREETED = DIRS + LINE_DIRS[:2]


def dot(a, b):
    return jnp.dot(a, b, preferred_element_type=F32)


def in_plane(step):
    return step[1] == 0


def off_plane(step):
    return step[1] != 0


def side(step):
    return 0 if step == 1 else 1


SCRATCH = dict(
    k_top=((1728, 64), BF16),
    k_da=((1728, 128), BF16),
    k_db=((3456, 128), BF16),
    k_la=((3456, 256), BF16),
    k_lb=((6912, 256), BF16),
    k_ll=((256, 1024), BF16),
    k_um=((6912, 128), BF16),
    k_lt=((512, 128), BF16),
    k_out=((1728, 128), BF16),
    raw_ll=((256, 4, 2, 128), BF16),
    t_top=((9, 512, 256), BF16),
    t_skip=((9, 512, 256), BF16),
    t_lift=((9, 384, 256), BF16),
    t_da=((9, 256, 256), BF16),
    t_lt=((256, 256), BF16),
    t_um=((2, 9, 512, 256), BF16),
    wide=((10, 320, 128), F32),
    vol0=((10, 16, 1280), BF16),
    vol1=((10, 16, 1280), BF16),
    vol2=((10, 16, 1280), BF16),
    skip0=((10, 16, 1280), BF16),
    skip1=((10, 16, 1280), BF16),
    skip2=((10, 16, 1280), BF16),
    lift0=((10, 16, 1152), BF16),
    lift1=((10, 16, 1152), BF16),
    lift2=((10, 16, 1152), BF16),
    vol_a=((2, 4, 16, 128), BF16),
    vol_b=((2, 2, 16, 128), BF16),
    vol_r=((2, 12, 16, 128), BF16),
    skip_a=((2, 4, 16, 128), BF16),
    skip_b=((2, 2, 16, 128), BF16),
    skip_r=((2, 12, 16, 128), BF16),
    tmp=((4, 16, 128), F32),
    top_out=((8, 128, 128), F32),
    part=((512, 256), F32),
    pm=((4, 6, 16, 128), BF16),
    pm_y=((2, 2, 16, 128), BF16),
    pm_r=((2, 3, 3, 2, 16, 128), BF16),
    pm_t=((2, 2, 16, 128), F32),
    pm_wide=((8, 24, 768), F32),
    pm_s=((3, 8, 16, 768), BF16),
    fm_wide=((6, 10, 24, 128), F32),
    fm_s=((2, 3, 6, 80, 128), BF16),
    sm_out=((4, 8, 8, 128), F32),
    sm=((8, 6, 16, 128), BF16),
    sm_y=((2, 4, 16, 128), BF16),
    sm_e=((2, 2, 16, 128), BF16),
    sm_r=((2, 3, 4, 16, 128), BF16),
    sm_c=((2, 3, 2, 16, 128), BF16),
    sm_u=((2, 16, 128), F32),
    sm_t=((4, 16, 128), F32),
    pl_t=((2, 4, 8, 128), F32),
    pl_f=((2, 16, 128), F32),
    pl_r=((3, 3, 8, 16, 128), BF16),
    pl_g=((3, 16, 128), F32),
    pl_wide=((8, 10, 16, 128), F32),
    pl_s=((2, 3, 8, 80, 128), BF16),
    fl_wide=((6, 8, 16, 256), F32),
    fl_s=((2, 3, 6, 64, 256), BF16),
    jm_wide=((2, 8, 12, 24, 128), F32),
    jm_s=((2, 3, 8, 16, 1536), BF16),
    jm_part=((480, 256), F32),
    mg_wide=((2, 6, 10, 32, 128), F32),
)
NAMES = list(SCRATCH)
WEIGHTS = ("k_top", "k_da", "k_db", "k_la", "k_lb", "raw_ll", "k_um", "k_lt", "k_out")
ORDER = ("k_top", "k_da", "raw_ll", "k_out", "k_um", "k_db", "k_lt", "k_la", "k_lb")


class Exchange:
    def __init__(self, dirs, message, send, recv, here, sizes):
        self.dirs, self.message = dirs, message
        self.send, self.recv = send, recv
        self.here, self.sizes = here, sizes

    def inside(self, step, sign):
        ok = None
        for at, size, s in zip(self.here, self.sizes, step):
            s = s * sign
            if s == 0:
                continue
            this = at + s < size if s > 0 else at + s >= 0
            ok = this if ok is None else jnp.logical_and(ok, this)
        return ok

    def copy(self, i):
        step = self.dirs[i]
        src, dst = self.message(step)
        there = tuple(at + s for at, s in zip(self.here, step))
        return pltpu.make_async_remote_copy(
            src_ref=src,
            dst_ref=dst,
            send_sem=self.send.at[i],
            recv_sem=self.recv.at[i],
            device_id=there,
            device_id_type=MESH,
        )

    def start(self, chosen=lambda step: True):
        for i, step in enumerate(self.dirs):
            if not chosen(step):
                continue
            pl.when(self.inside(step, 1))(lambda i=i: self.copy(i).start())

    def wait_recv(self):
        for i, step in enumerate(self.dirs):
            pl.when(self.inside(step, -1))(lambda i=i: self.copy(i).wait_recv())

    def wait_send(self):
        for i, step in enumerate(self.dirs):
            pl.when(self.inside(step, 1))(lambda i=i: self.copy(i).wait_send())


def kernel(sizes, *refs):
    vol, weights, out = refs[0], refs[1:10], refs[10]
    n = len(NAMES)
    b = dict(zip(NAMES, refs[11 : 11 + n]))
    (load_sem, vol_ss, vol_rs, skip_ss, skip_rs, pm_ss, pm_rs, sm_ss, sm_rs, line_ss, line_rs, pl_ss, pl_rs) = refs[11 + n :]
    here = tuple(lax.axis_index(name) for name in ("gx", "gy", "gz"))
    gx, gy, gz = here
    tile = lambda t: slice(128 * t, 128 * t + 128)

    vol1 = b["vol1"]
    vol_loads = [
        pltpu.make_async_copy(vol.at[x], vol1.at[x + 1, :, 128:1152], load_sem.at[9 + x]) for x in range(8)
    ]
    for load in vol_loads:
        load.start()

    def zero(ref, *at):
        if at:
            ref[at] = jnp.zeros(ref.at[at].shape, ref.dtype)
        else:
            ref[...] = jnp.zeros(ref.shape, ref.dtype)

    everything = slice(None)
    for name in ("vol1", "skip1"):
        zero(b[name], slice(0, 1))
        zero(b[name], slice(9, 10))
        zero(b[name], slice(1, 9), everything, tile(0))
        zero(b[name], slice(1, 9), everything, tile(9))
    for name in ("vol_r", "skip_r", "pm_r", "sm_r", "sm_c", "pl_r"):
        zero(b[name])
    for name, width, lo, hi in (("pm", 4, 1, 3), ("sm", 8, 2, 6)):
        zero(b[name], slice(0, lo))
        zero(b[name], slice(hi, width))
        zero(b[name], slice(lo, hi), slice(0, 1))
        zero(b[name], slice(lo, hi), slice(5, 6))

    barrier = pltpu.get_barrier_semaphore()
    greeting = Exchange(GREETED, None, None, None, here, sizes)
    for step in GREETED:

        @pl.when(greeting.inside(step, 1))
        def _(step=step):
            pl.semaphore_signal(
                barrier,
                inc=1,
                device_id=tuple(at + s for at, s in zip(here, step)),
                device_id_type=MESH,
            )

    loads = {}
    for name in ORDER:
        i = WEIGHTS.index(name)
        loads[name] = pltpu.make_async_copy(weights[i], b[name], load_sem.at[i])
        loads[name].start()

    def reach(at, size, far):
        return jnp.where(at >= far, 1, 0) + jnp.where(at + far < size, 1, 0)

    greeted = reach(gx, sizes[0], 2) - 1
    around = 1
    for at, size in zip(here, sizes):
        around = around * (1 + reach(at, size, 1))
    greeted = greeted + around

    wide = b["wide"]
    tmp = b["tmp"]

    def stage_top(cells, a, bb):
        for x in range(1, 9):
            for t in range(1, 9):
                wide[t, 32 * x + 8 : 32 * x + 24, :] = cells[x, :, tile(t)].astype(F32)
        for s, y in ((0, 15), (1, 0)):
            for tp in range(4):
                pair = [
                    wide[2 * tp + h + 1, pl.ds(32 + 8 + y, 8, stride=32), :] for h in range(2)
                ]
                a[s, tp] = jnp.concatenate(pair, axis=0).astype(BF16)
            for xs, x in ((0, 8), (1, 1)):
                for t in range(8):
                    tmp[2 * s + xs, t : t + 1, :] = wide[t + 1, 32 * x + 8 + y : 32 * x + 9 + y, :]
                for t in range(8, 16):
                    tmp[2 * s + xs, t : t + 1, :] = jnp.zeros((1, 128), F32)
                bb[s, xs] = tmp[2 * s + xs].astype(BF16)

    def top_message(cells, a, bb, r):
        def message(step):
            dx, dy, dz = step
            if dy == 0:
                sx = {0: slice(1, 9), 1: slice(8, 9), -1: slice(1, 2)}[dx]
                tx = {0: slice(1, 9), 1: slice(0, 1), -1: slice(9, 10)}[dx]
                sz = {0: slice(128, 1152), 1: tile(8), -1: tile(1)}[dz]
                tz = {0: slice(128, 1152), 1: tile(0), -1: tile(9)}[dz]
                return cells.at[sx, :, sz], cells.at[tx, :, tz]
            s = side(dy)
            if dx == 0 and dz == 0:
                return a.at[s], r.at[s, 0:4]
            if dz == 0:
                return bb.at[s, side(dx)], r.at[s, 6 + side(dx)]
            tp = 3 if dz == 1 else 0
            slot = 4 + side(dz) if dx == 0 else 8 + 2 * side(dx) + side(dz)
            return a.at[s, tp], r.at[s, slot]

        return message

    def shift_top(cells, r, below, above):
        for x in range(10):
            for t in range(10) if x in (0, 9) else (0, 9):
                wide[t, 32 * x + 8 : 32 * x + 24, :] = cells[x, :, tile(t)].astype(F32)
        for s, row in ((0, 7), (1, 24)):
            rows = pl.ds(32 + row, 8, stride=32)
            for tp in range(4):
                both = r[s, tp].astype(F32)
                wide[2 * tp + 1, rows, :] = both[0:8]
                wide[2 * tp + 2, rows, :] = both[8:16]
            for zs, t, half in ((0, 0, 8), (1, 9, 0)):
                wide[t, rows, :] = r[s, 4 + zs].astype(F32)[half : half + 8]
            for xs, x, keep in ((0, 0, 7), (1, 9, 0)):
                at = slice(32 * x + row, 32 * x + row + 1)
                tmp[xs] = r[s, 6 + xs].astype(F32)
                for t in range(8):
                    wide[t + 1, at, :] = tmp[xs, t : t + 1, :]
                for zs, t, half in ((0, 0, 8), (1, 9, 0)):
                    tmp[2 + zs] = r[s, 8 + 2 * xs + zs].astype(F32)
                    wide[t, at, :] = tmp[2 + zs, half + keep : half + keep + 1, :]
        for x in range(10):
            for t in range(10):
                below[x, :, tile(t)] = wide[t, 32 * x + 7 : 32 * x + 23, :].astype(BF16)
                above[x, :, tile(t)] = wide[t, 32 * x + 9 : 32 * x + 25, :].astype(BF16)

    def conv_top(shifted, kernels, depth=512):
        total = None
        for dx in range(3):
            for dy in range(3):
                piece = jnp.concatenate(
                    [
                        shifted[dy][dx : dx + 8, :, 256 * g : 256 * g + depth].reshape(128, depth)
                        for g in range(4)
                    ],
                    axis=0,
                )
                term = dot(piece, kernels[3 * dx + dy])
                total = term if total is None else total + term
        return total

    low_half = lax.broadcasted_iota(jnp.int32, (64, 128), 1) < 64

    def band(block, target, k, lead=1):
        nothing = jnp.zeros((64, 128), F32)
        blocks = [block(dz) for dz in range(3)]
        pick = lambda dz: blocks[dz] if 0 <= dz < 3 else nothing
        for zi in range(6 + 2 * lead):
            for h in range(2):
                both = jnp.where(low_half, pick(zi - lead - 2 * h), pick(zi - lead - 1 - 2 * h))
                target[k, 64 * zi : 64 * zi + 64, tile(h)] = both.astype(BF16)

    def pairs(block, count, depth, target):
        for zi in range(count):
            for zo in range(count - 2):
                value = block(zi - zo) if 0 <= zi - zo < 3 else jnp.zeros((depth, 128), BF16)
                target[depth * zi : depth * zi + depth, tile(zo)] = value

    eye = jnp.where(
        lax.broadcasted_iota(jnp.int32, (128, 128), 0) == lax.broadcasted_iota(jnp.int32, (128, 128), 1),
        1.0,
        0.0,
    ).astype(BF16)

    def turned(block):
        return lax.dot_general(eye, block, (((1,), (1,)), ((), ())), preferred_element_type=F32)

    for load in vol_loads:
        load.wait()
    stage_top(vol1, b["vol_a"], b["vol_b"])
    vol_x = Exchange(
        DIRS, top_message(vol1, b["vol_a"], b["vol_b"], b["vol_r"]), vol_ss, vol_rs, here, sizes
    )
    pl.semaphore_wait(barrier, greeted)
    vol_x.start()
    loads["k_top"].wait()
    for k in range(9):

        def top_block(dz, k=k):
            half = b["k_top"][64 * (3 * k + dz) : 64 * (3 * k + dz) + 64, :].astype(F32)
            return jnp.concatenate([half, half], axis=1)

        band(top_block, b["t_top"], k)
    loads["k_da"].wait()
    for k in range(9):
        pairs(
            lambda dz, k=k: b["k_da"][64 * (3 * k + dz) : 64 * (3 * k + dz) + 64, :],
            4,
            64,
            b["t_da"].at[k],
        )
    vol_x.wait_recv()
    shift_top(vol1, b["vol_r"], b["vol0"], b["vol2"])
    top_out = b["top_out"]
    skip1 = b["skip1"]

    kept = jnp.maximum(conv_top((b["vol0"], vol1, b["vol2"]), b["t_top"]), 0.0)
    for g in range(4):
        block = kept[128 * g : 128 * g + 128]
        for h in range(2):
            top_out[2 * g + h] = block[:, tile(h)]
        skip1[1:9, :, 256 * g + 128 : 256 * g + 384] = block.astype(BF16).reshape(8, 16, 256)

    pm, pm_wide = b["pm"], b["pm_wide"]
    first_lanes = lax.broadcasted_iota(jnp.int32, (8, 128), 1) < 64
    for xp in range(2):
        for q in range(4):
            held = []
            for xm in (2 * xp, 2 * xp + 1):
                found = []
                for j in (2 * q, 2 * q + 1):
                    parts = [
                        top_out[j, pl.ds(16 * x + p, 8, stride=2), :]
                        for x in (2 * xm, 2 * xm + 1)
                        for p in range(2)
                    ]
                    most = jnp.maximum(jnp.maximum(parts[0], parts[1]), jnp.maximum(parts[2], parts[3]))
                    found.append(jnp.maximum(most, pltpu.roll(most, 64, 1)))
                cell = jnp.where(first_lanes, found[0], found[1])
                pm_wide[xm + 2, 2:10, tile(q + 1)] = cell
                held.append(cell)
            pm[xp + 1, q + 1] = jnp.concatenate(held, axis=0).astype(BF16)
    def pm_message(step):
        dx, dy, dz = step
        if dy == 0:
            sx = {0: slice(1, 3), 1: slice(2, 3), -1: slice(1, 2)}[dx]
            tx = {0: slice(1, 3), 1: slice(0, 1), -1: slice(3, 4)}[dx]
            sz = {0: slice(1, 5), 1: slice(4, 5), -1: slice(1, 2)}[dz]
            tz = {0: slice(1, 5), 1: slice(0, 1), -1: slice(5, 6)}[dz]
            return pm.at[sx, sz], pm.at[tx, tz]
        s = side(dy)
        xs = {0: slice(0, 2), 1: slice(1, 2), -1: slice(0, 1)}[dx]
        return b["pm_y"].at[s, xs], b["pm_r"].at[s, dx + 1, dz + 1, xs]

    pm_x = Exchange(DIRS, pm_message, pm_ss, pm_rs, here, sizes)
    pm_x.start(in_plane)
    for s, y in ((0, 6), (1, 0)):
        for xm in range(4):
            for q in range(4):
                row = 4 * q + 2 * (xm % 2)
                b["pm_t"][s, xm // 2, row : row + 2, :] = pm_wide[xm + 2, y + 2 : y + 4, tile(q + 1)]
        for xp in range(2):
            b["pm_y"][s, xp] = b["pm_t"][s, xp].astype(BF16)
    pm_x.start(off_plane)

    skip_x = Exchange(
        DIRS, top_message(skip1, b["skip_a"], b["skip_b"], b["skip_r"]), skip_ss, skip_rs, here, sizes
    )
    skip_x.start(in_plane)
    stage_top(skip1, b["skip_a"], b["skip_b"])
    skip_x.start(off_plane)
    loads["k_out"].wait()
    for k in range(9):
        turns = []
        for dz in range(3):
            block = b["k_out"][64 * (3 * k + dz) : 64 * (3 * k + dz) + 64, :]
            turns.append(turned(jnp.concatenate([block, block], axis=0)))
        band(lambda dz: turns[dz][0:64], b["t_lift"], k, 0)
        band(lambda dz: turns[dz][64:128], b["t_skip"], k)
    loads["raw_ll"].wait()
    for q in range(0, 256, 64):
        raw = b["raw_ll"][q : q + 64].astype(F32)
        for i in range(4):
            for k in range(2):
                b["k_ll"][q : q + 64, tile(2 * i + k)] = raw[:, i, k, :].astype(BF16)
    pm_x.wait_recv()
    for xp in range(4):
        for zp in range(6):
            if 1 <= xp < 3 and 1 <= zp < 5:
                continue
            both = pm[xp, zp].astype(F32)
            pm_wide[2 * xp, 2:10, tile(zp)] = both[0:8]
            pm_wide[2 * xp + 1, 2:10, tile(zp)] = both[8:16]
    for s, y in ((0, 0), (1, 10)):
        for dx in (-1, 0, 1):
            for xp in {0: (0, 1), 1: (1,), -1: (0,)}[dx]:
                base = {0: 2 + 2 * xp, 1: 0, -1: 6}[dx]
                for dz in (-1, 0, 1):
                    slot = b["pm_t"].at[0, (dz + 1) % 2]
                    slot[...] = b["pm_r"][s, dx + 1, dz + 1, xp].astype(F32)
                    for q in {0: (0, 1, 2, 3), 1: (3,), -1: (0,)}[dz]:
                        to = {0: q + 1, 1: 0, -1: 5}[dz]
                        for xi in range(2):
                            row = 4 * q + 2 * xi
                            pm_wide[base + xi, y : y + 2, tile(to)] = slot[row : row + 2, :]
    pm_s = b["pm_s"]
    for x in range(8):
        for dy in range(3):
            pm_s[dy, x] = pm_wide[x, dy : dy + 16, :].astype(BF16)

    def flag(ok):
        return jnp.where(ok, 1.0, 0.0).astype(F32)

    def valid(at, local, size, first, index):
        place = at * local + first + index
        return flag(jnp.logical_and(place >= 0, place < local * size))

    def row_mask(rows, lanes, used, at, local, size, first):
        place = lax.broadcasted_iota(jnp.int32, (rows, lanes), 0)
        whole = place + (at * local + first)
        ok = jnp.logical_and(whole >= 0, whole < local * size)
        return jnp.logical_and(ok, place < used)

    fm_wide = b["fm_wide"]
    mid_rows = row_mask(16, 128, 10, gy, 8, sizes[1], -1)
    first_mid = None
    for dx in range(3):
        for dy in range(3):
            piece = jnp.concatenate(
                [pm_s[dy, dx : dx + 6, :, 128 * j : 128 * j + 256].reshape(96, 256) for j in range(5)],
                axis=0,
            )
            term = dot(piece, b["t_da"][3 * dx + dy])
            first_mid = term if first_mid is None else first_mid + term
    first_mid = jnp.maximum(first_mid, 0.0)
    for x in range(6):
        for z in range(10):
            keep = valid(gx, 4, sizes[0], -1, x) * valid(gz, 8, sizes[2], -1, z)
            at = 96 * (z // 2) + 16 * x
            cell = first_mid[at : at + 16, tile(z % 2)]
            fm_wide[x, z, 0:16, :] = jnp.where(mid_rows, cell, 0.0) * keep

    def gather(wide_ref, target, xs, count):
        for x in range(xs):
            for dy in range(3):
                for odd in range(2):
                    for zp in range(count + 1 - odd):
                        z = 2 * zp + odd
                        both = jnp.concatenate(
                            [wide_ref[x, z + h, dy : dy + 8, :] for h in range(2)], axis=0
                        )
                        target[odd, dy, x, 16 * zp : 16 * zp + 16, :] = both.astype(BF16)

    def conv_rows(source, xs, count, kernels):
        total = None
        for dx in range(3):
            pieces = []
            for dy in range(3):
                for dz in range(3):
                    first = 16 * (dz // 2)
                    piece = source[dz % 2, dy, dx : dx + xs, first : first + 16 * count, :]
                    pieces.append(piece.reshape(xs * 16 * count, source.shape[4]))
            depth = 9 * source.shape[4]
            term = dot(jnp.concatenate(pieces, axis=1), kernels[dx * depth : (dx + 1) * depth, :])
            total = term if total is None else total + term
        return jnp.maximum(total, 0.0)

    gather(fm_wide, b["fm_s"], 6, 4)
    loads["k_db"].wait()
    sm_out, sm = b["sm_out"], b["sm"]
    skip_mid = conv_rows(b["fm_s"], 4, 4, b["k_db"])
    sm_out[...] = skip_mid.reshape(4, 8, 8, 128)
    sm[2:6, 1:5] = skip_mid.astype(BF16).reshape(4, 4, 16, 128)

    pl_t, pl_f, pl_r = b["pl_t"], b["pl_f"], b["pl_r"]
    for x in range(2):
        for z in range(4):
            parts = [sm_out[2 * x + i, 2 * z + k] for i in range(2) for k in range(2)]
            pl_t[x, z] = jnp.maximum(jnp.maximum(parts[0], parts[1]), jnp.maximum(parts[2], parts[3]))
            pl_f[x, 4 * z : 4 * z + 4, :] = jnp.maximum(
                pl_t[x, z, pl.ds(0, 4, stride=2), :], pl_t[x, z, pl.ds(1, 4, stride=2), :]
            )
        pl_r[1, 1, 3 + x] = pl_f[x].astype(BF16)

    def line_message(step):
        sx, tx = {
            1: (slice(3, 5), slice(1, 3)),
            -1: (slice(3, 5), slice(5, 7)),
            2: (slice(4, 5), slice(0, 1)),
            -2: (slice(3, 4), slice(7, 8)),
        }[step[0]]
        return pl_r.at[1, 1, sx], pl_r.at[1, 1, tx]

    def pl_message(step):
        return pl_r.at[1, 1], pl_r.at[1 - step[2], 1 - step[1]]

    line_x = Exchange(LINE_DIRS, line_message, line_ss, line_rs, here, sizes)
    pl_x = Exchange(PLANE_DIRS, pl_message, pl_ss, pl_rs, here, sizes)
    line_x.start()

    sm_t = b["sm_t"]
    for s, y in ((0, 6), (1, 0)):
        for x in range(4):
            for z in range(8):
                sm_t[x, 2 * z : 2 * z + 2, :] = sm_out[x, z, y : y + 2, :]
            b["sm_y"][s, x] = sm_t[x].astype(BF16)
        for zs, z in ((0, 6), (1, 0)):
            for x in range(4):
                b["sm_u"][zs, 4 * x : 4 * x + 4, :] = sm_t[x, 2 * z : 2 * z + 4, :]
            b["sm_e"][s, zs] = b["sm_u"][zs].astype(BF16)

    def sm_message(step):
        dx, dy, dz = step
        if dy == 0:
            sx = {0: slice(2, 6), 1: slice(4, 6), -1: slice(2, 4)}[dx]
            tx = {0: slice(2, 6), 1: slice(0, 2), -1: slice(6, 8)}[dx]
            sz = {0: slice(1, 5), 1: slice(4, 5), -1: slice(1, 2)}[dz]
            tz = {0: slice(1, 5), 1: slice(0, 1), -1: slice(5, 6)}[dz]
            return sm.at[sx, sz], sm.at[tx, tz]
        s = side(dy)
        if dz != 0:
            return b["sm_e"].at[s, side(dz)], b["sm_c"].at[s, dx + 1, side(dz)]
        xs = {0: slice(0, 4), 1: slice(2, 4), -1: slice(0, 2)}[dx]
        return b["sm_y"].at[s, xs], b["sm_r"].at[s, dx + 1, xs]

    sm_x = Exchange(DIRS[::-1], sm_message, sm_ss, sm_rs, here, sizes)
    sm_x.start()

    skip_x.wait_recv()
    shift_top(skip1, b["skip_r"], b["skip0"], b["skip2"])

    b["part"][...] = conv_top((b["skip0"], skip1, b["skip2"]), b["t_skip"])
    line_x.wait_recv()
    pl_x.start()
    loads["k_um"].wait()
    for half in range(2):
        for k in range(9):

            def up_block(dz, half=half, k=k):
                at = 256 * (3 * k + dz) + 128 * half
                return b["k_um"][at : at + 128, :]

            pairs(up_block, 4, 128, b["t_um"].at[half, k])
    mg_wide = b["mg_wide"]
    zero(mg_wide)

    t_lt = b["t_lt"]
    loads["k_lt"].wait()
    for i in range(2):
        for h in range(2):
            at = 128 * (2 * i + h)
            swapped = [b["k_lt"][at + 64 : at + 128, :], b["k_lt"][at : at + 64, :]]
            t_lt[128 * h : 128 * h + 128, tile(i)] = turned(jnp.concatenate(swapped, axis=0)).astype(BF16)

    jm_wide, jm_s = b["jm_wide"], b["jm_s"]
    sm_x.wait_recv()
    for x in range(8):
        for zp in range(6):
            both = sm[x, zp].astype(F32)
            for h in range(2):
                jm_wide[1, x, 2 * zp + h, 2:10, :] = both[8 * h : 8 * h + 8]
    for s, y in ((0, 0), (1, 10)):
        for dx in (-1, 0, 1):
            for xi in {0: (0, 1, 2, 3), 1: (2, 3), -1: (0, 1)}[dx]:
                x = {0: 2 + xi, 1: xi - 2, -1: 6 + xi}[dx]
                slot = sm_t.at[xi % 2]
                slot[...] = b["sm_r"][s, dx + 1, xi].astype(F32)
                for z in range(8):
                    jm_wide[1, x, z + 2, y : y + 2, :] = slot[2 * z : 2 * z + 2, :]
            for zs, to in ((0, 0), (1, 10)):
                slot = sm_t.at[2 + zs]
                slot[...] = b["sm_c"][s, dx + 1, zs].astype(F32)
                for xi in {0: (0, 1, 2, 3), 1: (2, 3), -1: (0, 1)}[dx]:
                    x = {0: 2 + xi, 1: xi - 2, -1: 6 + xi}[dx]
                    for z in range(2):
                        row = 4 * xi + 2 * z
                        jm_wide[1, x, to + z, y : y + 2, :] = slot[row : row + 2, :]

    def shift_mid(half):
        for x in range(8):
            for z in range(12):
                for dy in range(3):
                    jm_s[half, dy, x, :, tile(z)] = jm_wide[half, x, z, dy : dy + 16, :].astype(BF16)

    def conv_mid(half):
        total = None
        for dx in range(3):
            for dy in range(3):
                piece = jnp.concatenate(
                    [
                        jm_s[half, dy, dx : dx + 6, :, 256 * j : 256 * j + 512].reshape(96, 512)
                        for j in range(5)
                    ],
                    axis=0,
                )
                term = dot(piece, b["t_um"][half, 3 * dx + dy])
                total = term if total is None else total + term
        return total

    shift_mid(1)
    b["jm_part"][...] = conv_mid(1)

    pl_x.wait_recv()
    pl_wide, pl_g = b["pl_wide"], b["pl_g"]
    for x in range(8):
        for zs in range(3):
            for ys in range(3):
                pl_g[ys] = pl_r[zs, ys, x].astype(F32)
            for z, to in {0: ((1, 0), (2, 1), (3, 2)), 1: ((0, 3), (1, 4), (2, 5), (3, 6)), 2: ((0, 7), (1, 8), (2, 9))}[zs]:
                pl_wide[x, to, 0:3, :] = pl_g[0, 4 * z + 1 : 4 * z + 4, :]
                pl_wide[x, to, 3:7, :] = pl_g[1, 4 * z : 4 * z + 4, :]
                pl_wide[x, to, 7:10, :] = pl_g[2, 4 * z : 4 * z + 3, :]
    gather(pl_wide, b["pl_s"], 8, 4)
    loads["k_la"].wait()
    first_low = conv_rows(b["pl_s"], 6, 4, b["k_la"])
    fl_wide = b["fl_wide"]
    low_rows = row_mask(8, 256, 8, gy, 4, sizes[1], -2)
    for x in range(6):
        for z in range(8):
            keep = valid(gx, 2, sizes[0], -2, x) * valid(gz, 4, sizes[2], -2, z)
            at = 64 * x + 8 * z
            fl_wide[x, z, 0:8, :] = jnp.where(low_rows, first_low[at : at + 8, :], 0.0) * keep
            fl_wide[x, z, 8:16, :] = jnp.zeros((8, 256), F32)
    gather(fl_wide, b["fl_s"], 6, 3)
    loads["k_lb"].wait()
    coarse = conv_rows(b["fl_s"], 4, 3, b["k_lb"])
    coarse_rows = row_mask(8, 256, 6, gy, 4, sizes[1], -1)
    cells = []
    for x in range(4):
        for z in range(6):
            keep = valid(gx, 2, sizes[0], -1, x) * valid(gz, 4, sizes[2], -1, z)
            at = 48 * x + 8 * z
            cells.append(jnp.where(coarse_rows, coarse[at : at + 8, :], 0.0) * keep)
    coarse = jnp.concatenate(cells, axis=0).astype(BF16)

    lifted = dot(coarse, b["k_ll"][...])
    for x in range(4):
        for z in range(6):
            for i in range(2):
                for h in range(2):
                    for k in range(2):
                        at = 48 * x + 8 * z
                        jm_wide[0, 2 * x + i, 2 * z + k, pl.ds(h, 8, stride=2), :] = lifted[
                            at : at + 8, tile(4 * i + 2 * h + k)
                        ]

    mg_wide = b["mg_wide"]
    shift_mid(0)
    merged = jnp.maximum(conv_mid(0) + b["jm_part"][...], 0.0)
    for x in range(6):
        for z in range(10):
            keep = valid(gx, 4, sizes[0], -1, x) * valid(gz, 8, sizes[2], -1, z)
            at = 96 * (z // 2) + 16 * x
            cell = jnp.where(mid_rows, merged[at : at + 16, tile(z % 2)], 0.0) * keep
            for h in range(2):
                mg_wide[h, x, z, pl.ds(h, 16, stride=2), :] = cell

    lift_half = lax.broadcasted_iota(jnp.int32, (16, 128), 1) < 64
    lift = (b["lift0"], b["lift1"], b["lift2"])
    for x in range(6):
        for dy in range(3):
            halves = [mg_wide[h, x, :, dy + 1 : dy + 17, :].astype(BF16).reshape(160, 128) for h in range(2)]
            piece = jnp.concatenate(halves, axis=1)
            value = dot(piece, t_lt[...]).astype(BF16)
            for i in range(2):
                to = 2 * x + i - 1
                if 0 <= to < 10:
                    for t in range(9):
                        lift[dy][to, :, tile(t)] = jnp.where(
                            lift_half,
                            value[16 * t : 16 * t + 16, tile(i)],
                            value[16 * t + 16 : 16 * t + 32, tile(i)],
                        )

    total = conv_top(lift, b["t_lift"], 384) + b["part"][...]
    for g in range(4):
        out[:, :, 256 * g : 256 * g + 256] = total[128 * g : 128 * g + 128].astype(BF16).reshape(8, 16, 256)
    for exchange in (vol_x, pm_x, skip_x, line_x, pl_x, sm_x):
        exchange.wait_send()


def body(sizes, volume, *weights):
    w_top, w_da, w_db, w_la, w_lb, w_ll, w_um, w_lt, w_out = weights
    flat = [
        w_top.reshape(1728, 64),
        w_da.reshape(1728, 128),
        w_db.reshape(3456, 128),
        w_la.reshape(3456, 256),
        w_lb.reshape(6912, 256),
        w_ll.reshape(256, 4, 2, 128),
        w_um.reshape(6912, 128),
        w_lt.transpose(1, 2, 3, 4, 0).reshape(512, 128),
        w_out.swapaxes(3, 4).reshape(1728, 128),
    ]
    any_space = pl.BlockSpec(memory_space=pl.ANY)
    few, line, plane = len(DIRS), len(LINE_DIRS), len(PLANE_DIRS)
    counts = (17, few, few, few, few, few, few, few, few, line, line, plane, plane)
    return pl.pallas_call(
        functools.partial(kernel, sizes),
        out_shape=pltpu.VMEM(volume.shape, BF16),
        in_specs=[any_space] * 10,
        out_specs=pl.BlockSpec(memory_space=pltpu.VMEM),
        scratch_shapes=[pltpu.VMEM(s, d) for s, d in SCRATCH.values()]
        + [pltpu.SemaphoreType.DMA((c,)) for c in counts],
        compiler_params=pltpu.CompilerParams(
            collective_id=0, has_side_effects=True, vmem_limit_bytes=56 * 1024 * 1024
        ),
    )(volume, *flat)


def solution(mesh):
    placed = (P("gx", "gy", "gz"),) + (P(),) * 9
    sizes = tuple(mesh.shape[name] for name in ("gx", "gy", "gz"))
    return jax.shard_map(
        functools.partial(body, sizes),
        mesh=mesh,
        in_specs=placed,
        out_specs=P("gx", "gy", "gz"),
        check_vma=False,
    )
```
